128 devices in a mesh: samp: 8 (over z, y_lo), seq: 16 (over x, y_hi, core).
Axes of the slice: x: 4, y: 4 (y_hi: 2, y_lo: 2; y = y_hi * 2 + y_lo), z: 4, core: 2. Of those that a mesh axis runs over, the one named last changes fastest.
Arguments:
- atom_in: bfloat16 [32, 4096, 128], P('samp', 'seq'), may hold values from -6 to 6
- tok_in: bfloat16 [32, 1024, 768], P('samp', 'seq'), may hold values from -6 to 6
- atom_cond: bfloat16 [4096, 128], P('seq'), may hold values from -6 to 6
- single_cond: bfloat16 [1024, 384], P('seq'), may hold values from -6 to 6
- atom_pair: bfloat16 [16, 4096, 128], P(None, 'seq'), may hold values from -6 to 6
- token_pair: bfloat16 [128, 1024, 1024], P(None, 'seq'), may hold values from -6 to 6
- atom_w_cond: bfloat16 [128, 768], replicated, may hold values from -0.5 to 0.5
- atom_w_qkvg: bfloat16 [128, 512], replicated, may hold values from -0.5 to 0.5
- atom_w_out: bfloat16 [128, 128], replicated, may hold values from -1.5 to 1.5
- atom_w_up: bfloat16 [128, 512], replicated, may hold values from -0.5 to 0.5
- atom_w_down: bfloat16 [256, 128], replicated, may hold values from -0.75 to 0.75
- atom_w_pair: bfloat16 [16, 4], replicated, may hold values from -1.5 to 1.5
- pool_weight: bfloat16 [128, 768], replicated, may hold values from -0.5 to 0.5
- token_w_cond: bfloat16 [384, 4608], replicated, may hold values from -0.3125 to 0.3125
- token_w_qkvg: bfloat16 [768, 3072], replicated, may hold values from -0.21875 to 0.21875
- token_w_out: bfloat16 [768, 768], replicated, may hold values from -0.625 to 0.625
- token_w_up: bfloat16 [768, 3072], replicated, may hold values from -0.21875 to 0.21875
- token_w_down: bfloat16 [1536, 768], replicated, may hold values from -0.3125 to 0.3125
- token_w_pair: bfloat16 [16, 128], replicated, may hold values from -0.5 to 0.5
- cotangent: bfloat16 [32, 1024, 768], P('samp', 'seq'), may hold values from -6 to 6
Outputs:
- token_out: bfloat16 [32, 1024, 768], P('samp', 'seq')
- grad_atom_in: float32 [32, 4096, 128], P('samp', 'seq')
- grad_tok_in: float32 [32, 1024, 768], P('samp', 'seq')
- grad_atom_w_cond: float32 [128, 768], P('seq')
- grad_atom_w_qkvg: float32 [128, 512], P('seq')
- grad_atom_w_out: float32 [128, 128], P('seq')
- grad_atom_w_up: float32 [128, 512], P('seq')
- grad_atom_w_down: float32 [256, 128], P('seq')
- grad_atom_w_pair: float32 [16, 4], P('seq')
- grad_pool_weight: float32 [128, 768], P('seq')
- grad_token_w_cond: float32 [384, 4608], P('seq')
- grad_token_w_qkvg: float32 [768, 3072], P('seq')
- grad_token_w_out: float32 [768, 768], P('seq')
- grad_token_w_up: float32 [768, 3072], P('seq')
- grad_token_w_down: float32 [1536, 768], P('seq')
- grad_token_w_pair: float32 [16, 128], P('seq')
The draws below stay inside these ranges and needn't reach their ends.
All inputs are finite; a program needn't handle non-finite values.
Results may differ from the reference program's by a relative error of at most 0.025.
Values may be sent and summed in bfloat16 or wider, within the bound.
No kernel may reach another device: no remote copies, remote signals or barrier semaphores. Data moves between devices by JAX's collectives and lax.ppermute only.
A program may use at most 320 MiB of HBM per device.

```python
import functools
import math
import jax
import jax.numpy as jnp
from jax import lax

DA = 128
HA = 4
FA = 256
CZA = 16
QWIN = 32
KWIN = 128
ATOMS_TOK = 4
D = 768
H = 16
CS = 384
CZ = 128
FT = 1536
SAMPLES = 32
NTOK = 1024
ATOMS = 4096


def level_of(rng, extent, cuts, smallest, high):
    level = 1.0
    for axis_at, blocks in cuts:
        steps = jax.random.uniform(jax.random.fold_in(jax.random.fold_in(rng, 6), axis_at), (blocks,), jnp.float32, smallest / len(cuts), high / len(cuts))
        level = level * jnp.repeat(jnp.exp(steps), extent[axis_at] // blocks).reshape((-1,) + (1,) * (len(extent) - 1 - axis_at))
    return level


def normal_values(own_key, dims, spread, bound, cuts=(), kind=jnp.bfloat16):
    array = spread * jax.random.normal(own_key, dims, jnp.float32)
    if cuts:
        array = array * level_of(own_key, dims, cuts, -0.22, 0.18)
    return jnp.clip(array, -bound, bound).astype(kind)


def setup_inputs(seed: int = 0) -> dict:
    key_list = jax.random.split(jax.random.key(seed), 21)
    return {
        "atom_in": normal_values(key_list[0], (SAMPLES, ATOMS, DA), 1.0, 6.0, ((0, 8), (1, 16))),
        "tok_in": normal_values(key_list[1], (SAMPLES, NTOK, D), 1.0, 6.0, ((0, 8), (1, 16))),
        "atom_cond": normal_values(key_list[2], (ATOMS, DA), 1.0, 6.0, ((0, 16),)),
        "single_cond": normal_values(key_list[3], (NTOK, CS), 1.0, 6.0, ((0, 16),)),
        "atom_pair": normal_values(key_list[4], (CZA, ATOMS, KWIN), 1.0, 6.0, ((1, 16),)),
        "token_pair": normal_values(key_list[5], (CZ, NTOK, NTOK), 1.0, 6.0, ((1, 16),)),
        "atom_w_cond": normal_values(key_list[6], (DA, 6 * DA), DA ** -0.5, 0.5),
        "atom_w_qkvg": normal_values(key_list[7], (DA, 4 * DA), DA ** -0.5, 0.5),
        "atom_w_out": normal_values(key_list[8], (DA, DA), (DA // 8) ** -0.5, 1.5),
        "atom_w_up": normal_values(key_list[9], (DA, 2 * FA), DA ** -0.5, 0.5),
        "atom_w_down": normal_values(key_list[10], (FA, DA), (FA // 4) ** -0.5, 0.75),
        "atom_w_pair": normal_values(key_list[11], (CZA, HA), CZA ** -0.5, 1.5),
        "pool_weight": normal_values(key_list[12], (DA, D), DA ** -0.5, 0.5),
        "token_w_cond": normal_values(key_list[13], (CS, 6 * D), CS ** -0.5, 0.3125),
        "token_w_qkvg": normal_values(key_list[14], (D, 4 * D), D ** -0.5, 0.21875),
        "token_w_out": normal_values(key_list[15], (D, D), (D // 8) ** -0.5, 0.625),
        "token_w_up": normal_values(key_list[16], (D, 2 * FT), D ** -0.5, 0.21875),
        "token_w_down": normal_values(key_list[17], (FT, D), (FT // 4) ** -0.5, 0.3125),
        "token_w_pair": normal_values(key_list[18], (H, CZ), CZ ** -0.5, 0.5),
        "cotangent": normal_values(key_list[19], (SAMPLES, NTOK, D), 1.0, 6.0, ((0, 8), (1, 16))),
    }


@jax.custom_vjp
def low(v):
    return lax.optimization_barrier(v.astype(jnp.bfloat16)).astype(jnp.float32)

@jax.custom_vjp
def low_back(v):
    return v

def low_keep(v):
    return (low(v), None)

def low_pass(kept, grad):
    return (grad,)

def back_keep(v):
    return (v, None)

def back_low(kept, grad):
    return (low(grad),)
low.defvjp(low_keep, low_pass)
low_back.defvjp(back_keep, back_low)
highest = lax.Precision.HIGHEST
eps = 1e-05
masked = -1000000000.0

def matmul_high(left, right):
    return jnp.dot(left, right, precision=highest)

def norm_rows(x, axis):
    centred = x - lax.optimization_barrier(jnp.mean(x, axis=axis, keepdims=True))
    return centred * lax.rsqrt(lax.optimization_barrier(jnp.mean(centred * centred, axis=axis, keepdims=True)) + eps)

def softmax_rows(scores):
    row_max = lax.optimization_barrier(jnp.max(scores, axis=-1, keepdims=True))
    exponent = jnp.exp(scores - row_max)
    return exponent / lax.optimization_barrier(jnp.sum(exponent, axis=-1, keepdims=True))

def window_keys(padded, n_windows):
    rim_width = (KWIN - QWIN) // 2
    block_rows = math.gcd(QWIN, rim_width)
    stride = QWIN // block_rows
    blocks = padded.reshape(padded.shape[0], -1, block_rows, padded.shape[-1])
    pieces = [blocks[:, m:m + stride * n_windows:stride] for m in range(KWIN // block_rows)]
    return jnp.concatenate(pieces, axis=2)

def token_attend(query_part, key_part, value_part, score_bias, head_count):
    row_count, channels = query_part.shape
    head_size = channels // head_count
    query_heads = query_part.reshape(row_count, head_count, head_size)
    key_heads = key_part.reshape(-1, head_count, head_size)
    value_heads = value_part.reshape(-1, head_count, head_size)
    raw = jnp.einsum('qhd,khd->hqk', query_heads, key_heads, precision=highest) * head_size ** (-0.5) + score_bias
    scores = low_back(raw)
    attention = low(softmax_rows(scores))
    attended = jnp.einsum('hqk,khd->qhd', attention, value_heads, precision=highest)
    return low_back(attended.reshape(row_count, channels))

def atom_attend(query_part, key_part, value_part, score_bias, key_valid, head_count):
    row_count, channels = query_part.shape
    head_size = channels // head_count
    n_windows = row_count // QWIN
    rim_width = (KWIN - QWIN) // 2
    joined = jnp.concatenate([key_part, value_part], axis=-1)
    padded = jnp.pad(joined, ((rim_width, rim_width), (0, 0)))
    windows = window_keys(padded[None], n_windows)[0]
    query_heads = query_part.reshape(n_windows, QWIN, head_count, head_size)
    key_heads = windows[..., :channels].reshape(n_windows, KWIN, head_count, head_size)
    value_heads = windows[..., channels:].reshape(n_windows, KWIN, head_count, head_size)
    raw = jnp.einsum('wqhd,wkhd->whqk', query_heads, key_heads, precision=highest) * head_size ** (-0.5) + score_bias
    scores = low_back(jnp.where(key_valid[:, None, None, :], raw, masked))
    attention = low(softmax_rows(scores))
    attended = jnp.einsum('whqk,wkhd->wqhd', attention, value_heads, precision=highest)
    return low_back(attended.reshape(row_count, channels))

def gated_block(x, cond_low, weights, attend):
    cond_weight, qkvg_weight, out_weight, up_weight, down_weight = weights
    channels = x.shape[-1]
    cond_proj = low_back(matmul_high(cond_low, cond_weight))
    cond_parts = [cond_proj[:, i * channels:(i + 1) * channels] for i in range(6)]
    first_in = jax.nn.sigmoid(cond_parts[0]) * norm_rows(x, -1) + cond_parts[1]
    projected = low_back(matmul_high(low(first_in), qkvg_weight))
    attended = attend(low(projected[:, :channels]), low(projected[:, channels:2 * channels]), low(projected[:, 2 * channels:3 * channels]))
    gated = low(jax.nn.sigmoid(projected[:, 3 * channels:]) * attended)
    middle = x + jax.nn.sigmoid(cond_parts[2]) * low_back(matmul_high(gated, out_weight))
    second = jax.nn.sigmoid(cond_parts[3]) * norm_rows(middle, -1) + cond_parts[4]
    up_out = low_back(matmul_high(low(second), up_weight))
    hidden_width = up_out.shape[-1] // 2
    gate_half = up_out[:, :hidden_width]
    hidden = low(gate_half * jax.nn.sigmoid(gate_half) * up_out[:, hidden_width:])
    return middle + jax.nn.sigmoid(cond_parts[5]) * low_back(matmul_high(hidden, down_weight))

def reference(atom_in, tok_in, atom_cond, single_cond, atom_pair, token_pair, atom_w_cond, atom_w_qkvg, atom_w_out, atom_w_up, atom_w_down, atom_w_pair, pool_weight, token_w_cond, token_w_qkvg, token_w_out, token_w_up, token_w_down, token_w_pair, cotangent):
    n_windows = ATOMS // QWIN
    atom_low = low(norm_rows(atom_cond.astype(jnp.float32), -1))
    single_low = low(norm_rows(single_cond.astype(jnp.float32), -1))
    atom_pair_low = low(norm_rows(atom_pair.astype(jnp.float32), 0)).reshape(CZA, n_windows, QWIN, KWIN)
    token_pair_low = low(norm_rows(token_pair.astype(jnp.float32), 0))
    window_start = QWIN * jnp.arange(n_windows, dtype=jnp.int32)[:, None] - (KWIN - QWIN) // 2
    key_index = window_start + jnp.arange(KWIN, dtype=jnp.int32)[None, :]
    key_valid = (key_index >= 0) & (key_index < ATOMS)
    weights = tuple((weight.astype(jnp.float32) for weight in (atom_w_cond, atom_w_qkvg, atom_w_out, atom_w_up, atom_w_down, atom_w_pair, pool_weight, token_w_cond, token_w_qkvg, token_w_out, token_w_up, token_w_down, token_w_pair)))

    def forward(atom_batch, token_batch, params):
        atom_bias = jnp.einsum('cwqk,ch->whqk', atom_pair_low, params[5], precision=highest)
        token_bias = jnp.einsum('cqk,hc->hqk', token_pair_low, params[12], precision=highest)
        atom_fn = functools.partial(atom_attend, score_bias=atom_bias, key_valid=key_valid, head_count=HA)
        token_fn = functools.partial(token_attend, score_bias=token_bias, head_count=H)

        def one_sample(pair_in):
            atom_x, token_x = pair_in
            atom_out = gated_block(atom_x, atom_low, params[0:5], atom_fn)
            pooled = lax.optimization_barrier(jnp.mean(atom_out.reshape(NTOK, ATOMS_TOK, DA), axis=1))
            token_start = token_x + low_back(matmul_high(low(pooled), params[6]))
            return gated_block(token_start, single_low, params[7:12], token_fn)
        return lax.map(jax.checkpoint(one_sample), (atom_batch, token_batch))
    token_out, pullback = jax.vjp(forward, atom_in.astype(jnp.float32), tok_in.astype(jnp.float32), weights)
    grad_atoms, grad_tokens, grad_params = pullback(cotangent.astype(jnp.float32))
    return (token_out.astype(jnp.bfloat16), grad_atoms, grad_tokens, grad_params[0], grad_params[1], grad_params[2], grad_params[3], grad_params[4], grad_params[5], grad_params[6], grad_params[7], grad_params[8], grad_params[9], grad_params[10], grad_params[11], grad_params[12])
```

```python
import functools
import math

import jax
import jax.numpy as jnp
from jax import lax
from jax.sharding import PartitionSpec as P

QWIN = 32
KWIN = 128


eps = 1e-05
masked = -1000000000.0


def with_halo(cells, sides, width):
    for axis, dim in sides:
        count = lax.axis_size(axis)
        ends = count - 1
        head = lax.slice_in_dim(cells, 0, width, axis=dim)
        tail = lax.slice_in_dim(cells, cells.shape[dim] - width, cells.shape[dim], axis=dim)
        cells = jnp.concatenate(
            [
                lax.ppermute(tail, axis, [(i, (i + 1) % count) for i in range(ends)]),
                cells,
                lax.ppermute(head, axis, [((i + 1) % count, i) for i in range(ends)]),
            ],
            axis=dim,
        )
    return cells


def shifted(value, axis, steps):
    count = lax.axis_size(axis)
    leading, last = (max(0, -steps), min(count, count - steps))
    return lax.ppermute(value, axis, [(source, source + steps) for source in range(leading, last)])


def for_sending(x):
    return jax.tree.map(lambda a: a.astype(jnp.bfloat16) if a.dtype == jnp.float32 else a, x)


def product(left, right):
    return jnp.dot(left, right, preferred_element_type=jnp.float32)


def product_right(left, right):
    return lax.dot_general(
        left, right, (((left.ndim - 1,), (1,)), ((), ())), preferred_element_type=jnp.float32
    )


def weight_grad(inputs, outputs):
    flat_in = inputs.reshape(-1, inputs.shape[-1])
    flat_out = outputs.reshape(-1, outputs.shape[-1])
    return lax.dot_general(
        flat_in, flat_out, (((0,), (0,)), ((), ())), preferred_element_type=jnp.float32
    )


def sig_slope(squashed):
    return squashed * (1.0 - squashed)


def norm_stats(x, axis):
    centred = x - jnp.mean(x, axis=axis, keepdims=True)
    inverse = lax.rsqrt(jnp.mean(centred * centred, axis=axis, keepdims=True) + eps)
    return (centred * inverse, inverse)


def norm_back(gradient, normed, inverse):
    return inverse * (
        gradient
        - jnp.mean(gradient, axis=-1, keepdims=True)
        - normed * jnp.mean(gradient * normed, axis=-1, keepdims=True)
    )


def window_keys(padded, n_windows):
    rim_width = (KWIN - QWIN) // 2
    block_rows = math.gcd(QWIN, rim_width)
    stride = QWIN // block_rows
    blocks = padded.reshape(padded.shape[0], -1, block_rows, padded.shape[-1])
    pieces = [blocks[:, m : m + stride * n_windows : stride] for m in range(KWIN // block_rows)]
    return jnp.concatenate(pieces, axis=2)


def window_back(grad_windows, n_windows, length):
    rim_width = (KWIN - QWIN) // 2
    block_rows = math.gcd(QWIN, rim_width)
    stride = QWIN // block_rows
    sample_count = grad_windows.shape[0]
    channels = grad_windows.shape[-1]
    blocks = jnp.zeros((sample_count, length // block_rows, block_rows, channels), jnp.float32)
    for m in range(KWIN // block_rows):
        blocks = blocks.at[:, m : m + stride * n_windows : stride].add(
            grad_windows[:, :, m * block_rows : (m + 1) * block_rows]
        )
    return blocks.reshape(sample_count, length, channels)


def token_scores(query_heads, key_heads, score_bias):
    head_size = query_heads.shape[-1]
    return (
        jnp.einsum("sqhd,skhd->shqk", query_heads, key_heads, preferred_element_type=jnp.float32)
        * head_size ** (-0.5)
        + score_bias[None]
    )


def token_forward(query_part, key_part, value_part, score_bias, head_count):
    sample_count, row_count, channels = query_part.shape
    head_size = channels // head_count
    joined = jnp.concatenate([key_part, value_part], axis=-1)
    gathered = lax.all_gather(joined, "seq", axis=1, tiled=True)
    key_heads = gathered[..., :channels].reshape(sample_count, -1, head_count, head_size)
    value_heads = gathered[..., channels:].reshape(sample_count, -1, head_count, head_size)
    query_heads = query_part.reshape(sample_count, row_count, head_count, head_size)
    scores = token_scores(query_heads, key_heads, score_bias)
    row_max = jnp.max(scores, axis=-1, keepdims=True)
    exponent = jnp.exp(scores - row_max)
    row_total = jnp.sum(exponent, axis=-1, keepdims=True)
    attention = (exponent / row_total).astype(jnp.bfloat16)
    attended = jnp.einsum(
        "shqk,skhd->sqhd", attention, value_heads, preferred_element_type=jnp.float32
    )
    log_total = row_max + jnp.log(row_total)
    return (
        attended.reshape(sample_count, row_count, channels),
        (query_heads, key_heads, value_heads, log_total),
    )


def token_backward(grad_attended, stored, score_bias, pair_low, head_count):
    query_heads, key_heads, value_heads, log_total = stored
    sample_count, row_count, channels = grad_attended.shape
    head_size = channels // head_count
    score_scale = head_size ** (-0.5)
    grad_heads = grad_attended.reshape(query_heads.shape)
    attention = jnp.exp(token_scores(query_heads, key_heads, score_bias) - log_total)
    grad_attention = jnp.einsum(
        "sqhd,skhd->shqk", grad_heads, value_heads, preferred_element_type=jnp.float32
    )
    row_dot = jnp.sum(attention * grad_attention, axis=-1, keepdims=True)
    grad_scores = (attention * (grad_attention - row_dot)).astype(jnp.bfloat16)
    grad_query = (
        jnp.einsum("shqk,skhd->sqhd", grad_scores, key_heads, preferred_element_type=jnp.float32)
        * score_scale
    )
    grad_keys = (
        jnp.einsum("shqk,sqhd->skhd", grad_scores, query_heads, preferred_element_type=jnp.float32)
        * score_scale
    )
    grad_values = jnp.einsum(
        "shqk,sqhd->skhd",
        attention.astype(jnp.bfloat16),
        grad_heads,
        preferred_element_type=jnp.float32,
    )
    grad_pair = jnp.einsum(
        "shqk,cqk->hc", grad_scores, pair_low, preferred_element_type=jnp.float32
    )
    grad_joined = jnp.concatenate(
        [
            grad_keys.reshape(sample_count, -1, channels),
            grad_values.reshape(sample_count, -1, channels),
        ],
        axis=-1,
    )
    own_grads = lax.psum_scatter(
        grad_joined.astype(jnp.bfloat16), "seq", scatter_dimension=1, tiled=True
    ).astype(jnp.float32)
    return (
        grad_query.reshape(sample_count, row_count, channels),
        own_grads[..., :channels],
        own_grads[..., channels:],
        grad_pair,
    )


def atom_scores(query_heads, key_heads, score_bias, key_valid):
    head_size = query_heads.shape[-1]
    raw = (
        jnp.einsum("swqhd,swkhd->swhqk", query_heads, key_heads, preferred_element_type=jnp.float32)
        * head_size ** (-0.5)
        + score_bias[None]
    )
    return jnp.where(key_valid[None, :, None, None, :], raw, masked)


def atom_forward(query_part, key_part, value_part, score_bias, key_valid, head_count):
    sample_count, row_count, channels = query_part.shape
    head_size = channels // head_count
    n_windows = row_count // QWIN
    rim_width = (KWIN - QWIN) // 2
    joined = jnp.concatenate([key_part, value_part], axis=-1)
    padded = with_halo(joined, (("seq", 1),), rim_width)
    windows = window_keys(padded, n_windows)
    key_heads = windows[..., :channels].reshape(
        sample_count, n_windows, KWIN, head_count, head_size
    )
    value_heads = windows[..., channels:].reshape(
        sample_count, n_windows, KWIN, head_count, head_size
    )
    query_heads = query_part.reshape(sample_count, n_windows, QWIN, head_count, head_size)
    scores = atom_scores(query_heads, key_heads, score_bias, key_valid)
    row_max = jnp.max(scores, axis=-1, keepdims=True)
    exponent = jnp.exp(scores - row_max)
    row_total = jnp.sum(exponent, axis=-1, keepdims=True)
    attention = (exponent / row_total).astype(jnp.bfloat16)
    attended = jnp.einsum(
        "swhqk,swkhd->swqhd", attention, value_heads, preferred_element_type=jnp.float32
    )
    log_total = row_max + jnp.log(row_total)
    return (
        attended.reshape(sample_count, row_count, channels),
        (query_heads, key_heads, value_heads, log_total),
    )


def atom_backward(grad_attended, stored, score_bias, key_valid, pair_low, head_count):
    query_heads, key_heads, value_heads, log_total = stored
    sample_count, row_count, channels = grad_attended.shape
    head_size = channels // head_count
    n_windows = row_count // QWIN
    rim_width = (KWIN - QWIN) // 2
    score_scale = head_size ** (-0.5)
    grad_heads = grad_attended.reshape(query_heads.shape)
    attention = jnp.exp(atom_scores(query_heads, key_heads, score_bias, key_valid) - log_total)
    grad_attention = jnp.einsum(
        "swqhd,swkhd->swhqk", grad_heads, value_heads, preferred_element_type=jnp.float32
    )
    row_dot = jnp.sum(attention * grad_attention, axis=-1, keepdims=True)
    grad_scores = (attention * (grad_attention - row_dot)).astype(jnp.bfloat16)
    grad_query = (
        jnp.einsum("swhqk,swkhd->swqhd", grad_scores, key_heads, preferred_element_type=jnp.float32)
        * score_scale
    )
    grad_keys = (
        jnp.einsum(
            "swhqk,swqhd->swkhd", grad_scores, query_heads, preferred_element_type=jnp.float32
        )
        * score_scale
    )
    grad_values = jnp.einsum(
        "swhqk,swqhd->swkhd",
        attention.astype(jnp.bfloat16),
        grad_heads,
        preferred_element_type=jnp.float32,
    )
    grad_pair = jnp.einsum(
        "swhqk,cwqk->ch", grad_scores, pair_low, preferred_element_type=jnp.float32
    )
    grad_windows = jnp.concatenate(
        [
            grad_keys.reshape(sample_count, n_windows, KWIN, channels),
            grad_values.reshape(sample_count, n_windows, KWIN, channels),
        ],
        axis=-1,
    )
    grad_padded = window_back(grad_windows, n_windows, row_count + 2 * rim_width)
    own_grads = grad_padded[:, rim_width : rim_width + row_count]
    from_next = shifted(grad_padded[:, :rim_width].astype(jnp.bfloat16), "seq", -1).astype(
        jnp.float32
    )
    from_prev = shifted(
        grad_padded[:, rim_width + row_count :].astype(jnp.bfloat16), "seq", 1
    ).astype(jnp.float32)
    own_grads = own_grads.at[:, row_count - rim_width :].add(from_next)
    own_grads = own_grads.at[:, :rim_width].add(from_prev)
    return (
        grad_query.reshape(sample_count, row_count, channels),
        own_grads[..., :channels],
        own_grads[..., channels:],
        grad_pair,
    )


def block_forward(x, cond_low, weights, attend):
    cond_weight, qkvg_weight, out_weight, up_weight, down_weight = weights
    channels = x.shape[-1]
    cond_proj = product(cond_low, cond_weight)[None]
    cond_parts = [cond_proj[..., i * channels : (i + 1) * channels] for i in range(6)]
    normed_a, inverse_a = norm_stats(x, -1)
    scale_a = jax.nn.sigmoid(cond_parts[0])
    first_low = (scale_a * normed_a + cond_parts[1]).astype(jnp.bfloat16)
    projected = product(first_low, qkvg_weight)
    qkv_low = projected[..., : 3 * channels].astype(jnp.bfloat16)
    gate_sig = jax.nn.sigmoid(projected[..., 3 * channels :])
    attended, kept_attn = attend(
        qkv_low[..., :channels], qkv_low[..., channels : 2 * channels], qkv_low[..., 2 * channels :]
    )
    gated_low = (gate_sig * attended).astype(jnp.bfloat16)
    branch = product(gated_low, out_weight)
    gate_a = jax.nn.sigmoid(cond_parts[2])
    middle = x + gate_a * branch
    normed_b, inverse_b = norm_stats(middle, -1)
    scale_b = jax.nn.sigmoid(cond_parts[3])
    second_low = (scale_b * normed_b + cond_parts[4]).astype(jnp.bfloat16)
    up_out = product(second_low, up_weight)
    hidden_width = up_out.shape[-1] // 2
    gate_half = up_out[..., :hidden_width]
    up_half = up_out[..., hidden_width:]
    half_sig = jax.nn.sigmoid(gate_half)
    hidden_low = (gate_half * half_sig * up_half).astype(jnp.bfloat16)
    down_out = product(hidden_low, down_weight)
    gate_b = jax.nn.sigmoid(cond_parts[5])
    stored = (
        normed_a,
        inverse_a,
        scale_a,
        first_low,
        gate_sig,
        attended,
        kept_attn,
        gated_low,
        branch,
        gate_a,
        normed_b,
        inverse_b,
        scale_b,
        second_low,
        gate_half,
        up_half,
        half_sig,
        hidden_low,
        down_out,
        gate_b,
    )
    return (middle + gate_b * down_out, stored)


def block_backward(upstream, stored, cond_low, weights, attend_back):
    cond_weight, qkvg_weight, out_weight, up_weight, down_weight = weights
    (
        normed_a,
        inverse_a,
        scale_a,
        first_low,
        gate_sig,
        attended,
        kept_attn,
        gated_low,
        branch,
        gate_a,
        normed_b,
        inverse_b,
        scale_b,
        second_low,
        gate_half,
        up_half,
        half_sig,
        hidden_low,
        down_out,
        gate_b,
    ) = stored
    grad_gate_b = upstream * down_out * sig_slope(gate_b)
    grad_down = (upstream * gate_b).astype(jnp.bfloat16)
    grad_hidden = product_right(grad_down, down_weight)
    grad_gate_half = grad_hidden * up_half * half_sig * (1.0 + gate_half * (1.0 - half_sig))
    grad_up_half = grad_hidden * gate_half * half_sig
    grad_up = jnp.concatenate([grad_gate_half, grad_up_half], axis=-1).astype(jnp.bfloat16)
    grad_second = product_right(grad_up, up_weight)
    grad_scale_b = grad_second * normed_b * sig_slope(scale_b)
    grad_middle = upstream + norm_back(grad_second * scale_b, normed_b, inverse_b)
    grad_gate_a = grad_middle * branch * sig_slope(gate_a)
    grad_branch = (grad_middle * gate_a).astype(jnp.bfloat16)
    grad_gated = product_right(grad_branch, out_weight)
    grad_gates = grad_gated * attended * sig_slope(gate_sig)
    grad_attended = (grad_gated * gate_sig).astype(jnp.bfloat16)
    grad_query, grad_keys, grad_values, grad_pair = attend_back(grad_attended, kept_attn)
    grad_projected = jnp.concatenate(
        [grad_query, grad_keys, grad_values, grad_gates], axis=-1
    ).astype(jnp.bfloat16)
    grad_first = product_right(grad_projected, qkvg_weight)
    grad_scale_a = grad_first * normed_a * sig_slope(scale_a)
    grad_x = grad_middle + norm_back(grad_first * scale_a, normed_a, inverse_a)
    grad_cond = jnp.concatenate(
        [grad_scale_a, grad_first, grad_gate_a, grad_scale_b, grad_second, grad_gate_b], axis=-1
    ).astype(jnp.bfloat16)
    grad_cond_weight = jnp.einsum(
        "rc,srn->cn", cond_low, grad_cond, preferred_element_type=jnp.float32
    )
    return (
        grad_x,
        (
            grad_cond_weight,
            weight_grad(first_low, grad_projected),
            weight_grad(gated_low, grad_branch),
            weight_grad(second_low, grad_up),
            weight_grad(hidden_low, grad_down),
            grad_pair,
        ),
    )


def reduce_weights(grads):
    runs, samples, cores = lax.axis_size("seq"), lax.axis_size("samp"), 2
    lanes = 256
    pieces = [g.astype(jnp.bfloat16).reshape(runs, -1) for g in grads]
    lengths = [piece.shape[1] for piece in pieces]
    flat = jnp.concatenate(pieces, axis=1)
    unit = samples * 16 * lanes
    padded = -(-flat.shape[1] // unit) * unit
    flat = jnp.pad(flat, ((0, 0), (0, padded - flat.shape[1])))
    rows = padded // (samples * lanes)
    parts = flat.reshape(runs // cores, cores, samples, rows, lanes).transpose(1, 2, 0, 3, 4)
    parts = parts.reshape(cores, samples * (runs // cores) * rows, lanes)
    core_groups = [[i, i + 1] for i in range(0, runs, cores)]
    met = lax.all_to_all(parts, "seq", 0, 0, tiled=True, axis_index_groups=core_groups)
    chip = (met[0].astype(jnp.float32) + met[1].astype(jnp.float32)).astype(jnp.bfloat16)
    chips = samples * runs // cores
    chip_groups = [[c + cores * i for i in range(chips)] for c in range(cores)]
    spread = lax.all_to_all(
        chip.reshape(chips, rows, lanes), ("samp", "seq"), 0, 0, tiled=True, axis_index_groups=chip_groups
    )
    own = jnp.sum(spread.astype(jnp.float32), axis=0).astype(jnp.bfloat16)
    copies = jnp.broadcast_to(own[None], (samples, rows, lanes))
    total = lax.all_to_all(copies, "samp", 0, 0, tiled=True).reshape(-1)
    shares, at = [], 0
    for g, length in zip(grads, lengths):
        shares.append(total[at : at + length].reshape(g.shape[0] // runs, -1).astype(jnp.float32))
        at += length
    return shares


def body(
    atom_in,
    tok_in,
    atom_cond,
    single_cond,
    atom_pair,
    token_pair,
    atom_w_cond,
    atom_w_qkvg,
    atom_w_out,
    atom_w_up,
    atom_w_down,
    atom_w_pair,
    pool_weight,
    token_w_cond,
    token_w_qkvg,
    token_w_out,
    token_w_up,
    token_w_down,
    token_w_pair,
    cotangent,
):
    sample_count, atom_rows, atom_width = atom_in.shape
    tok_rows = tok_in.shape[1]
    n_windows = atom_rows // QWIN
    rim_width = (KWIN - QWIN) // 2
    atom_low = norm_stats(atom_cond.astype(jnp.float32), -1)[0].astype(jnp.bfloat16)
    single_low = norm_stats(single_cond.astype(jnp.float32), -1)[0].astype(jnp.bfloat16)
    atom_pair_low = (
        norm_stats(atom_pair.astype(jnp.float32), 0)[0]
        .astype(jnp.bfloat16)
        .reshape(atom_pair.shape[0], n_windows, QWIN, KWIN)
    )
    token_pair_low = norm_stats(token_pair.astype(jnp.float32), 0)[0].astype(jnp.bfloat16)
    atom_bias = jnp.einsum(
        "cwqk,ch->whqk", atom_pair_low, atom_w_pair, preferred_element_type=jnp.float32
    )
    token_bias = jnp.einsum(
        "cqk,hc->hqk", token_pair_low, token_w_pair, preferred_element_type=jnp.float32
    )
    window_index = lax.axis_index("seq") * n_windows + jnp.arange(n_windows, dtype=jnp.int32)
    key_index = (
        QWIN * window_index[:, None] - rim_width + jnp.arange(KWIN, dtype=jnp.int32)[None, :]
    )
    key_valid = (key_index >= 0) & (key_index < atom_rows * lax.axis_size("seq"))
    atom_heads = atom_w_pair.shape[1]
    token_heads = token_w_pair.shape[0]
    atom_fwd = functools.partial(
        atom_forward, score_bias=atom_bias, key_valid=key_valid, head_count=atom_heads
    )
    atom_bwd = functools.partial(
        atom_backward,
        score_bias=atom_bias,
        key_valid=key_valid,
        pair_low=atom_pair_low,
        head_count=atom_heads,
    )
    token_fwd = functools.partial(token_forward, score_bias=token_bias, head_count=token_heads)
    token_bwd = functools.partial(
        token_backward, score_bias=token_bias, pair_low=token_pair_low, head_count=token_heads
    )
    atom_weights = (atom_w_cond, atom_w_qkvg, atom_w_out, atom_w_up, atom_w_down)
    token_weights = (token_w_cond, token_w_qkvg, token_w_out, token_w_up, token_w_down)
    atom_out, atom_stored = block_forward(
        atom_in.astype(jnp.float32), atom_low, atom_weights, atom_fwd
    )
    per_token = atom_rows // tok_rows
    pooled_low = jnp.mean(
        atom_out.reshape(sample_count, tok_rows, per_token, atom_width), axis=2
    ).astype(jnp.bfloat16)
    token_start = tok_in.astype(jnp.float32) + product(pooled_low, pool_weight)
    token_out, token_stored = block_forward(token_start, single_low, token_weights, token_fwd)
    grad_start, token_grads = block_backward(
        cotangent.astype(jnp.float32), token_stored, single_low, token_weights, token_bwd
    )
    grad_pool = grad_start.astype(jnp.bfloat16)
    grad_pooled = product_right(grad_pool, pool_weight) / per_token
    grad_atom_out = jnp.broadcast_to(
        grad_pooled[:, :, None, :], (sample_count, tok_rows, per_token, atom_width)
    ).reshape(sample_count, atom_rows, atom_width)
    grad_atoms, atom_grads = block_backward(
        grad_atom_out, atom_stored, atom_low, atom_weights, atom_bwd
    )
    all_grads = atom_grads + (weight_grad(pooled_low, grad_pool),) + token_grads
    shares = reduce_weights(all_grads)
    return (token_out.astype(jnp.bfloat16), grad_atoms, grad_start) + tuple(shares)


def solution(mesh):
    in_specs = (
        P("samp", "seq", None),
        P("samp", "seq", None),
        P("seq", None),
        P("seq", None),
        P(None, "seq", None),
        P(None, "seq", None),
        P(),
        P(),
        P(),
        P(),
        P(),
        P(),
        P(),
        P(),
        P(),
        P(),
        P(),
        P(),
        P(),
        P("samp", "seq", None),
    )
    out_specs = (
        P("samp", "seq", None),
        P("samp", "seq", None),
        P("samp", "seq", None),
        P("seq", None),
        P("seq", None),
        P("seq", None),
        P("seq", None),
        P("seq", None),
        P("seq", None),
        P("seq", None),
        P("seq", None),
        P("seq", None),
        P("seq", None),
        P("seq", None),
        P("seq", None),
        P("seq", None),
    )
    return jax.shard_map(body, mesh=mesh, in_specs=in_specs, out_specs=out_specs, check_vma=False)
```

```python
import jax
import jax.numpy as jnp
from jax import lax
from jax.experimental import pallas as pl
from jax.experimental.pallas import tpu as pltpu
from jax.sharding import PartitionSpec as P

eps = 1e-05
masked = -1000000000.0

MIB = 1 << 20
F32, BF16 = jnp.float32, jnp.bfloat16


def kernel_call(kernel, out_shape, grid=(1,), in_specs=None, out_specs=None, scratch=(), vmem=60, flops=0, moved=0, name=None):
    def run(*args):
        return pl.pallas_call(
            kernel,
            out_shape=list(out_shape),
            grid=grid,
            in_specs=in_specs or [fixed(*a.shape) for a in args],
            out_specs=out_specs or [fixed(*o.shape) for o in out_shape],
            scratch_shapes=list(scratch),
            compiler_params=pltpu.CompilerParams(vmem_limit_bytes=vmem * MIB),
            cost_estimate=pl.CostEstimate(flops=flops, bytes_accessed=moved, transcendentals=0),
            name=name,
        )(*args)

    return run


def fixed(*shape):
    return pl.BlockSpec(shape, lambda *_: (0,) * len(shape), pipeline_mode=pl.Buffered(1))


def dot(left, right, over=((1,), (0,))):
    return lax.dot_general(left, right, (over, ((), ())), preferred_element_type=F32)


def swap_halves(first, second):
    low = lax.broadcasted_iota(jnp.int32, first.shape, 1) < 64
    half = first.shape[1] // 2
    return (
        jnp.where(low, first, pltpu.roll(second, half, 1)),
        jnp.where(low, pltpu.roll(first, half, 1), second),
    )


def runs_to_tokens(runs_ref, tokens_ref):
    for pair in range(runs_ref.shape[0] // 2):
        for duo in range(2):
            lanes = slice(128 * duo, 128 * duo + 128)
            made = swap_halves(
                runs_ref[2 * pair, :, lanes].astype(F32), runs_ref[2 * pair + 1, :, lanes].astype(F32)
            )
            for k in range(2):
                tokens_ref[2 * duo + k, :, 128 * pair : 128 * pair + 128] = made[k].astype(
                    tokens_ref.dtype
                )


def tokens_to_runs(tokens_ref, runs_ref):
    for pair in range(runs_ref.shape[0] // 2):
        lanes = slice(128 * pair, 128 * pair + 128)
        for duo in range(2):
            made = swap_halves(tokens_ref[2 * duo, :, lanes], tokens_ref[2 * duo + 1, :, lanes])
            for k in range(2):
                runs_ref[2 * pair + k, :, 128 * duo : 128 * duo + 128] = made[k].astype(runs_ref.dtype)


HS = 48
NT = 1024
QB = 256


def attention_kernel(runs_ref, bias_ref, qkv_ref, probs_ref, out_ref, heads_ref):
    sample = pl.program_id(0)

    @pl.when(sample == 0)
    def _():
        runs_to_tokens(runs_ref, qkv_ref)

    keys = qkv_ref[sample, HS : 2 * HS, :]
    values = qkv_ref[sample, 2 * HS :, :]

    @pl.loop(0, NT // QB)
    def _(block):
        rows = pl.ds(pl.multiple_of(block * QB, QB), QB)
        scores = dot(qkv_ref[sample, :HS, rows], keys, ((0,), (0,))) * HS ** (-0.5)
        scores += jnp.concatenate([bias_ref[i, rows, :] for i in range(8)], axis=1).astype(F32)
        exponent = jnp.exp(scores - jnp.max(scores, axis=1, keepdims=True))
        probs = exponent * (1.0 / jnp.sum(exponent, axis=1, keepdims=True))
        probs = probs.astype(BF16)
        probs_ref[0, rows, :] = probs
        heads_ref[sample, :, rows] = dot(probs, values, ((1,), (1,))).T

    @pl.when(sample == 3)
    def _():
        tokens_to_runs(heads_ref, out_ref)


def token_attention(runs, bias):
    return kernel_call(
        attention_kernel,
        [
            jax.ShapeDtypeStruct((4, 3 * HS, NT), BF16),
            jax.ShapeDtypeStruct((4, NT, NT), BF16),
            jax.ShapeDtypeStruct((16, HS, 256), BF16),
        ],
        grid=(4,),
        in_specs=[fixed(16, 3 * HS, 256), fixed(8, NT, 128)],
        out_specs=[fixed(4, 3 * HS, NT), pl.BlockSpec((1, NT, NT), lambda s: (s, 0, 0)), fixed(16, HS, 256)],
        scratch=[pltpu.VMEM((4, HS, NT), F32)],
        flops=4 * 4 * NT * NT * HS * 5,
        moved=14 * MIB,
        name="token_attention",
    )(runs, bias)


def attention_back_kernel(
    qkv_ref, probs_ref, cot_ref, out_ref, pair_ref, cots_ref, grads_ref, total_ref
):
    sample = pl.program_id(0)

    @pl.when(sample == 0)
    def _():
        runs_to_tokens(cot_ref, cots_ref)

    keys = qkv_ref[sample, HS : 2 * HS, :]
    values = qkv_ref[sample, 2 * HS :, :]

    @pl.loop(0, NT // QB)
    def _(block):
        rows = pl.ds(pl.multiple_of(block * QB, QB), QB)
        cots = cots_ref[sample, :, rows]
        low = probs_ref[0, rows, :]
        probs = low.astype(F32)
        weighed = probs * dot(cots, values, ((0,), (0,)))
        slopes = weighed - probs * jnp.sum(weighed, axis=1, keepdims=True)
        slopes_low = slopes.astype(BF16)

        @pl.when(sample == 0)
        def _():
            total_ref[rows, :] = slopes

        @pl.when(sample > 0)
        def _():
            total_ref[rows, :] += slopes

        grads_ref[sample, :HS, rows] = dot(keys, slopes_low, ((1,), (1,))) * HS ** (-0.5)
        key_part = dot(qkv_ref[sample, :HS, rows], slopes_low) * HS ** (-0.5)
        value_part = dot(cots, low)

        @pl.when(block == 0)
        def _():
            grads_ref[sample, HS : 2 * HS, :] = key_part
            grads_ref[sample, 2 * HS :, :] = value_part

        @pl.when(block > 0)
        def _():
            grads_ref[sample, HS : 2 * HS, :] += key_part
            grads_ref[sample, 2 * HS :, :] += value_part

    @pl.when(sample == 3)
    def _():
        tokens_to_runs(grads_ref, out_ref)
        for i in range(8):
            pair_ref[i] = total_ref[:, 128 * i : 128 * i + 128].astype(BF16)


def token_attention_back(qkv, probs, cots):
    return kernel_call(
        attention_back_kernel,
        [jax.ShapeDtypeStruct((16, 3 * HS, 256), BF16), jax.ShapeDtypeStruct((8, NT, 128), BF16)],
        grid=(4,),
        in_specs=[fixed(4, 3 * HS, NT), pl.BlockSpec((1, NT, NT), lambda s: (s, 0, 0)), fixed(16, HS, 256)],
        out_specs=[fixed(16, 3 * HS, 256), fixed(8, NT, 128)],
        scratch=[
            pltpu.VMEM((4, HS, NT), BF16),
            pltpu.VMEM((4, 3 * HS, NT), F32),
            pltpu.VMEM((NT, NT), F32),
        ],
        flops=4 * 8 * NT * NT * HS * 5,
        moved=14 * MIB,
        name="token_attention_back",
    )(qkv, probs, cots)


def pair_kernel(pair_ref, weight_ref, normed_ref, bias_ref):
    pair = pair_ref[...].astype(F32)
    centred = pair - jnp.mean(pair, axis=1, keepdims=True)
    inverse = lax.rsqrt(jnp.mean(centred * centred, axis=1, keepdims=True) + eps)
    low = (centred * inverse).astype(BF16)
    normed_ref[...] = low
    weight = weight_ref[...]
    bias = jnp.stack([dot(weight, low[i]) for i in range(low.shape[0])], axis=0)
    bias_ref[...] = jnp.swapaxes(bias, 0, 1).astype(BF16)


def pair_bias(pair, weight):
    return kernel_call(
        pair_kernel,
        [jax.ShapeDtypeStruct((64, 128, 128), BF16), jax.ShapeDtypeStruct((16, 64, 128), BF16)],
        grid=(4,),
        in_specs=[pl.BlockSpec((16, 128, 128), lambda i: (i, 0, 0)), fixed(16, 128)],
        out_specs=[pl.BlockSpec((16, 128, 128), lambda i: (i, 0, 0)), pl.BlockSpec((16, 16, 128), lambda i: (0, i, 0))],
        flops=1 << 30,
        moved=8 * MIB,
        name="pair_bias",
    )(pair, weight)


def pair_back_kernel(slopes_ref, normed_ref, grad_ref):
    slopes = slopes_ref[0].astype(F32)
    for i in range(1, 8):
        slopes += slopes_ref[i].astype(F32)
    slopes = jnp.swapaxes(slopes, 0, 1).astype(BF16)
    part = dot(slopes[0], normed_ref[0], ((1,), (1,)))
    for i in range(1, slopes.shape[0]):
        part += dot(slopes[i], normed_ref[i], ((1,), (1,)))

    @pl.when(pl.program_id(0) == 0)
    def _():
        grad_ref[...] = part

    @pl.when(pl.program_id(0) > 0)
    def _():
        grad_ref[...] += part


def pair_grad(slopes, normed):
    return kernel_call(
        pair_back_kernel,
        [jax.ShapeDtypeStruct((16, 128), F32)],
        grid=(4,),
        in_specs=[
            pl.BlockSpec((8, 16, 16, 128), lambda i: (0, 0, i, 0)),
            pl.BlockSpec((16, 128, 128), lambda i: (i, 0, 0)),
        ],
        out_specs=[fixed(16, 128)],
        flops=1 << 30,
        moved=8 * MIB,
        name="pair_grad",
    )(slopes, normed)[0]


DA, DT, FT, FA = 128, 768, 1536, 256
RIM = 48
SPAN = 256 + 2 * RIM


def normed(x):
    centred = x - jnp.mean(x, axis=-1, keepdims=True)
    inverse = lax.rsqrt(jnp.mean(centred * centred, axis=-1, keepdims=True) + eps)
    return centred * inverse, inverse


def sigmoid(x):
    return 1.0 / (1.0 + jnp.exp(-x))


def head_rows(rows):
    head = lax.broadcasted_iota(jnp.int32, rows.shape, 1) // 32
    return jnp.concatenate([jnp.where(head == h, rows, 0.0) for h in range(4)], axis=0).astype(BF16)


def rows_of_heads(full):
    head = lax.broadcasted_iota(jnp.int32, (32, 128), 1) // 32
    made = jnp.where(head == 0, full[:32], 0.0)
    for h in range(1, 4):
        made = jnp.where(head == h, full[32 * h : 32 * h + 32], made)
    return made


def pair_norm(pair):
    centred = pair - jnp.mean(pair, axis=0, keepdims=True)
    inverse = lax.rsqrt(jnp.mean(centred * centred, axis=0, keepdims=True) + eps)
    return (centred * inverse).astype(BF16).astype(F32)


def part(ref, i, width, rows=slice(None)):
    return ref[rows, i * width : (i + 1) * width]


def front_kernel(
    x_ref, prev_ref, next_ref, cond_ref, pair_ref, mask_ref, w_pair_ref, w_cond_ref, w_qkvg_ref, w_out_ref,
    w_up_ref, w_down_ref, pool_ref, tok_ref, single_ref, tw_cond_ref, tw_qkvg_ref,
    first_ref, q_ref, kv_ref, probs_ref, gate_ref, att_ref, mid_ref, cond_low_ref, u_ref, pooled_ref,
    start_ref, tfirst_ref, tgate_ref, tu_ref, single_low_ref, runs_ref,
    bias_ref, y_ref, uh_ref,
):
    cond = jnp.concatenate([prev_ref[4], cond_ref[...], next_ref[4]], axis=0).astype(F32)
    cond_low = normed(cond)[0].astype(BF16)
    cond_low_ref[...] = cond_low[RIM : RIM + 256]
    u_ref[...] = dot(cond_low[RIM : RIM + 256], w_cond_ref[...])
    uh_ref[...] = dot(cond_low, w_cond_ref[:, : 2 * DA])
    pairs = pair_norm(pair_ref[...].astype(F32))
    for h in range(4):
        bias = pairs[0] * w_pair_ref[0, h]
        for c in range(1, 16):
            bias += pairs[c] * w_pair_ref[c, h]
        for w in range(8):
            bias_ref[w, 32 * h : 32 * h + 32, :] = bias[32 * w : 32 * w + 32] + mask_ref[w : w + 1, :]

    @pl.loop(0, 4)
    def _(s):
        x = jnp.concatenate([prev_ref[s], x_ref[s], next_ref[s]], axis=0).astype(F32)
        first = (sigmoid(part(uh_ref, 0, DA)) * normed(x)[0] + part(uh_ref, 1, DA)).astype(BF16)
        projected = dot(first, w_qkvg_ref[...])
        own = projected[RIM : RIM + 256]
        first_ref[s] = first[RIM : RIM + 256]
        query = own[:, :DA].astype(BF16)
        q_ref[s] = query
        kv_ref[s] = projected[:, DA : 3 * DA].astype(BF16)
        gate = sigmoid(own[:, 3 * DA :])
        gate_ref[s] = gate
        made = []
        for w in range(8):
            keys = kv_ref[s, 32 * w : 32 * w + 128, :DA]
            values = kv_ref[s, 32 * w : 32 * w + 128, DA:]
            rows = head_rows(query[32 * w : 32 * w + 32].astype(F32))
            scores = dot(rows, keys, ((1,), (1,))) * 32 ** (-0.5) + bias_ref[w]
            exponent = jnp.exp(scores - jnp.max(scores, axis=1, keepdims=True))
            probs = (exponent * (1.0 / jnp.sum(exponent, axis=1, keepdims=True))).astype(BF16)
            probs_ref[s, w] = probs
            made.append(rows_of_heads(dot(probs, values)))
        attended = jnp.concatenate(made, axis=0)
        att_ref[s] = attended
        branch = dot((gate * attended).astype(BF16), w_out_ref[...])
        middle = x[RIM : RIM + 256] + sigmoid(part(u_ref, 2, DA)) * branch
        mid_ref[s] = middle
        second = (sigmoid(part(u_ref, 3, DA)) * normed(middle)[0] + part(u_ref, 4, DA)).astype(BF16)
        up = dot(second, w_up_ref[...])
        hidden = (up[:, :FA] * sigmoid(up[:, :FA]) * up[:, FA:]).astype(BF16)
        y_ref[...] = middle + sigmoid(part(u_ref, 5, DA)) * dot(hidden, w_down_ref[...])
        pooled = y_ref[pl.ds(0, 64, stride=4), :]
        for k in range(1, 4):
            pooled += y_ref[pl.ds(k, 64, stride=4), :]
        pooled_ref[s] = (pooled * 0.25).astype(BF16)

    single_low = normed(single_ref[...].astype(F32))[0].astype(BF16)
    single_low_ref[...] = single_low
    for i in range(6):
        tu_ref[:, DT * i : DT * i + DT] = dot(single_low, tw_cond_ref[:, DT * i : DT * i + DT])
    pooled = pooled_ref[...].reshape(256, DA)
    start = tok_ref[...].reshape(256, DT).astype(F32) + dot(pooled, pool_ref[...])
    start_ref[...] = start
    lines = normed(start)[0]
    scale, shift = sigmoid(part(tu_ref, 0, DT)), part(tu_ref, 1, DT)
    for s in range(4):
        tfirst_ref[64 * s : 64 * s + 64, :] = (scale * lines[64 * s : 64 * s + 64] + shift).astype(BF16)
    first = tfirst_ref[...]
    for i in range(3):
        turned = dot(first, part(tw_qkvg_ref, i, DT)).T.astype(BF16)
        for h in range(16):
            runs_ref[h, HS * i : HS * i + HS, :] = turned[HS * h : HS * h + HS]
    tgate_ref[...] = sigmoid(dot(first, part(tw_qkvg_ref, 3, DT)))


def front(*args):
    sds = jax.ShapeDtypeStruct
    specs = [fixed(*a.shape) for a in args]
    specs[6] = pl.BlockSpec(memory_space=pltpu.SMEM)
    return kernel_call(
        front_kernel,
        [
            sds((4, 256, DA), BF16), sds((4, 256, DA), BF16), sds((4, SPAN, 2 * DA), BF16),
            sds((4, 8, 128, 128), BF16), sds((4, 256, DA), F32), sds((4, 256, DA), F32),
            sds((4, 256, DA), F32), sds((256, DA), BF16), sds((256, 6 * DA), F32), sds((4, 64, DA), BF16),
            sds((256, DT), F32), sds((256, DT), BF16), sds((256, DT), F32), sds((64, 6 * DT), F32),
            sds((64, 384), BF16), sds((16, 3 * HS, 256), BF16),
        ],
        in_specs=specs,
        scratch=[pltpu.VMEM((8, 128, 128), F32), pltpu.VMEM((256, DA), F32), pltpu.VMEM((SPAN, 2 * DA), F32)],
        flops=3 << 30,
        moved=40 * MIB,
        name="front",
    )(*args)


def slope(squashed):
    return squashed * (1.0 - squashed)


def norm_back_rows(gradient, lines, inverse):
    return inverse * (
        gradient
        - jnp.mean(gradient, axis=-1, keepdims=True)
        - lines * jnp.mean(gradient * lines, axis=-1, keepdims=True)
    )


def turn_kernel(
    runs_ref, tgate_ref, start_ref, tu_ref, cot_ref, w_out_ref, w_up_ref, w_down_ref,
    out_ref, cots_ref, dgate_ref, dmid_ref, a_ref, gbranch_ref, second_ref, dup_ref, hidden_ref, gdown_ref,
    du_ref,
    up_ref, mid_ref, branch_ref, down_ref,
):
    attended = runs_ref[...].reshape(DT, 256).astype(F32).T
    gate = tgate_ref[...]
    gated = (gate * attended).astype(BF16)
    a_ref[...] = gated
    branch_ref[...] = dot(gated, w_out_ref[...])
    gate_a, scale_b, shift_b, gate_b = (
        sigmoid(part(tu_ref, 2, DT)), sigmoid(part(tu_ref, 3, DT)), part(tu_ref, 4, DT), sigmoid(part(tu_ref, 5, DT)),
    )
    runs = [slice(64 * s, 64 * s + 64) for s in range(4)]
    for r in runs:
        middle = start_ref[r, :] + gate_a * branch_ref[r, :]
        mid_ref[r, :] = middle
        second_ref[r, :] = (scale_b * normed(middle)[0] + shift_b).astype(BF16)
    second = second_ref[...]
    cut = 512
    for j in range(FT // cut):
        e = dot(second, w_up_ref[:, cut * j : cut * j + cut])
        f = dot(second, w_up_ref[:, FT + cut * j : FT + cut * j + cut])
        up_ref[:, cut * j : cut * j + cut] = e
        up_ref[:, FT + cut * j : FT + cut * j + cut] = f
        hidden = (e * sigmoid(e) * f).astype(BF16)
        hidden_ref[:, cut * j : cut * j + cut] = hidden
        piece = dot(hidden, w_down_ref[cut * j : cut * j + cut, :])
        if j == 0:
            down_ref[...] = piece
        else:
            down_ref[...] += piece
    total = jnp.zeros((64, DT), F32)
    for s, r in enumerate(runs):
        cot = cot_ref[s].astype(F32)
        out_ref[s] = (mid_ref[r, :] + gate_b * down_ref[r, :]).astype(BF16)
        gdown_ref[r, :] = (cot * gate_b).astype(BF16)
        total += cot * down_ref[r, :]
    du_ref[:, 3 * DT :] = (total * slope(gate_b)).astype(BF16)
    gdown = gdown_ref[...]
    dsecond = jnp.zeros((256, DT), F32)
    for j in range(FT // cut):
        dhidden = dot(gdown, w_down_ref[cut * j : cut * j + cut, :], ((1,), (1,)))
        e = up_ref[:, cut * j : cut * j + cut]
        f = up_ref[:, FT + cut * j : FT + cut * j + cut]
        half = sigmoid(e)
        de = (dhidden * f * half * (1.0 + e * (1.0 - half))).astype(BF16)
        df = (dhidden * e * half).astype(BF16)
        dup_ref[:, cut * j : cut * j + cut] = de
        dup_ref[:, FT + cut * j : FT + cut * j + cut] = df
        piece = dot(de, w_up_ref[:, cut * j : cut * j + cut], ((1,), (1,)))
        piece += dot(df, w_up_ref[:, FT + cut * j : FT + cut * j + cut], ((1,), (1,)))
        dsecond += piece
    down_ref[...] = dsecond
    total_a = jnp.zeros((64, DT), F32)
    total_b = jnp.zeros((64, DT), F32)
    total_c = jnp.zeros((64, DT), F32)
    for s, r in enumerate(runs):
        d = down_ref[r, :]
        lines, inverse = normed(mid_ref[r, :])
        dmid = cot_ref[s].astype(F32) + norm_back_rows(d * scale_b, lines, inverse)
        dmid_ref[r, :] = dmid
        gbranch_ref[r, :] = (dmid * gate_a).astype(BF16)
        total_a += dmid * branch_ref[r, :]
        total_b += d * lines
        total_c += d
    du_ref[:, :DT] = (total_a * slope(gate_a)).astype(BF16)
    du_ref[:, DT : 2 * DT] = (total_b * slope(scale_b)).astype(BF16)
    du_ref[:, 2 * DT : 3 * DT] = total_c.astype(BF16)
    dgated = dot(gbranch_ref[...], w_out_ref[...], ((1,), (1,)))
    dgate_ref[...] = (dgated * attended * slope(gate)).astype(BF16)
    cots_ref[...] = (dgated * gate).T.astype(BF16).reshape(16, HS, 256)


def turn(*args):
    sds = jax.ShapeDtypeStruct
    rows = lambda n, t=BF16: sds((256, n), t)
    return kernel_call(
        turn_kernel,
        [
            sds((4, 64, DT), BF16), sds((16, HS, 256), BF16), rows(DT), rows(DT, F32), rows(DT), rows(DT),
            rows(DT), rows(2 * FT), rows(FT), rows(DT), sds((64, 4 * DT), BF16),
        ],
        scratch=[pltpu.VMEM((256, 2 * FT), F32)] + [pltpu.VMEM((256, DT), F32)] * 3,
        flops=5 << 30,
        moved=24 * MIB,
        name="turn",
    )(*args)


def weights_kernel(
    a_ref, gbranch_ref, first_ref, dgate_ref, second_ref, dup_ref, hidden_ref, gdown_ref, single_ref, du_ref, du_next_ref,
    out_ref, kept_ref,
):
    step = pl.program_id(0)

    def square(left, right):
        out_ref[...] = dot(left[...], right[...], ((0,), (0,))).astype(BF16)

    @pl.when(step < 4)
    def _():
        square(second_ref, dup_ref)

    @pl.when(step == 4)
    def _():
        square(a_ref, gbranch_ref)

    @pl.when(step == 5)
    def _():
        square(first_ref, dgate_ref)

    @pl.when(step == 6)
    def _():
        for half in range(2):
            lanes = slice(384 * half, 384 * half + 384)
            made = dot(hidden_ref[...], gdown_ref[:, lanes], ((0,), (0,))).astype(BF16).reshape(16, 2, 48, 384)
            out_ref[:, lanes] = made[:, 0].reshape(DT, 384)
            kept_ref[:, lanes] = made[:, 1].reshape(DT, 384)

    @pl.when(step == 7)
    def _():
        out_ref[...] = kept_ref[...]

    @pl.when(step >= 8)
    def _():
        upper = dot(single_ref[...], du_ref[...], ((0,), (0,))).reshape(16, 24, DT)
        lower = dot(single_ref[...], du_next_ref[...], ((0,), (0,))).reshape(16, 24, DT)
        out_ref[...] = jnp.concatenate([upper, lower], axis=1).reshape(DT, DT).astype(BF16)


def token_weights(a, gbranch, first, dgate, second, dup, hidden, gdown, single_low, du):
    def late(first):
        return pl.BlockSpec((64, DT), lambda i: (0, first + jnp.maximum(i - 8, 0)))

    return kernel_call(
        weights_kernel,
        [jax.ShapeDtypeStruct((DT, 10 * DT), BF16)],
        grid=(10,),
        in_specs=[fixed(256, DT)] * 5
        + [
            pl.BlockSpec((256, DT), lambda i: (0, jnp.minimum(i, 3))),
            fixed(256, FT),
            fixed(256, DT),
            fixed(64, 384),
            late(0),
            late(2),
        ],
        out_specs=[pl.BlockSpec((DT, DT), lambda i: (0, i))],
        scratch=[pltpu.VMEM((DT, DT), BF16)],
        flops=2 * 256 * DT * 8 * DT,
        moved=20 * MIB,
        name="token_weights",
    )(a, gbranch, first, dgate, second, dup, hidden, gdown, single_low, du, du)[0]


def head_weights_kernel(grads_ref, lines_ref, out_ref, total_ref):
    run = pl.program_id(0)

    @pl.when(run == 0)
    def _():
        total_ref[...] = jnp.zeros_like(total_ref)

    for k in range(4):
        total_ref[...] += dot(grads_ref[k], lines_ref[k])

    @pl.when(run == 3)
    def _():
        out_ref[...] = total_ref[...].T.astype(BF16).reshape(16, 48, 3 * HS)


def head_weights(grads, lines):
    return kernel_call(
        head_weights_kernel,
        [jax.ShapeDtypeStruct((16, 48, 3 * HS), BF16)],
        grid=(4,),
        in_specs=[
            pl.BlockSpec((4, 3 * HS, 256), lambda i: (i, 0, 0)),
            pl.BlockSpec((4, 256, DT), lambda i: (i, 0, 0)),
        ],
        out_specs=[fixed(16, 48, 3 * HS)],
        scratch=[pltpu.VMEM((3 * HS, DT), F32)],
        flops=2 * 4096 * DT * 256,
        moved=8 * MIB,
        name="head_weights",
    )(grads, lines)[0]


def back_kernel(
    runs_ref, dgate_ref, dmid_ref, start_ref, tu_ref, w_qkvg_ref, pool_ref, pooled_ref,
    out_ref, gpooled_ref, dpool_ref, ducat_ref,
    dfirst_ref, gpool_ref,
):
    dfirst = dot(dgate_ref[...], part(w_qkvg_ref, 3, DT), ((1,), (1,)))
    for i in range(3):
        piece = runs_ref[:, HS * i : HS * i + HS, :].reshape(DT, 256)
        dfirst += dot(piece.astype(F32).T.astype(BF16), part(w_qkvg_ref, i, DT), ((1,), (1,)))
    dfirst_ref[...] = dfirst
    scale = sigmoid(part(tu_ref, 0, DT))
    total_a = jnp.zeros((64, DT), F32)
    total_b = jnp.zeros((64, DT), F32)
    for s in range(4):
        r = slice(64 * s, 64 * s + 64)
        d = dfirst_ref[r, :]
        lines, inverse = normed(start_ref[r, :])
        grad = dmid_ref[r, :] + norm_back_rows(d * scale, lines, inverse)
        out_ref[s] = grad
        gpool_ref[r, :] = grad.astype(BF16)
        total_a += d * lines
        total_b += d
    ducat_ref[:, :DT] = (total_a * slope(scale)).astype(BF16)
    ducat_ref[:, DT : 2 * DT] = total_b.astype(BF16)
    gpool = gpool_ref[...]
    gpooled_ref[...] = dot(gpool, pool_ref[...], ((1,), (1,))) * 0.25
    dpool_ref[...] = dot(pooled_ref[...].reshape(256, DA), gpool, ((0,), (0,)))


def back(*args):
    sds = jax.ShapeDtypeStruct
    return kernel_call(
        back_kernel,
        [sds((4, 64, DT), F32), sds((256, DA), F32), sds((DA, DT), F32), sds((64, 2 * DT), BF16)],
        scratch=[pltpu.VMEM((256, DT), F32), pltpu.VMEM((256, DT), BF16)],
        flops=3 << 29,
        moved=12 * MIB,
        name="back",
    )(*args)


def atom_back_kernel(
    gpooled_ref, u_ref, mid_ref, gate_ref, att_ref, q_ref, kv_ref, probs_ref, pair_ref, w_out_ref, w_up_ref,
    w_down_ref,
    dq_ref, dgate_ref, dkv_ref, prev_ref, next_ref, dmid_ref, du_ref, dw_out_ref, dw_up_ref, dw_down_ref, dpair_ref,
    dy_ref, grads_ref, slopes_ref, sums_ref,
):
    gate_a, scale_b, shift_b, gate_b = (
        sigmoid(part(u_ref, 2, DA)), sigmoid(part(u_ref, 3, DA)), part(u_ref, 4, DA), sigmoid(part(u_ref, 5, DA)),
    )
    sums_ref[...] = jnp.zeros_like(sums_ref)
    slopes_ref[...] = jnp.zeros_like(slopes_ref)
    dw_out_ref[...] = jnp.zeros_like(dw_out_ref)
    dw_up_ref[...] = jnp.zeros_like(dw_up_ref)
    dw_down_ref[...] = jnp.zeros_like(dw_down_ref)

    @pl.loop(0, 4)
    def _(s):
        for k in range(4):
            dy_ref[pl.ds(k, 64, stride=4), :] = gpooled_ref[s]
        dy = dy_ref[...]
        middle = mid_ref[s]
        lines, inverse = normed(middle)
        second = (scale_b * lines + shift_b).astype(BF16)
        up = dot(second, w_up_ref[...])
        e, f = up[:, :FA], up[:, FA:]
        half = sigmoid(e)
        hidden = (e * half * f).astype(BF16)
        down = dot(hidden, w_down_ref[...])
        gdown = (dy * gate_b).astype(BF16)
        dhidden = dot(gdown, w_down_ref[...], ((1,), (1,)))
        de = dhidden * f * half * (1.0 + e * (1.0 - half))
        df = dhidden * e * half
        dup = jnp.concatenate([de, df], axis=1).astype(BF16)
        dsecond = dot(dup, w_up_ref[...], ((1,), (1,)))
        dmid = dy + norm_back_rows(dsecond * scale_b, lines, inverse)
        dmid_ref[s] = dmid
        gate, attended = gate_ref[s], att_ref[s]
        gated = (gate * attended).astype(BF16)
        branch = dot(gated, w_out_ref[...])
        gbranch = (dmid * gate_a).astype(BF16)
        sums_ref[:, :DA] += dmid * branch
        sums_ref[:, DA : 2 * DA] += dsecond * lines
        sums_ref[:, 2 * DA : 3 * DA] += dsecond
        sums_ref[:, 3 * DA :] += dy * down
        dgated = dot(gbranch, w_out_ref[...], ((1,), (1,)))
        dgate_ref[s] = (dgated * attended * slope(gate)).astype(BF16)
        cots = dgated * gate
        dw_out_ref[...] += dot(gated, gbranch, ((0,), (0,)))
        dw_up_ref[...] += dot(second, dup, ((0,), (0,)))
        dw_down_ref[...] += dot(hidden, gdown, ((0,), (0,)))
        grads_ref[s] = jnp.zeros((SPAN, 2 * DA), F32)
        made = []
        for w in range(8):
            span = slice(32 * w, 32 * w + 128)
            keys, values = kv_ref[s, span, :DA], kv_ref[s, span, DA:]
            rows = head_rows(q_ref[s, 32 * w : 32 * w + 32, :].astype(F32))
            cot = head_rows(cots[32 * w : 32 * w + 32])
            low = probs_ref[s, w]
            probs = low.astype(F32)
            weighed = probs * dot(cot, values, ((1,), (1,)))
            slopes = weighed - probs * jnp.sum(weighed, axis=1, keepdims=True)
            slopes_ref[w] += slopes
            slopes_low = slopes.astype(BF16)
            made.append(rows_of_heads(dot(slopes_low, keys)) * 32 ** (-0.5))
            grads_ref[s, span, :DA] += dot(slopes_low, rows, ((0,), (0,))) * 32 ** (-0.5)
            grads_ref[s, span, DA:] += dot(low, cot, ((0,), (0,)))
        dq_ref[s] = jnp.concatenate(made, axis=0).astype(BF16)
        dkv_ref[s] = grads_ref[s, RIM : RIM + 256, :]
        prev_ref[s] = grads_ref[s, :RIM, :].astype(BF16)
        next_ref[s] = grads_ref[s, RIM + 256 :, :].astype(BF16)

    du_ref[:, :DA] = sums_ref[:, :DA] * slope(gate_a)
    du_ref[:, DA : 2 * DA] = sums_ref[:, DA : 2 * DA] * slope(scale_b)
    du_ref[:, 2 * DA : 3 * DA] = sums_ref[:, 2 * DA : 3 * DA]
    du_ref[:, 3 * DA :] = sums_ref[:, 3 * DA :] * slope(gate_b)
    pairs = pair_norm(pair_ref[...].astype(F32))
    for h in range(4):
        slopes = jnp.concatenate([slopes_ref[w, 32 * h : 32 * h + 32, :] for w in range(8)], axis=0)
        for c in range(16):
            dpair_ref[16 * h + c : 16 * h + c + 1, :] = jnp.sum(slopes * pairs[c], axis=0, keepdims=True)


def atom_back(*args):
    sds = jax.ShapeDtypeStruct
    return kernel_call(
        atom_back_kernel,
        [
            sds((4, 256, DA), BF16), sds((4, 256, DA), BF16), sds((4, 256, 2 * DA), F32),
            sds((4, RIM, 2 * DA), BF16), sds((4, RIM, 2 * DA), BF16), sds((4, 256, DA), F32),
            sds((256, 4 * DA), F32), sds((DA, DA), F32), sds((DA, 2 * FA), F32), sds((FA, DA), F32), sds((64, 128), F32),
        ],
        scratch=[
            pltpu.VMEM((256, DA), F32), pltpu.VMEM((4, SPAN, 2 * DA), F32), pltpu.VMEM((8, 128, 128), F32),
            pltpu.VMEM((256, 4 * DA), F32),
        ],
        flops=3 << 29,
        moved=12 * MIB,
        name="atom_back",
    )(*args)


def atom_end_kernel(
    dq_ref, dgate_ref, dkv_ref, prev_ref, next_ref, dmid_ref, x_ref, first_ref, u_ref, du_ref, cond_low_ref,
    w_qkvg_ref, dw_out_ref, dw_up_ref, dw_down_ref, dpool_ref, misc_ref, single_ref, tdu_ref, narrow_ref,
    out_ref, packed_ref,
    dw_qkvg_ref, sums_ref, whole_ref,
):
    scale = sigmoid(part(u_ref, 0, DA))
    sums_ref[...] = jnp.zeros_like(sums_ref)
    dw_qkvg_ref[...] = jnp.zeros_like(dw_qkvg_ref)

    @pl.loop(0, 4)
    def _(s):
        whole_ref[...] = dkv_ref[s]
        whole_ref[:RIM, :] += prev_ref[s].astype(F32)
        whole_ref[256 - RIM :, :] += next_ref[s].astype(F32)
        grads = jnp.concatenate([dq_ref[s], whole_ref[...].astype(BF16), dgate_ref[s]], axis=1)
        dfirst = dot(grads, w_qkvg_ref[...], ((1,), (1,)))
        lines, inverse = normed(x_ref[s].astype(F32))
        out_ref[s] = dmid_ref[s] + norm_back_rows(dfirst * scale, lines, inverse)
        dw_qkvg_ref[...] += dot(first_ref[s], grads, ((0,), (0,)))
        sums_ref[:, :DA] += dfirst * lines
        sums_ref[:, DA:] += dfirst

    du = jnp.concatenate([sums_ref[:, :DA] * slope(scale), sums_ref[:, DA:], du_ref[...]], axis=1).astype(BF16)
    dw_cond = dot(cond_low_ref[...], du, ((0,), (0,)))
    down = dw_down_ref[...].reshape(16, 2, 8, DA)
    single = dot(single_ref[...], tdu_ref[...], ((0,), (0,))).reshape(16, 3, 8, 2 * DT)
    whole = jnp.concatenate(
        [
            dw_cond, dw_qkvg_ref[...], dw_out_ref[...], dw_up_ref[...], dpool_ref[...],
            down[:, 0].reshape(DA, DA), down[:, 1].reshape(DA, DA), misc_ref[...],
        ]
        + [single[:, i].reshape(DA, 2 * DT) for i in range(3)]
        + [jnp.zeros((DA, 512), F32)],
        axis=1,
    ).astype(BF16)
    for s in range(8):
        packed_ref[s, :, :1024] = whole[:, 1024 * s : 1024 * s + 1024]
        packed_ref[s, :, 1024:] = narrow_ref[s]


def atom_end(*args):
    sds = jax.ShapeDtypeStruct
    return kernel_call(
        atom_end_kernel,
        [sds((4, 256, DA), F32), sds((8, DA, 1152), BF16)],
        scratch=[pltpu.VMEM((DA, 4 * DA), F32), pltpu.VMEM((256, 2 * DA), F32), pltpu.VMEM((256, 2 * DA), F32)],
        flops=1 << 29,
        moved=8 * MIB,
        name="atom_end",
    )(*args)


def both_axes(x):
    return lax.all_to_all(x, ("samp", "seq"), 0, 0, tiled=True)


def along_seq(x):
    return lax.all_to_all(x, "seq", 0, 0, tiled=True)


def handed_on(x):
    return lax.all_to_all(jnp.broadcast_to(x[None], (8, *x.shape)), "samp", 0, 0, tiled=True)


ordered = lambda *x: lax.optimization_barrier(x)


def summed(x):
    return jnp.sum(x.astype(F32), axis=0).astype(BF16)


def body(
    atom_in,
    tok_in,
    atom_cond,
    single_cond,
    atom_pair,
    token_pair,
    atom_w_cond,
    atom_w_qkvg,
    atom_w_out,
    atom_w_up,
    atom_w_down,
    atom_w_pair,
    pool_weight,
    token_w_cond,
    token_w_qkvg,
    token_w_out,
    token_w_up,
    token_w_down,
    token_w_pair,
    cotangent,
):
    samp, seq = lax.axis_index("samp"), lax.axis_index("seq")
    up, down = [(i, i + 1) for i in range(15)], [(i + 1, i) for i in range(15)]
    rims = jnp.concatenate([atom_in, atom_cond[None]], axis=0)
    from_prev = lax.ppermute(rims[:, 256 - RIM :], "seq", up)
    from_next = lax.ppermute(rims[:, :RIM], "seq", down)

    pair_part = lax.dynamic_slice_in_dim(token_pair, samp * 128, 128, axis=2)
    normed_pair, token_bias = pair_bias(pair_part.transpose(1, 0, 2), token_w_pair)
    atom_in, token_bias = ordered(atom_in, token_bias)
    token_bias = jnp.broadcast_to(token_bias[None], (8, 16, 64, 128)).reshape(128, 64, 128)
    token_bias = both_axes(token_bias).reshape(8, NT, 128)

    key_index = 256 * seq - RIM + 32 * jnp.arange(8)[:, None] + jnp.arange(128)[None, :]
    mask = jnp.where((key_index >= 0) & (key_index < 4096), 0.0, masked).astype(F32)
    (
        first, query, keyval, probs, gate, attended, middle, cond_low, cond_proj, pooled,
        start, tfirst, tgate, tcond_proj, single_low, runs,
    ) = front(
        atom_in, from_prev, from_next, atom_cond, atom_pair, mask, atom_w_pair.astype(F32), atom_w_cond,
        atom_w_qkvg, atom_w_out, atom_w_up, atom_w_down, pool_weight, tok_in, single_cond, token_w_cond, token_w_qkvg,
    )
    lines = lax.all_gather(tfirst, "seq", axis=0)
    runs, token_bias = ordered(runs, token_bias)
    qkv, tprobs, tattended = token_attention(along_seq(runs), token_bias)
    (
        token_out, cots, tdgate, tdmid, gated, gbranch, second, dup, hidden, gdown, tdu,
    ) = turn(
        along_seq(tattended), tgate, start, tcond_proj, cotangent, token_w_out, token_w_up, token_w_down
    )
    cots = along_seq(cots)
    wide = token_weights(gated, gbranch, tfirst, tdgate, second, dup, hidden, gdown, single_low, tdu)
    cots, wide = ordered(cots, wide)
    wide = lax.psum_scatter(wide, "seq", scatter_dimension=0, tiled=True)
    tgrads, slopes = token_attention_back(qkv, tprobs, cots)
    narrow = head_weights(tgrads, lines)
    narrow = narrow.reshape(16, 8, 6, 8, 18).transpose(3, 0, 1, 2, 4).reshape(8, DA, 108)
    narrow = jnp.pad(narrow, ((0, 0), (0, 0), (0, 20)))
    tgrads, narrow, slopes = ordered(along_seq(tgrads), narrow, slopes)
    slopes = both_axes(slopes.reshape(128, 64, 128))
    grad_tok, gpooled, dpool, tdu = back(
        tgrads, tdgate, tdmid, start, tcond_proj, token_w_qkvg, pool_weight, pooled
    )
    (
        dquery, dgate, dkeyval, to_prev, to_next, dmid, du, dw_out, dw_up, dw_down, dpair,
    ) = atom_back(
        gpooled.reshape(4, 64, DA), cond_proj, middle, gate, attended, query, keyval, probs, atom_pair,
        atom_w_out, atom_w_up, atom_w_down,
    )
    back_next = lax.ppermute(to_prev, "seq", down)
    back_prev = lax.ppermute(to_next, "seq", up)
    tok_pair_grad = pair_grad(slopes.reshape(8, 16, 64, 128), normed_pair)
    atom_pair_grad = jnp.sum(dpair, axis=1).reshape(4, 16).T
    misc = jnp.zeros((16, 8, DA), F32).at[:, 0, :].set(tok_pair_grad).at[:, 1, :4].set(atom_pair_grad)
    grad_atoms, packed = atom_end(
        dquery, dgate, dkeyval, back_prev, back_next, dmid, atom_in, first, cond_proj, du, cond_low,
        atom_w_qkvg, dw_out, dw_up, dw_down, dpool, misc.reshape(DA, DA), single_low, tdu, narrow,
    )
    packed = both_axes(packed.reshape(128, 8, 1152))
    wide = jnp.pad(wide, ((0, 0), (0, 512))).reshape(48, 8, 1024).transpose(1, 0, 2)
    wide = lax.all_to_all(wide, "samp", 0, 0, tiled=True)
    narrow = summed(packed[:, :, 1024:].reshape(8, DA, DA)).reshape(16, 1024)
    mine = jnp.concatenate([summed(wide), summed(packed[:, :, :1024]), narrow], axis=0)
    parts = handed_on(mine).astype(F32)
    wide = parts[:, :48].transpose(1, 0, 2).reshape(48, 64 * DA)
    atoms = parts[:, 48:56].transpose(1, 0, 2).reshape(8, 64 * DA)
    narrow = parts[:, 56:].reshape(8, 16, 8, 128)[..., :108].reshape(8, 16, 48, 18)
    narrow = narrow.transpose(2, 1, 0, 3).reshape(48, 16, 3, 48).transpose(0, 2, 1, 3).reshape(48, 3 * DT)
    conds = jnp.concatenate(
        [atoms[:, 3072 + 1536 * i : 4608 + 1536 * i] for i in range(3)], axis=0
    )
    conds = jnp.concatenate([conds, wide[:24, 8 * DT : 10 * DT], wide[24:, 8 * DT : 10 * DT]], axis=1)

    return (
        token_out,
        grad_atoms,
        grad_tok,
        atoms[:, :768],
        atoms[:, 768:1280],
        atoms[:, 1280:1408],
        atoms[:, 1408:1920],
        jnp.concatenate([atoms[:, 2688:2816], atoms[:, 2816:2944]], axis=0),
        atoms[1:2, 2944:2948],
        atoms[:, 1920:2688],
        conds,
        jnp.concatenate([narrow, wide[:, 5 * DT : 6 * DT]], axis=1),
        wide[:, 4 * DT : 5 * DT],
        wide[:, : 4 * DT],
        jnp.concatenate([wide[:, 6 * DT : 7 * DT], wide[:, 7 * DT : 8 * DT]], axis=0),
        atoms[0:1, 2944:3072],
    )


def solution(mesh):
    rows, both, whole = P("seq", None), P("samp", "seq", None), P()
    in_specs = (both, both, rows, rows, P(None, "seq", None), P(None, "seq", None)) + (whole,) * 13 + (both,)
    out_specs = (both,) * 3 + (rows,) * 13
    mapped = jax.shard_map(body, mesh=mesh, in_specs=in_specs, out_specs=out_specs, check_vma=False)

    def run(*args):
        with jax.sharding.use_abstract_mesh(mesh.abstract_mesh):
            return mapped(*args)

    return run
```

```python
import jax
import jax.numpy as jnp
from jax import lax
from jax.experimental import pallas as pl
from jax.experimental.pallas import tpu as pltpu
from jax.sharding import PartitionSpec as P

eps = 1e-05
masked = -1000000000.0

MIB = 1 << 20
F32, BF16 = jnp.float32, jnp.bfloat16


def kernel_call(kernel, out_shape, grid=(1,), in_specs=None, out_specs=None, scratch=(), scalars=0, us=1, name=None):
    def run(*args):
        return pl.pallas_call(
            kernel,
            out_shape=list(out_shape),
            grid_spec=pltpu.PrefetchScalarGridSpec(
                num_scalar_prefetch=scalars,
                grid=grid,
                in_specs=in_specs or [fixed(*a.shape) for a in args[scalars:]],
                out_specs=out_specs or [fixed(*o.shape) for o in out_shape],
                scratch_shapes=list(scratch),
            ),
            compiler_params=pltpu.CompilerParams(vmem_limit_bytes=60 * MIB),
            cost_estimate=pl.CostEstimate(flops=us << 30, bytes_accessed=us << 20, transcendentals=0),
            name=name,
        )(*args)

    return run


def fixed(*shape):
    return pl.BlockSpec(shape, lambda *_: (0,) * len(shape), pipeline_mode=pl.Buffered(1))


def dot(left, right, over=((1,), (0,))):
    return lax.dot_general(left, right, (over, ((), ())), preferred_element_type=F32)


def swap_halves(first, second):
    low = lax.broadcasted_iota(jnp.int32, first.shape, 1) < 64
    half = first.shape[1] // 2
    return (
        jnp.where(low, first, pltpu.roll(second, half, 1)),
        jnp.where(low, pltpu.roll(first, half, 1), second),
    )


def runs_to_tokens(runs_ref, tokens_ref):
    for pair in range(runs_ref.shape[0] // 2):
        for duo in range(2):
            lanes = slice(128 * duo, 128 * duo + 128)
            made = swap_halves(
                runs_ref[2 * pair, :, lanes].astype(F32), runs_ref[2 * pair + 1, :, lanes].astype(F32)
            )
            for k in range(2):
                tokens_ref[2 * duo + k, :, 128 * pair : 128 * pair + 128] = made[k].astype(
                    tokens_ref.dtype
                )


def tokens_to_runs(tokens_ref, runs_ref):
    for pair in range(runs_ref.shape[0] // 2):
        lanes = slice(128 * pair, 128 * pair + 128)
        for duo in range(2):
            made = swap_halves(tokens_ref[2 * duo, :, lanes], tokens_ref[2 * duo + 1, :, lanes])
            for k in range(2):
                runs_ref[2 * pair + k, :, 128 * duo : 128 * duo + 128] = made[k].astype(runs_ref.dtype)


HS = 48
NT = 1024
QB = 256
SAMP_RING = [0, 2, 4, 6, 7, 5, 3, 1]


def attention_kernel(runs_ref, bias_ref, qkv_ref, probs_ref, out_ref, heads_ref):
    sample = pl.program_id(0)

    @pl.when(sample == 0)
    def _():
        runs_to_tokens(runs_ref, qkv_ref)

    keys = qkv_ref[sample, HS : 2 * HS, :]
    values = qkv_ref[sample, 2 * HS :, :]

    def scores_of(block):
        rows = slice(block * QB, block * QB + QB)
        made = dot(qkv_ref[sample, :HS, rows], keys, ((0,), (0,))) * HS ** (-0.5)
        return made + jnp.concatenate([bias_ref[SAMP_RING.index(i), rows, :] for i in range(8)], axis=1).astype(F32)

    count = NT // QB
    ahead = scores_of(0)
    for block in range(count):
        rows = slice(block * QB, block * QB + QB)
        scores = ahead
        if block + 1 < count:
            ahead = scores_of(block + 1)
        exponent = jnp.exp(scores - jnp.max(scores, axis=1, keepdims=True))
        probs = (exponent * (1.0 / jnp.sum(exponent, axis=1, keepdims=True))).astype(BF16)
        probs_ref[0, rows, :] = probs
        heads_ref[sample, :, rows] = dot(probs, values, ((1,), (1,))).T

    @pl.when(sample == 3)
    def _():
        tokens_to_runs(heads_ref, out_ref)


def token_attention(runs, bias):
    return kernel_call(
        attention_kernel,
        [
            jax.ShapeDtypeStruct((4, 3 * HS, NT), BF16),
            jax.ShapeDtypeStruct((4, NT, NT), BF16),
            jax.ShapeDtypeStruct((16, HS, 256), BF16),
        ],
        grid=(4,),
        in_specs=[fixed(16, 3 * HS, 256)] + [fixed(8, NT, 128)],
        out_specs=[
            fixed(4, 3 * HS, NT), pl.BlockSpec((1, NT, NT), lambda s: (s, 0, 0)), fixed(16, HS, 256),
        ],
        scratch=[pltpu.VMEM((4, HS, NT), F32)],
        us=13,
        name="token_attention",
    )(runs, bias)


def attention_back_kernel(samp_ref, qkv_ref, probs_ref, cot_ref, out_ref, *refs):
    pair_refs, (cots_ref, grads_ref, total_ref) = refs[:4], refs[4:]
    sample = pl.program_id(0)

    @pl.when(sample == 0)
    def _():
        runs_to_tokens(cot_ref, cots_ref)
        total_ref[...] = jnp.zeros_like(total_ref)

    keys = qkv_ref[sample, HS : 2 * HS, :]
    values = qkv_ref[sample, 2 * HS :, :]

    def weights_of(block):
        return dot(cots_ref[sample, :, block * QB : block * QB + QB], values, ((0,), (0,)))

    key_grad, value_grad = 0.0, 0.0
    count = NT // QB
    ahead = weights_of(0)
    for block in range(count):
        rows = slice(block * QB, block * QB + QB)
        now = ahead
        if block + 1 < count:
            ahead = weights_of(block + 1)
        low = probs_ref[0, rows, :]
        probs = low.astype(F32)
        weighed = probs * now
        slopes = weighed - probs * jnp.sum(weighed, axis=1, keepdims=True)
        slopes_low = slopes.astype(BF16)
        total_ref[rows, :] += slopes
        grads_ref[sample, :HS, rows] = dot(keys, slopes_low, ((1,), (1,))) * HS ** (-0.5)
        key_grad += dot(qkv_ref[sample, :HS, rows], slopes_low)
        value_grad += dot(cots_ref[sample, :, rows], low)
    grads_ref[sample, HS : 2 * HS, :] = key_grad * HS ** (-0.5)
    grads_ref[sample, 2 * HS :, :] = value_grad

    @pl.when(sample == 3)
    def _():
        tokens_to_runs(grads_ref, out_ref)
        for k in range(8):
            lanes = pl.ds(pl.multiple_of((samp_ref[0] ^ k) * 128, 128), 128)
            pair_refs[k // 2][k % 2] = total_ref[:, lanes].astype(BF16)


def token_attention_back(samp, qkv, probs, cots):
    return kernel_call(
        attention_back_kernel,
        [jax.ShapeDtypeStruct((16, 3 * HS, 256), BF16)] + [jax.ShapeDtypeStruct((2, NT, 128), BF16)] * 4,
        grid=(4,),
        in_specs=[fixed(4, 3 * HS, NT), pl.BlockSpec((1, NT, NT), lambda s, _: (s, 0, 0)), fixed(16, HS, 256)],
        out_specs=[fixed(16, 3 * HS, 256)] + [fixed(2, NT, 128)] * 4,
        scratch=[
            pltpu.VMEM((4, HS, NT), BF16),
            pltpu.VMEM((4, 3 * HS, NT), F32),
            pltpu.VMEM((NT, NT), F32),
        ],
        scalars=1,
        us=14,
        name="token_attention_back",
    )(samp, qkv, probs, cots)


def pair_kernel(samp_ref, pair_ref, weight_ref, normed_ref, bias_ref):
    pair = pair_ref[...].astype(F32)
    centred = pair - jnp.mean(pair, axis=0, keepdims=True)
    inverse = lax.rsqrt(jnp.mean(centred * centred, axis=0, keepdims=True) + eps)
    low = jnp.swapaxes((centred * inverse).astype(BF16), 0, 1)
    normed_ref[...] = low
    weight = weight_ref[...]
    bias = jnp.stack([dot(weight, low[i]) for i in range(low.shape[0])], axis=0)
    bias = jnp.swapaxes(bias, 0, 1).astype(BF16)
    bias_ref[...] = bias


def pair_bias(samp, pair, weight):
    return kernel_call(
        pair_kernel,
        [jax.ShapeDtypeStruct((64, 128, 128), BF16), jax.ShapeDtypeStruct((16, 64, 128), BF16)],
        grid=(2,),
        in_specs=[pl.BlockSpec((128, 32, 128), lambda i, samp: (0, i, samp[0])), fixed(16, 128)],
        out_specs=[
            pl.BlockSpec((32, 128, 128), lambda i, _: (i, 0, 0)),
            pl.BlockSpec((16, 32, 128), lambda i, _: (0, i, 0)),
        ],
        scalars=1,
        us=5,
        name="pair_bias",
    )(samp, pair, weight)


def pair_back_kernel(slopes_ref, normed_ref, atoms_ref, out_ref, grad_ref):
    step = pl.program_id(0)
    slopes = jnp.swapaxes(slopes_ref[...], 0, 1)
    made = dot(slopes[0], normed_ref[0], ((1,), (1,)))
    for i in range(1, slopes.shape[0]):
        made += dot(slopes[i], normed_ref[i], ((1,), (1,)))

    @pl.when(step == 0)
    def _():
        grad_ref[...] = made

    @pl.when(step > 0)
    def _():
        grad_ref[...] += made

    @pl.when(step == 3)
    def _():
        atoms = jnp.sum(atoms_ref[...], axis=1, keepdims=True)
        lane = lax.broadcasted_iota(jnp.int32, (16, 128), 1)
        rows = jnp.where(lane == 0, atoms[:16], 0.0)
        for h in range(1, 4):
            rows += jnp.where(lane == h, atoms[16 * h : 16 * h + 16], 0.0)
        line = lax.broadcasted_iota(jnp.int32, (16, 8, 128), 1)
        both = jnp.where(line == 0, grad_ref[...][:, None, :], 0.0) + jnp.where(line == 1, rows[:, None, :], 0.0)
        out_ref[...] = both.reshape(128, 128).astype(BF16)


def pair_grad(slopes, normed, atoms):
    return kernel_call(
        pair_back_kernel,
        [jax.ShapeDtypeStruct((128, 128), BF16)],
        grid=(4,),
        in_specs=[
            pl.BlockSpec((16, 16, 128), lambda i: (0, i, 0)),
            pl.BlockSpec((16, 128, 128), lambda i: (i, 0, 0)),
            fixed(64, 128),
        ],
        out_specs=[fixed(128, 128)],
        scratch=[pltpu.VMEM((16, 128), F32)],
        us=4,
        name="pair_grad",
    )(slopes, normed, atoms)[0]


DA, DT, FT, FA = 128, 768, 1536, 256
RIM = 48
RING = [0, 1, 4, 5, 8, 9, 12, 13, 14, 15, 10, 11, 6, 7, 2, 3]
SPAN = 256 + 2 * RIM


def normed(x):
    centred = x - jnp.mean(x, axis=-1, keepdims=True)
    inverse = lax.rsqrt(jnp.mean(centred * centred, axis=-1, keepdims=True) + eps)
    return centred * inverse, inverse


def sigmoid(x):
    return 1.0 / (1.0 + jnp.exp(-x))


def own_head():
    shape = (1, 4, 32, 128)
    return lax.broadcasted_iota(jnp.int32, shape, 3) // 32 == lax.broadcasted_iota(jnp.int32, shape, 1)


def head_rows(rows):
    return jnp.where(own_head(), rows.reshape(8, 1, 32, 128), 0.0).reshape(1024, 128).astype(BF16)


def rows_of_heads(full):
    return jnp.sum(jnp.where(own_head(), full.reshape(8, 4, 32, 128), 0.0), axis=1).reshape(256, 128)


def by_window(made):
    return jnp.concatenate([made(w) for w in range(8)], axis=0)


def pair_norm(pair):
    centred = pair - jnp.mean(pair, axis=0, keepdims=True)
    inverse = lax.rsqrt(jnp.mean(centred * centred, axis=0, keepdims=True) + eps)
    return (centred * inverse).astype(BF16).astype(F32)


def part(ref, i, width, rows=slice(None)):
    return ref[rows, i * width : (i + 1) * width]


def front_kernel(
    x_ref, prev_ref, next_ref, cond_ref, pair_ref, mask_ref, w_pair_ref, w_cond_ref, w_qkvg_ref, w_out_ref,
    w_up_ref, w_down_ref, pool_ref, tok_ref, single_ref, tw_cond_hbm, tw_qkvg_hbm,
    first_ref, q_ref, kv_ref, probs_ref, gate_ref, att_ref, mid_ref, cond_low_ref, u_ref, pooled_ref,
    start_ref, tfirst_ref, tgate_ref, tu_ref, single_low_ref, runs_ref,
    bias_ref, y_ref, uh_ref, tw_cond_ref, tw_qkvg_ref, sems,
):
    loads = [
        pltpu.make_async_copy(tw_cond_hbm, tw_cond_ref, sems.at[0]),
        pltpu.make_async_copy(tw_qkvg_hbm, tw_qkvg_ref, sems.at[1]),
    ]
    for load in loads:
        load.start()
    cond = jnp.concatenate([prev_ref[4], cond_ref[...], next_ref[4]], axis=0).astype(F32)
    cond_low = normed(cond)[0].astype(BF16)
    cond_low_ref[...] = cond_low[RIM : RIM + 256]
    u_ref[...] = dot(cond_low[RIM : RIM + 256], w_cond_ref[...])
    uh_ref[...] = dot(cond_low, w_cond_ref[:, : 2 * DA])
    pairs = pair_norm(pair_ref[...].astype(F32))
    for h in range(4):
        bias = pairs[0] * w_pair_ref[0, h]
        for c in range(1, 16):
            bias += pairs[c] * w_pair_ref[c, h]
        for w in range(8):
            at = 128 * w + 32 * h
            bias_ref[at : at + 32, :] = bias[32 * w : 32 * w + 32] + mask_ref[w : w + 1, :]

    scale_a, shift_a = sigmoid(part(uh_ref, 0, DA)), part(uh_ref, 1, DA)
    gate_a, scale_b, shift_b, gate_b = (
        sigmoid(part(u_ref, 2, DA)), sigmoid(part(u_ref, 3, DA)), part(u_ref, 4, DA), sigmoid(part(u_ref, 5, DA)),
    )

    def atoms(s):
        x = jnp.concatenate([prev_ref[s], x_ref[s], next_ref[s]], axis=0).astype(F32)
        first = (scale_a * normed(x)[0] + shift_a).astype(BF16)
        projected = dot(first, w_qkvg_ref[...])
        own = projected[RIM : RIM + 256]
        first_ref[s] = first[RIM : RIM + 256]
        query = own[:, :DA].astype(BF16)
        q_ref[s] = query
        keys = projected[:, DA : 2 * DA].astype(BF16)
        values = projected[:, 2 * DA : 3 * DA].astype(BF16)
        kv_ref[s, :, :DA] = keys
        kv_ref[s, :, DA:] = values
        gate = sigmoid(own[:, 3 * DA :])
        gate_ref[s] = gate
        rows = head_rows(query.astype(F32))
        scores = by_window(lambda w: dot(rows[128 * w : 128 * w + 128], keys[32 * w : 32 * w + 128], ((1,), (1,))))
        scores = scores * 32 ** (-0.5) + bias_ref[...]
        exponent = jnp.exp(scores - jnp.max(scores, axis=1, keepdims=True))
        probs = (exponent * (1.0 / jnp.sum(exponent, axis=1, keepdims=True))).astype(BF16)
        probs_ref[s] = probs
        attended = rows_of_heads(
            by_window(lambda w: dot(probs[128 * w : 128 * w + 128], values[32 * w : 32 * w + 128]))
        )
        att_ref[s] = attended
        branch = dot((gate * attended).astype(BF16), w_out_ref[...])
        middle = x[RIM : RIM + 256] + gate_a * branch
        mid_ref[s] = middle
        second = (scale_b * normed(middle)[0] + shift_b).astype(BF16)
        up = dot(second, w_up_ref[...])
        hidden = (up[:, :FA] * sigmoid(up[:, :FA]) * up[:, FA:]).astype(BF16)
        y_ref[s] = middle + gate_b * dot(hidden, w_down_ref[...])
        pooled = y_ref[s, pl.ds(0, 64, stride=4), :]
        for k in range(1, 4):
            pooled += y_ref[s, pl.ds(k, 64, stride=4), :]
        pooled_ref[s] = (pooled * 0.25).astype(BF16)

    for s in range(4):
        atoms(s)

    for load in loads:
        load.wait()
    single_low = normed(single_ref[...].astype(F32))[0].astype(BF16)
    single_low_ref[...] = single_low
    for i in range(6):
        tu_ref[:, DT * i : DT * i + DT] = dot(single_low, tw_cond_ref[:, DT * i : DT * i + DT])
    pooled = pooled_ref[...].reshape(256, DA)
    start = tok_ref[...].reshape(256, DT).astype(F32) + dot(pooled, pool_ref[...])
    start_ref[...] = start
    lines = normed(start)[0]
    scale, shift = sigmoid(part(tu_ref, 0, DT)), part(tu_ref, 1, DT)
    for s in range(4):
        tfirst_ref[64 * s : 64 * s + 64, :] = (scale * lines[64 * s : 64 * s + 64] + shift).astype(BF16)
    first = tfirst_ref[...]
    for i in range(3):
        turned = dot(first, part(tw_qkvg_ref, i, DT)).T.astype(BF16)
        for h in range(16):
            runs_ref[h, HS * i : HS * i + HS, :] = turned[HS * h : HS * h + HS]
    tgate_ref[...] = sigmoid(dot(first, part(tw_qkvg_ref, 3, DT)))


def front(*args):
    sds = jax.ShapeDtypeStruct
    specs = [fixed(*a.shape) for a in args]
    specs[6] = pl.BlockSpec(memory_space=pltpu.SMEM)
    specs[15] = specs[16] = pl.BlockSpec(memory_space=pl.ANY)
    return kernel_call(
        front_kernel,
        [
            sds((4, 256, DA), BF16), sds((4, 256, DA), BF16), sds((4, SPAN, 2 * DA), BF16),
            sds((4, 1024, 128), BF16), sds((4, 256, DA), F32), sds((4, 256, DA), F32),
            sds((4, 256, DA), F32), sds((256, DA), BF16), sds((256, 6 * DA), F32), sds((4, 64, DA), BF16),
            sds((256, DT), F32), sds((256, DT), BF16), sds((256, DT), F32), sds((64, 6 * DT), F32),
            sds((64, 384), BF16), sds((16, 3 * HS, 256), BF16),
        ],
        in_specs=specs,
        scratch=[
            pltpu.VMEM((1024, 128), F32), pltpu.VMEM((4, 256, DA), F32), pltpu.VMEM((SPAN, 2 * DA), F32),
            pltpu.VMEM((384, 6 * DT), BF16), pltpu.VMEM((DT, 4 * DT), BF16), pltpu.SemaphoreType.DMA((2,)),
        ],
        us=24,
        name="front",
    )(*args)


def slope(squashed):
    return squashed * (1.0 - squashed)


def norm_back_rows(gradient, lines, inverse):
    return inverse * (
        gradient
        - jnp.mean(gradient, axis=-1, keepdims=True)
        - lines * jnp.mean(gradient * lines, axis=-1, keepdims=True)
    )


def turn_kernel(
    runs_ref, tgate_ref, start_ref, tu_ref, cot_ref, w_out_hbm, w_up_hbm, w_down_hbm,
    out_ref, cots_ref, dgate_ref, dmid_ref, a_ref, gbranch_ref, second_ref, dup_ref, hidden_ref, gdown_ref,
    du_ref,
    up_ref, mid_ref, branch_ref, down_ref, w_out_ref, w_up_ref, w_down_ref, sems,
):
    loads = [
        pltpu.make_async_copy(w_out_hbm, w_out_ref, sems.at[0]),
        pltpu.make_async_copy(w_up_hbm, w_up_ref, sems.at[1]),
        pltpu.make_async_copy(w_down_hbm, w_down_ref, sems.at[2]),
    ]
    for load in loads:
        load.start()
    attended = runs_ref[...].reshape(DT, 256).astype(F32).T
    gate = tgate_ref[...]
    gated = (gate * attended).astype(BF16)
    a_ref[...] = gated
    loads[0].wait()
    branch_ref[...] = dot(gated, w_out_ref[...])
    gate_a, scale_b, shift_b, gate_b = (
        sigmoid(part(tu_ref, 2, DT)), sigmoid(part(tu_ref, 3, DT)), part(tu_ref, 4, DT), sigmoid(part(tu_ref, 5, DT)),
    )
    runs = [slice(64 * s, 64 * s + 64) for s in range(4)]
    for r in runs:
        middle = start_ref[r, :] + gate_a * branch_ref[r, :]
        mid_ref[r, :] = middle
        second_ref[r, :] = (scale_b * normed(middle)[0] + shift_b).astype(BF16)
    second = second_ref[...]
    loads[1].wait()
    loads[2].wait()
    cut = 512
    for j in range(FT // cut):
        e = dot(second, w_up_ref[:, cut * j : cut * j + cut])
        f = dot(second, w_up_ref[:, FT + cut * j : FT + cut * j + cut])
        up_ref[:, cut * j : cut * j + cut] = e
        up_ref[:, FT + cut * j : FT + cut * j + cut] = f
        hidden = (e * sigmoid(e) * f).astype(BF16)
        hidden_ref[:, cut * j : cut * j + cut] = hidden
        piece = dot(hidden, w_down_ref[cut * j : cut * j + cut, :])
        if j == 0:
            down_ref[...] = piece
        else:
            down_ref[...] += piece
    total = jnp.zeros((64, DT), F32)
    for s, r in enumerate(runs):
        cot = cot_ref[s].astype(F32)
        out_ref[s] = (mid_ref[r, :] + gate_b * down_ref[r, :]).astype(BF16)
        gdown_ref[r, :] = (cot * gate_b).astype(BF16)
        total += cot * down_ref[r, :]
    du_ref[:, 3 * DT :] = (total * slope(gate_b)).astype(BF16)
    gdown = gdown_ref[...]
    dsecond = jnp.zeros((256, DT), F32)
    for j in range(FT // cut):
        dhidden = dot(gdown, w_down_ref[cut * j : cut * j + cut, :], ((1,), (1,)))
        e = up_ref[:, cut * j : cut * j + cut]
        f = up_ref[:, FT + cut * j : FT + cut * j + cut]
        half = sigmoid(e)
        de = (dhidden * f * half * (1.0 + e * (1.0 - half))).astype(BF16)
        df = (dhidden * e * half).astype(BF16)
        dup_ref[:, cut * j : cut * j + cut] = de
        dup_ref[:, FT + cut * j : FT + cut * j + cut] = df
        piece = dot(de, w_up_ref[:, cut * j : cut * j + cut], ((1,), (1,)))
        piece += dot(df, w_up_ref[:, FT + cut * j : FT + cut * j + cut], ((1,), (1,)))
        dsecond += piece
    down_ref[...] = dsecond
    total_a = jnp.zeros((64, DT), F32)
    total_b = jnp.zeros((64, DT), F32)
    total_c = jnp.zeros((64, DT), F32)
    for s, r in enumerate(runs):
        d = down_ref[r, :]
        lines, inverse = normed(mid_ref[r, :])
        dmid = cot_ref[s].astype(F32) + norm_back_rows(d * scale_b, lines, inverse)
        dmid_ref[r, :] = dmid
        gbranch_ref[r, :] = (dmid * gate_a).astype(BF16)
        total_a += dmid * branch_ref[r, :]
        total_b += d * lines
        total_c += d
    du_ref[:, :DT] = (total_a * slope(gate_a)).astype(BF16)
    du_ref[:, DT : 2 * DT] = (total_b * slope(scale_b)).astype(BF16)
    du_ref[:, 2 * DT : 3 * DT] = total_c.astype(BF16)
    dgated = dot(gbranch_ref[...], w_out_ref[...], ((1,), (1,)))
    dgate_ref[...] = (dgated * attended * slope(gate)).astype(BF16)
    cots_ref[...] = (dgated * gate).T.astype(BF16).reshape(16, HS, 256)


def turn(*args):
    sds = jax.ShapeDtypeStruct
    rows = lambda n, t=BF16: sds((256, n), t)
    return kernel_call(
        turn_kernel,
        [
            sds((4, 64, DT), BF16), sds((16, HS, 256), BF16), rows(DT), rows(DT, F32), rows(DT), rows(DT),
            rows(DT), rows(2 * FT), rows(FT), rows(DT), sds((64, 4 * DT), BF16),
        ],
        in_specs=[fixed(*a.shape) for a in args[:5]] + [pl.BlockSpec(memory_space=pl.ANY)] * 3,
        scratch=[pltpu.VMEM((256, 2 * FT), F32)]
        + [pltpu.VMEM((256, DT), F32)] * 3
        + [pltpu.VMEM(a.shape, BF16) for a in args[5:]]
        + [pltpu.SemaphoreType.DMA((3,))],
        us=12,
        name="turn",
    )(*args)


def weights_kernel(
    a_ref, gbranch_ref, first_ref, dgate_ref, second_ref, dup_ref, hidden_ref, gdown_ref, single_ref, du_ref, du_next_ref,
    out_ref, kept_ref,
):
    step = pl.program_id(0)

    def write(rows, lanes=slice(None)):
        for at, run in enumerate(RING):
            out_ref[48 * at : 48 * at + 48, lanes] = rows[run]

    def square(left, right):
        write(dot(left[...], right[...], ((0,), (0,))).astype(BF16).reshape(16, 48, DT))

    @pl.when(step < 4)
    def _():
        square(second_ref, dup_ref)

    @pl.when(step == 4)
    def _():
        square(a_ref, gbranch_ref)

    @pl.when(step == 5)
    def _():
        square(first_ref, dgate_ref)

    @pl.when(step == 6)
    def _():
        for half in range(2):
            lanes = slice(384 * half, 384 * half + 384)
            made = dot(hidden_ref[...], gdown_ref[:, lanes], ((0,), (0,))).astype(BF16).reshape(16, 2, 48, 384)
            write(made[:, 0], lanes)
            kept_ref[:, :, lanes] = made[:, 1]

    @pl.when(step == 7)
    def _():
        write(kept_ref)

    @pl.when(step >= 8)
    def _():
        upper = dot(single_ref[...], du_ref[...], ((0,), (0,))).reshape(16, 24, DT)
        lower = dot(single_ref[...], du_next_ref[...], ((0,), (0,))).reshape(16, 24, DT)
        write(jnp.concatenate([upper, lower], axis=1).astype(BF16))


def token_weights(a, gbranch, first, dgate, second, dup, hidden, gdown, single_low, du):
    def late(first):
        return pl.BlockSpec((64, DT), lambda i: (0, first + jnp.maximum(i - 8, 0)))

    return kernel_call(
        weights_kernel,
        [jax.ShapeDtypeStruct((DT, 10 * DT), BF16)],
        grid=(10,),
        in_specs=[fixed(256, DT)] * 5
        + [
            pl.BlockSpec((256, DT), lambda i: (0, jnp.minimum(i, 3))),
            fixed(256, FT),
            fixed(256, DT),
            fixed(64, 384),
            late(0),
            late(2),
        ],
        out_specs=[pl.BlockSpec((DT, DT), lambda i: (0, i))],
        scratch=[pltpu.VMEM((16, 48, DT), BF16)],
        us=12,
        name="token_weights",
    )(a, gbranch, first, dgate, second, dup, hidden, gdown, single_low, du, du)[0]


def head_weights_kernel(grads_ref, lines_ref, out_ref, total_ref):
    step = pl.program_id(0)

    @pl.when(step == 0)
    def _():
        total_ref[...] = jnp.zeros_like(total_ref)

    for k in range(2):
        total_ref[...] += dot(grads_ref[k], lines_ref[k])

    @pl.when(step == 7)
    def _():
        made = total_ref[...].T.reshape(16, 6, 8, 3 * HS)
        out_ref[...] = jnp.zeros_like(out_ref)
        for s in range(6):
            out_ref[s, :, : 3 * HS] = made[:, s].reshape(DA, 3 * HS).astype(BF16)


def head_weights(grads, lines):
    return kernel_call(
        head_weights_kernel,
        [jax.ShapeDtypeStruct((8, DA, 256), BF16)],
        grid=(8,),
        in_specs=[
            pl.BlockSpec((2, 3 * HS, 256), lambda i: (jnp.where(i < 4, 2 * i, 15 - 2 * i), 0, 0)),
            pl.BlockSpec((2, 256, DT), lambda i: (i, 0, 0)),
        ],
        out_specs=[fixed(8, DA, 256)],
        scratch=[pltpu.VMEM((3 * HS, DT), F32)],
        us=6,
        name="head_weights",
    )(grads, lines)[0]


def back_kernel(
    runs_ref, dgate_ref, dmid_ref, start_ref, tu_ref, w_qkvg_hbm, pool_ref, pooled_ref,
    out_ref, gpooled_ref, dpool_ref, ducat_ref,
    dfirst_ref, gpool_ref, w_qkvg_ref, sems,
):
    loads = [
        pltpu.make_async_copy(
            w_qkvg_hbm.at[:, DT * i : DT * i + DT], w_qkvg_ref.at[:, DT * i : DT * i + DT], sems.at[i]
        )
        for i in range(4)
    ]
    for i in (3, 0, 1, 2):
        loads[i].start()
    loads[3].wait()
    dfirst = dot(dgate_ref[...], part(w_qkvg_ref, 3, DT), ((1,), (1,)))
    for i in range(3):
        piece = runs_ref[:, HS * i : HS * i + HS, :].reshape(DT, 256)
        loads[i].wait()
        dfirst += dot(piece.astype(F32).T.astype(BF16), part(w_qkvg_ref, i, DT), ((1,), (1,)))
    dfirst_ref[...] = dfirst
    scale = sigmoid(part(tu_ref, 0, DT))
    total_a = jnp.zeros((64, DT), F32)
    total_b = jnp.zeros((64, DT), F32)
    for s in range(4):
        r = slice(64 * s, 64 * s + 64)
        d = dfirst_ref[r, :]
        lines, inverse = normed(start_ref[r, :])
        grad = dmid_ref[r, :] + norm_back_rows(d * scale, lines, inverse)
        out_ref[s] = grad
        gpool_ref[r, :] = grad.astype(BF16)
        total_a += d * lines
        total_b += d
    ducat_ref[:, :DT] = (total_a * slope(scale)).astype(BF16)
    ducat_ref[:, DT : 2 * DT] = total_b.astype(BF16)
    gpool = gpool_ref[...]
    gpooled_ref[...] = dot(gpool, pool_ref[...], ((1,), (1,))) * 0.25
    dpool_ref[...] = dot(pooled_ref[...].reshape(256, DA), gpool, ((0,), (0,)))


def back(*args):
    sds = jax.ShapeDtypeStruct
    return kernel_call(
        back_kernel,
        [sds((4, 64, DT), F32), sds((256, DA), F32), sds((DA, DT), F32), sds((64, 2 * DT), BF16)],
        in_specs=[
            pl.BlockSpec(memory_space=pl.ANY) if i == 5 else fixed(*a.shape) for i, a in enumerate(args)
        ],
        scratch=[
            pltpu.VMEM((256, DT), F32), pltpu.VMEM((256, DT), BF16), pltpu.VMEM((DT, 4 * DT), BF16),
            pltpu.SemaphoreType.DMA((4,)),
        ],
        us=7,
        name="back",
    )(*args)


def atom_prep_kernel(
    u_ref, mid_ref, gate_ref, att_ref, w_out_ref, w_up_ref, w_down_ref,
    second_ref, hidden_ref, rate_ref, down_ref, gated_ref, branch_ref,
):
    scale_b, shift_b = sigmoid(part(u_ref, 3, DA)), part(u_ref, 4, DA)
    for s in range(4):
        second = (scale_b * normed(mid_ref[s])[0] + shift_b).astype(BF16)
        second_ref[s] = second
        up = dot(second, w_up_ref[...])
        e, f = up[:, :FA], up[:, FA:]
        half = sigmoid(e)
        rate_ref[s, :, :FA] = f * half * (1.0 + e * (1.0 - half))
        rate_ref[s, :, FA:] = e * half
        hidden = (e * half * f).astype(BF16)
        hidden_ref[s] = hidden
        down_ref[s] = dot(hidden, w_down_ref[...])
        gated = (gate_ref[s] * att_ref[s]).astype(BF16)
        gated_ref[s] = gated
        branch_ref[s] = dot(gated, w_out_ref[...])


def atom_prep(*args):
    sds = jax.ShapeDtypeStruct
    return kernel_call(
        atom_prep_kernel,
        [
            sds((4, 256, DA), BF16), sds((4, 256, FA), BF16), sds((4, 256, 2 * FA), F32), sds((4, 256, DA), F32),
            sds((4, 256, DA), BF16), sds((4, 256, DA), F32),
        ],
        us=6,
        name="atom_prep",
    )(*args)


def atom_back_kernel(
    gpooled_ref, u_ref, mid_ref, gate_ref, att_ref, q_ref, kv_ref, probs_ref, pair_ref, w_out_ref, w_up_ref,
    w_down_ref, second_ref, hidden_ref, rate_ref, down_ref, gated_ref, branch_ref,
    dq_ref, dgate_ref, dkv_ref, prev_ref, next_ref, dmid_ref, du_ref, dw_out_ref, dw_up_ref, dw_down_ref, dpair_ref,
    dy_ref, grads_ref, slopes_ref, sums_ref, gbranch_ref, dup_ref, gdown_ref,
):
    gate_a, scale_b, gate_b = sigmoid(part(u_ref, 2, DA)), sigmoid(part(u_ref, 3, DA)), sigmoid(part(u_ref, 5, DA))

    def atoms(s):
        for k in range(4):
            dy_ref[s, pl.ds(k, 64, stride=4), :] = gpooled_ref[s]
        dy = dy_ref[s]
        gdown = (dy * gate_b).astype(BF16)
        gdown_ref[s] = gdown
        dhidden = dot(gdown, w_down_ref[...], ((1,), (1,)))
        dup = (jnp.concatenate([dhidden, dhidden], axis=1) * rate_ref[s]).astype(BF16)
        dup_ref[s] = dup
        dsecond = dot(dup, w_up_ref[...], ((1,), (1,)))
        lines, inverse = normed(mid_ref[s])
        dmid = dy + norm_back_rows(dsecond * scale_b, lines, inverse)
        dmid_ref[s] = dmid
        gate, attended = gate_ref[s], att_ref[s]
        gbranch = (dmid * gate_a).astype(BF16)
        gbranch_ref[s] = gbranch
        sums = [dmid * branch_ref[s], dsecond * lines, dsecond, dy * down_ref[s]]
        for i in range(4):
            lanes = slice(DA * i, DA * i + DA)
            sums_ref[:, lanes] = sums[i] if s == 0 else sums_ref[:, lanes] + sums[i]
        dgated = dot(gbranch, w_out_ref[...], ((1,), (1,)))
        dgate_ref[s] = (dgated * attended * slope(gate)).astype(BF16)
        cots = head_rows(dgated * gate)
        rows = head_rows(q_ref[s].astype(F32))
        low = probs_ref[s]
        probs = low.astype(F32)

        def window(w):
            return slice(128 * w, 128 * w + 128), slice(32 * w, 32 * w + 128)

        def weights_of(w):
            at, span = window(w)
            return dot(cots[at], kv_ref[s, span, DA:], ((1,), (1,)))

        weighed = probs * by_window(weights_of)
        slopes = weighed - probs * jnp.sum(weighed, axis=1, keepdims=True)
        slopes_ref[...] = slopes if s == 0 else slopes_ref[...] + slopes
        slopes_low = slopes.astype(BF16)

        def query_of(w):
            at, span = window(w)
            return dot(slopes_low[at], kv_ref[s, span, :DA])

        dq_ref[s] = (rows_of_heads(by_window(query_of)) * 32 ** (-0.5)).astype(BF16)
        grads_ref[s] = jnp.zeros((SPAN, 2 * DA), F32)
        for w in range(8):
            at, span = window(w)
            grads_ref[s, span, :DA] += dot(slopes_low[at], rows[at], ((0,), (0,))) * 32 ** (-0.5)
            grads_ref[s, span, DA:] += dot(low[at], cots[at], ((0,), (0,)))
        dkv_ref[s] = grads_ref[s, RIM : RIM + 256, :]
        prev_ref[s] = grads_ref[s, :RIM, :].astype(BF16)
        next_ref[s] = grads_ref[s, RIM + 256 :, :].astype(BF16)

    for s in range(4):
        atoms(s)

    def rows_of(ref):
        return ref[...].reshape(1024, ref.shape[2])

    dw_out_ref[...] = dot(rows_of(gated_ref), rows_of(gbranch_ref), ((0,), (0,)))
    dw_up_ref[...] = dot(rows_of(second_ref), rows_of(dup_ref), ((0,), (0,)))
    dw_down_ref[...] = dot(rows_of(hidden_ref), rows_of(gdown_ref), ((0,), (0,)))
    du_ref[:, :DA] = sums_ref[:, :DA] * slope(gate_a)
    du_ref[:, DA : 2 * DA] = sums_ref[:, DA : 2 * DA] * slope(scale_b)
    du_ref[:, 2 * DA : 3 * DA] = sums_ref[:, 2 * DA : 3 * DA]
    du_ref[:, 3 * DA :] = sums_ref[:, 3 * DA :] * slope(gate_b)
    pairs = pair_norm(pair_ref[...].astype(F32))
    slopes = slopes_ref[...].reshape(8, 4, 32, 128)
    for h in range(4):
        own = slopes[:, h].reshape(256, 128)
        for c in range(16):
            dpair_ref[16 * h + c : 16 * h + c + 1, :] = jnp.sum(own * pairs[c], axis=0, keepdims=True)


def atom_back(*args):
    sds = jax.ShapeDtypeStruct
    return kernel_call(
        atom_back_kernel,
        [
            sds((4, 256, DA), BF16), sds((4, 256, DA), BF16), sds((4, 256, 2 * DA), F32),
            sds((4, RIM, 2 * DA), BF16), sds((4, RIM, 2 * DA), BF16), sds((4, 256, DA), F32),
            sds((256, 4 * DA), F32), sds((DA, DA), F32), sds((DA, 2 * FA), F32), sds((FA, DA), F32), sds((64, 128), F32),
        ],
        scratch=[
            pltpu.VMEM((4, 256, DA), F32), pltpu.VMEM((4, SPAN, 2 * DA), F32), pltpu.VMEM((1024, 128), F32),
            pltpu.VMEM((256, 4 * DA), F32), pltpu.VMEM((4, 256, DA), BF16), pltpu.VMEM((4, 256, 2 * FA), BF16),
            pltpu.VMEM((4, 256, DA), BF16),
        ],
        us=12,
        name="atom_back",
    )(*args)


def atom_end_kernel(
    dq_ref, dgate_ref, dkv_ref, prev_ref, next_ref, dmid_ref, x_ref, first_ref, u_ref, du_ref, cond_low_ref,
    w_qkvg_ref, dw_out_ref, dw_up_ref, dw_down_ref, dpool_ref, single_ref, tdu_ref, heads_ref, misc_ref,
    out_ref, packed_ref,
    dw_qkvg_ref, sums_ref, whole_ref,
):
    scale = sigmoid(part(u_ref, 0, DA))
    sums_ref[...] = jnp.zeros_like(sums_ref)
    dw_qkvg_ref[...] = jnp.zeros_like(dw_qkvg_ref)

    @pl.loop(0, 4)
    def _(s):
        whole_ref[...] = dkv_ref[s]
        whole_ref[:RIM, :] += prev_ref[s].astype(F32)
        whole_ref[256 - RIM :, :] += next_ref[s].astype(F32)
        grads = jnp.concatenate([dq_ref[s], whole_ref[...].astype(BF16), dgate_ref[s]], axis=1)
        dfirst = dot(grads, w_qkvg_ref[...], ((1,), (1,)))
        lines, inverse = normed(x_ref[s].astype(F32))
        out_ref[s] = dmid_ref[s] + norm_back_rows(dfirst * scale, lines, inverse)
        dw_qkvg_ref[...] += dot(first_ref[s], grads, ((0,), (0,)))
        sums_ref[:, :DA] += dfirst * lines
        sums_ref[:, DA:] += dfirst

    du = jnp.concatenate([sums_ref[:, :DA] * slope(scale), sums_ref[:, DA:], du_ref[...]], axis=1).astype(BF16)
    dw_cond = dot(cond_low_ref[...], du, ((0,), (0,)))
    down = dw_down_ref[...].reshape(16, 2, 8, DA)
    single = dot(single_ref[...], tdu_ref[...], ((0,), (0,))).reshape(16, 3, 8, 2 * DT)
    whole = jnp.concatenate(
        [
            dw_cond, dw_qkvg_ref[...], dw_out_ref[...], dw_up_ref[...], dpool_ref[...],
            down[:, 0].reshape(DA, DA), down[:, 1].reshape(DA, DA), misc_ref[...].astype(F32),
        ]
        + [single[:, i].reshape(DA, 2 * DT) for i in range(3)]
        + [jnp.zeros((DA, 512), F32)],
        axis=1,
    ).astype(BF16)
    for s in range(8):
        packed_ref[s, :, :1024] = whole[:, 1024 * s : 1024 * s + 1024]
        packed_ref[s, :, 1024:] = heads_ref[s]


def atom_end(*args):
    sds = jax.ShapeDtypeStruct
    return kernel_call(
        atom_end_kernel,
        [sds((4, 256, DA), F32), sds((8, DA, 1280), BF16)],
        scratch=[pltpu.VMEM((DA, 4 * DA), F32), pltpu.VMEM((256, 2 * DA), F32), pltpu.VMEM((256, 2 * DA), F32)],
        us=6,
        name="atom_end",
    )(*args)


def split_kernel(samp_ref, wide_ref, *refs):
    out_refs, whole_ref = refs[:4], refs[4]
    whole_ref[:, : 10 * DT] = wide_ref[...]
    whole_ref[:, 10 * DT :] = jnp.zeros((48, 512), BF16)
    for k in range(8):
        lanes = pl.ds(pl.multiple_of((samp_ref[0] ^ k) * 1024, 1024), 1024)
        out_refs[k // 2][k % 2] = whole_ref[:, lanes]


def split(samp, wide):
    return kernel_call(
        split_kernel,
        [jax.ShapeDtypeStruct((2, 48, 1024), BF16)] * 4,
        scratch=[pltpu.VMEM((48, 64 * DA), BF16)],
        scalars=1,
        us=2,
        name="split",
    )(samp, wide)


def collect_kernel(wide_ref, wide_part_ref, packed_ref, out_ref, total_ref):
    step = pl.program_id(0)

    @pl.when(step == 0)
    def _():
        total_ref[...] = jnp.zeros_like(total_ref)

    rows = packed_ref[0, :, :1024].astype(F32)
    for i in range(1, 32):
        rows += packed_ref[i, :, :1024].astype(F32)
    total_ref[:8] += rows
    for h in range(16):
        at = slice(8 + 8 * (h // 4), 16 + 8 * (h // 4))
        total_ref[at, 256 * (h % 4) : 256 * (h % 4) + 256] += packed_ref[h, :, 1024:].astype(F32) + packed_ref[
            16 + h, :, 1024:
        ].astype(F32)

    @pl.when(step == 3)
    def _():
        wide = wide_ref[...].astype(F32) + wide_part_ref[...].astype(F32)
        whole = jnp.concatenate([wide, total_ref[...]], axis=0).astype(BF16)
        for i in range(8):
            out_ref[i] = whole


def collect(wide, wide_part, packed):
    return kernel_call(
        collect_kernel,
        [jax.ShapeDtypeStruct((8, 88, 1024), BF16)],
        grid=(4,),
        in_specs=[fixed(48, 1024), fixed(48, 1024), pl.BlockSpec((32, 8, 1280), lambda i: (i, 0, 0))],
        out_specs=[fixed(8, 88, 1024)],
        scratch=[pltpu.VMEM((40, 1024), F32)],
        us=4,
        name="collect",
    )(wide, wide_part, packed)[0]


def hand_out_kernel(
    parts_ref, a_cond_ref, a_qkvg_ref, a_out_ref, a_up_ref, a_down_ref, a_pair_ref, pool_ref, t_cond_ref, t_qkvg_ref,
    t_out_ref, t_up_ref, t_down_ref, t_pair_ref,
):
    def wide(first, last, rows=slice(0, 48)):
        pieces = []
        while first < last:
            s, at = divmod(first, 1024)
            end = min(last - 1024 * s, 1024)
            pieces.append(parts_ref[s, rows, at:end].astype(F32))
            first = 1024 * s + end
        return jnp.concatenate(pieces, axis=1)

    def atoms(first, last):
        return wide(first, last, slice(48, 64))[:8]

    t_up_ref[...] = wide(0, 4 * DT)
    t_out_ref[...] = wide(4 * DT, 5 * DT)
    t_qkvg_ref[:, 3 * DT :] = wide(5 * DT, 6 * DT)
    t_down_ref[:48, :] = wide(6 * DT, 7 * DT)
    t_down_ref[48:, :] = wide(7 * DT, 8 * DT)
    conds = wide(8 * DT, 10 * DT)
    t_cond_ref[:, 2 * DT : 4 * DT] = conds[:24]
    t_cond_ref[:, 4 * DT :] = conds[24:]
    for i in range(3):
        t_cond_ref[8 * i : 8 * i + 8, : 2 * DT] = atoms(3072 + 2 * DT * i, 3072 + 2 * DT * (i + 1))
    a_cond_ref[...] = atoms(0, 768)
    a_qkvg_ref[...] = atoms(768, 1280)
    a_out_ref[...] = atoms(1280, 1408)
    a_up_ref[...] = atoms(1408, 1920)
    pool_ref[...] = atoms(1920, 2688)
    a_down_ref[:8] = atoms(2688, 2816)
    a_down_ref[8:] = atoms(2816, 2944)
    misc = atoms(2944, 3072)
    t_pair_ref[...] = misc[0:1]
    a_pair_ref[...] = misc[1:2, :4]
    heads = []
    for h in range(16):
        at = 56 + 8 * (h // 4)
        lanes = slice(256 * (h % 4), 256 * (h % 4) + 3 * HS)
        base = at // 16 * 16
        rows = [parts_ref[s, base : min(base + 16, 88), lanes].astype(F32) for s in range(6)]
        heads.append(jnp.concatenate([r[at - base : at - base + 8] for r in rows], axis=0))
    for i in range(3):
        t_qkvg_ref[:, DT * i : DT * i + DT] = jnp.concatenate(
            [head[:, HS * i : HS * i + HS] for head in heads], axis=1
        )


def hand_out(parts):
    sds = jax.ShapeDtypeStruct
    shapes = [
        (8, 768), (8, 512), (8, 128), (8, 512), (16, 128), (1, 4), (8, 768), (24, 6 * DT), (48, 4 * DT), (48, DT),
        (48, 2 * FT), (96, DT), (1, 128),
    ]
    return kernel_call(
        hand_out_kernel,
        [sds(shape, F32) for shape in shapes],
        us=4,
        name="hand_out",
    )(parts)


def both_axes(x):
    return lax.all_to_all(x, ("samp", "seq"), 0, 0, tiled=True)


def along_seq(x):
    return lax.all_to_all(x, "seq", 0, 0, tiled=True)


ordered = lambda *x: lax.optimization_barrier(x)


def from_samp(part, k):
    return lax.ppermute(part, "samp", [(i, i ^ k) for i in range(8)])


def total(*parts):
    return sum(part.astype(F32) for part in parts).astype(BF16)


def body(
    atom_in,
    tok_in,
    atom_cond,
    single_cond,
    atom_pair,
    token_pair,
    atom_w_cond,
    atom_w_qkvg,
    atom_w_out,
    atom_w_up,
    atom_w_down,
    atom_w_pair,
    pool_weight,
    token_w_cond,
    token_w_qkvg,
    token_w_out,
    token_w_up,
    token_w_down,
    token_w_pair,
    cotangent,
):
    samp, seq = lax.axis_index("samp"), lax.axis_index("seq")
    up, down = [(i, i + 1) for i in range(15)], [(i + 1, i) for i in range(15)]
    rims = jnp.concatenate([atom_in, atom_cond[None]], axis=0)
    from_prev = lax.ppermute(rims[:, 256 - RIM :], "seq", up)
    from_next = lax.ppermute(rims[:, :RIM], "seq", down)
    samp = samp.astype(jnp.int32).reshape(1)
    normed_pair, token_bias = pair_bias(samp, token_pair, token_w_pair)
    token_bias = along_seq(token_bias).reshape(NT, 128)
    atom_in, token_bias = ordered(atom_in, token_bias)
    token_bias = lax.all_gather(token_bias, "samp", axis=0, axis_index_groups=[SAMP_RING])

    key_index = 256 * seq - RIM + 32 * jnp.arange(8)[:, None] + jnp.arange(128)[None, :]
    mask = jnp.where((key_index >= 0) & (key_index < 4096), 0.0, masked).astype(F32)
    (
        first, query, keyval, probs, gate, attended, middle, cond_low, cond_proj, pooled,
        start, tfirst, tgate, tcond_proj, single_low, runs,
    ) = front(
        atom_in, from_prev, from_next, atom_cond, atom_pair, mask, atom_w_pair.astype(F32), atom_w_cond,
        atom_w_qkvg, atom_w_out, atom_w_up, atom_w_down, pool_weight, tok_in, single_cond, token_w_cond, token_w_qkvg,
    )
    prep = atom_prep(cond_proj, middle, gate, attended, atom_w_out, atom_w_up, atom_w_down)
    runs, *prep = ordered(along_seq(runs), *prep)
    qkv, tprobs, tattended = token_attention(runs, token_bias)
    tattended, sent = ordered(tattended, tfirst)
    lines = lax.all_gather(sent, "seq", axis=0, axis_index_groups=[RING])
    (
        token_out, cots, tdgate, tdmid, gated, gbranch, second, dup, hidden, gdown, tdu,
    ) = turn(
        along_seq(tattended), tgate, start, tcond_proj, cotangent, token_w_out, token_w_up, token_w_down
    )
    cots = along_seq(cots)
    wide = token_weights(gated, gbranch, tfirst, tdgate, second, dup, hidden, gdown, single_low, tdu)
    cots, wide = ordered(cots, wide)
    wide = lax.psum_scatter(wide, "seq", scatter_dimension=0, tiled=True, axis_index_groups=[RING])
    tgrads, *slopes = token_attention_back(samp, qkv, tprobs, cots)
    heads = head_weights(tgrads, lines)
    received = [from_samp(slopes[k], 2 * k) for k in range(1, 4)]
    tgrads, heads, *received = ordered(along_seq(tgrads), heads, *received)
    slopes = total(slopes[0], *received)
    slopes = total(slopes[0], from_samp(slopes[1], 1))
    slopes = along_seq(slopes.reshape(16, 64, 128))
    grad_tok, gpooled, dpool, tdu = back(
        tgrads, tdgate, tdmid, start, tcond_proj, token_w_qkvg, pool_weight, pooled
    )
    (
        dquery, dgate, dkeyval, to_prev, to_next, dmid, du, dw_out, dw_up, dw_down, dpair,
    ) = atom_back(
        gpooled.reshape(4, 64, DA), cond_proj, middle, gate, attended, query, keyval, probs, atom_pair,
        atom_w_out, atom_w_up, atom_w_down, *prep,
    )
    back_next = lax.ppermute(to_prev, "seq", down)
    back_prev = lax.ppermute(to_next, "seq", up)
    misc = pair_grad(slopes, normed_pair, dpair)
    grad_atoms, packed = atom_end(
        dquery, dgate, dkeyval, back_prev, back_next, dmid, atom_in, first, cond_proj, du, cond_low,
        atom_w_qkvg, dw_out, dw_up, dw_down, dpool, single_low, tdu, heads, misc,
    )
    packed = both_axes(packed.reshape(128, 8, 1280))
    wide = split(samp, wide)
    wide = total(wide[0], *[from_samp(wide[k], 2 * k) for k in range(1, 4)])
    wide = wide[0], from_samp(wide[1], 1)
    parts = lax.all_to_all(collect(*wide, packed), "samp", 0, 0, tiled=True)
    return (token_out, grad_atoms, grad_tok, *hand_out(parts))


def solution(mesh):
    rows, both, whole = P("seq", None), P("samp", "seq", None), P()
    in_specs = (both, both, rows, rows, P(None, "seq", None), P(None, "seq", None)) + (whole,) * 13 + (both,)
    out_specs = (both,) * 3 + (rows,) * 13
    mapped = jax.shard_map(body, mesh=mesh, in_specs=in_specs, out_specs=out_specs, check_vma=False)

    def run(*args):
        with jax.sharding.use_abstract_mesh(mesh.abstract_mesh):
            return mapped(*args)

    return run
```

```python
import jax
import jax.numpy as jnp
from jax import lax
from jax.experimental import pallas as pl
from jax.experimental.pallas import tpu as pltpu
from jax.sharding import PartitionSpec as P

eps = 1e-05
masked = -1000000000.0

MIB = 1 << 20
F32, BF16 = jnp.float32, jnp.bfloat16


def kernel_call(kernel, out_shape, grid=(1,), in_specs=None, out_specs=None, scratch=(), scalars=0, us=1, name=None):
    def run(*args):
        return pl.pallas_call(
            kernel,
            out_shape=list(out_shape),
            grid_spec=pltpu.PrefetchScalarGridSpec(
                num_scalar_prefetch=scalars,
                grid=grid,
                in_specs=in_specs or [fixed(*a.shape) for a in args[scalars:]],
                out_specs=out_specs or [fixed(*o.shape) for o in out_shape],
                scratch_shapes=list(scratch),
            ),
            compiler_params=pltpu.CompilerParams(vmem_limit_bytes=60 * MIB),
            cost_estimate=pl.CostEstimate(flops=us << 30, bytes_accessed=us << 20, transcendentals=0),
            name=name,
        )(*args)

    return run


def fixed(*shape):
    return pl.BlockSpec(shape, lambda *_: (0,) * len(shape), pipeline_mode=pl.Buffered(1))


def dot(left, right, over=((1,), (0,))):
    return lax.dot_general(left, right, (over, ((), ())), preferred_element_type=F32)


def swap_halves(first, second):
    low = lax.broadcasted_iota(jnp.int32, first.shape, 1) < 64
    half = first.shape[1] // 2
    return (
        jnp.where(low, first, pltpu.roll(second, half, 1)),
        jnp.where(low, pltpu.roll(first, half, 1), second),
    )


def runs_to_tokens(runs_ref, tokens_ref):
    for pair in range(runs_ref.shape[0] // 2):
        for duo in range(2):
            lanes = slice(128 * duo, 128 * duo + 128)
            made = swap_halves(
                runs_ref[2 * pair, :, lanes].astype(F32), runs_ref[2 * pair + 1, :, lanes].astype(F32)
            )
            for k in range(2):
                tokens_ref[2 * duo + k, :, 128 * pair : 128 * pair + 128] = made[k].astype(
                    tokens_ref.dtype
                )


def tokens_to_runs(tokens_ref, runs_ref):
    for pair in range(runs_ref.shape[0] // 2):
        lanes = slice(128 * pair, 128 * pair + 128)
        for duo in range(2):
            made = swap_halves(tokens_ref[2 * duo, :, lanes], tokens_ref[2 * duo + 1, :, lanes])
            for k in range(2):
                runs_ref[2 * pair + k, :, 128 * duo : 128 * duo + 128] = made[k].astype(runs_ref.dtype)


HS = 48
NT = 1024
QB = 256
SAMP_RING = [0, 2, 4, 6, 7, 5, 3, 1]


def attention_kernel(runs_ref, bias_ref, qkv_ref, probs_ref, out_ref, heads_ref):
    sample = pl.program_id(0)

    @pl.when(sample == 0)
    def _():
        runs_to_tokens(runs_ref, qkv_ref)

    keys = qkv_ref[sample, HS : 2 * HS, :]
    values = qkv_ref[sample, 2 * HS :, :]

    def scores_of(block):
        rows = slice(block * QB, block * QB + QB)
        made = dot(qkv_ref[sample, :HS, rows], keys, ((0,), (0,))) * HS ** (-0.5)
        return made + jnp.concatenate([bias_ref[SAMP_RING.index(i), rows, :] for i in range(8)], axis=1).astype(F32)

    count = NT // QB
    ahead = scores_of(0)
    for block in range(count):
        rows = slice(block * QB, block * QB + QB)
        scores = ahead
        if block + 1 < count:
            ahead = scores_of(block + 1)
        exponent = jnp.exp(scores - jnp.max(scores, axis=1, keepdims=True))
        probs = (exponent * (1.0 / jnp.sum(exponent, axis=1, keepdims=True))).astype(BF16)
        probs_ref[0, rows, :] = probs
        heads_ref[sample, :, rows] = dot(probs, values, ((1,), (1,))).T

    @pl.when(sample == 3)
    def _():
        tokens_to_runs(heads_ref, out_ref)


def token_attention(runs, bias):
    return kernel_call(
        attention_kernel,
        [
            jax.ShapeDtypeStruct((4, 3 * HS, NT), BF16),
            jax.ShapeDtypeStruct((4, NT, NT), BF16),
            jax.ShapeDtypeStruct((16, HS, 256), BF16),
        ],
        grid=(4,),
        in_specs=[fixed(16, 3 * HS, 256)] + [fixed(8, NT, 128)],
        out_specs=[
            fixed(4, 3 * HS, NT), pl.BlockSpec((1, NT, NT), lambda s: (s, 0, 0)), fixed(16, HS, 256),
        ],
        scratch=[pltpu.VMEM((4, HS, NT), F32)],
        us=13,
        name="token_attention",
    )(runs, bias)


def attention_back_kernel(samp_ref, qkv_ref, probs_ref, cot_ref, out_ref, *refs):
    pair_refs, (cots_ref, grads_ref, total_ref) = refs[:4], refs[4:]
    sample = pl.program_id(0)

    @pl.when(sample == 0)
    def _():
        runs_to_tokens(cot_ref, cots_ref)
        total_ref[...] = jnp.zeros_like(total_ref)

    keys = qkv_ref[sample, HS : 2 * HS, :]
    values = qkv_ref[sample, 2 * HS :, :]

    def weights_of(block):
        return dot(cots_ref[sample, :, block * QB : block * QB + QB], values, ((0,), (0,)))

    key_grad, value_grad = 0.0, 0.0
    count = NT // QB
    ahead = weights_of(0)
    for block in range(count):
        rows = slice(block * QB, block * QB + QB)
        now = ahead
        if block + 1 < count:
            ahead = weights_of(block + 1)
        low = probs_ref[0, rows, :]
        probs = low.astype(F32)
        weighed = probs * now
        slopes = weighed - probs * jnp.sum(weighed, axis=1, keepdims=True)
        slopes_low = slopes.astype(BF16)
        total_ref[rows, :] += slopes
        grads_ref[sample, :HS, rows] = dot(keys, slopes_low, ((1,), (1,))) * HS ** (-0.5)
        key_grad += dot(qkv_ref[sample, :HS, rows], slopes_low)
        value_grad += dot(cots_ref[sample, :, rows], low)
    grads_ref[sample, HS : 2 * HS, :] = key_grad * HS ** (-0.5)
    grads_ref[sample, 2 * HS :, :] = value_grad

    @pl.when(sample == 3)
    def _():
        tokens_to_runs(grads_ref, out_ref)
        for k in range(8):
            lanes = pl.ds(pl.multiple_of((samp_ref[0] ^ k) * 128, 128), 128)
            pair_refs[k // 2][:, k % 2] = total_ref[:, lanes].astype(BF16).reshape(16, 64, 128)


def token_attention_back(samp, qkv, probs, cots):
    return kernel_call(
        attention_back_kernel,
        [jax.ShapeDtypeStruct((16, 3 * HS, 256), BF16)] + [jax.ShapeDtypeStruct((16, 2, 64, 128), BF16)] * 4,
        grid=(4,),
        in_specs=[fixed(4, 3 * HS, NT), pl.BlockSpec((1, NT, NT), lambda s, _: (s, 0, 0)), fixed(16, HS, 256)],
        out_specs=[fixed(16, 3 * HS, 256)] + [fixed(16, 2, 64, 128)] * 4,
        scratch=[
            pltpu.VMEM((4, HS, NT), BF16),
            pltpu.VMEM((4, 3 * HS, NT), F32),
            pltpu.VMEM((NT, NT), F32),
        ],
        scalars=1,
        us=14,
        name="token_attention_back",
    )(samp, qkv, probs, cots)


def normed_rows(pair_ref):
    pair = pair_ref[...].astype(F32)
    centred = pair - jnp.mean(pair, axis=0, keepdims=True)
    inverse = lax.rsqrt(jnp.mean(centred * centred, axis=0, keepdims=True) + eps)
    return jnp.swapaxes((centred * inverse).astype(BF16), 0, 1)


def pair_kernel(samp_ref, pair_ref, weight_ref, normed_ref, bias_ref):
    low = normed_rows(pair_ref)
    normed_ref[...] = low
    weight = weight_ref[...]
    bias = jnp.stack([dot(weight, low[i]) for i in range(low.shape[0])], axis=0)
    bias_ref[...] = jnp.swapaxes(bias, 0, 1).astype(BF16)


def pair_beside_kernel(samp_ref, pair_ref, normed_ref):
    normed_ref[...] = normed_rows(pair_ref)


def pair_beside(samp, pair):
    return kernel_call(
        pair_beside_kernel,
        [jax.ShapeDtypeStruct((64, 128, 128), BF16)],
        grid=(2,),
        in_specs=[pl.BlockSpec((128, 32, 128), lambda i, samp: (0, i, samp[0] ^ 1))],
        out_specs=[pl.BlockSpec((32, 128, 128), lambda i, _: (i, 0, 0))],
        scalars=1,
        us=4,
        name="pair_beside",
    )(samp, pair)[0]


def pair_bias(samp, pair, weight):
    return kernel_call(
        pair_kernel,
        [jax.ShapeDtypeStruct((64, 128, 128), BF16), jax.ShapeDtypeStruct((16, 64, 128), BF16)],
        grid=(2,),
        in_specs=[pl.BlockSpec((128, 32, 128), lambda i, samp: (0, i, samp[0])), fixed(16, 128)],
        out_specs=[
            pl.BlockSpec((32, 128, 128), lambda i, _: (i, 0, 0)),
            pl.BlockSpec((16, 32, 128), lambda i, _: (0, i, 0)),
        ],
        scalars=1,
        us=5,
        name="pair_bias",
    )(samp, pair, weight)


def pair_back_kernel(slopes_ref, normed_ref, beside_ref, atoms_ref, out_ref, grad_ref):
    step = pl.program_id(0)
    slopes = jnp.swapaxes(slopes_ref[...], 0, 1)

    @pl.when(step == 0)
    def _():
        grad_ref[...] = jnp.zeros_like(grad_ref)

    def add(ref):
        made = dot(slopes[0], ref[0], ((1,), (1,)))
        for i in range(1, 32):
            made += dot(slopes[i], ref[i], ((1,), (1,)))
        grad_ref[...] += made

    @pl.when(step < 2)
    def _():
        add(normed_ref)

    @pl.when(step >= 2)
    def _():
        add(beside_ref)

    @pl.when(step == 3)
    def _():
        atoms = jnp.sum(atoms_ref[...], axis=1, keepdims=True)
        lane = lax.broadcasted_iota(jnp.int32, (16, 128), 1)
        rows = jnp.where(lane == 0, atoms[:16], 0.0)
        for h in range(1, 4):
            rows += jnp.where(lane == h, atoms[16 * h : 16 * h + 16], 0.0)
        line = lax.broadcasted_iota(jnp.int32, (16, 8, 128), 1)
        both = jnp.where(line == 0, grad_ref[...][:, None, :], 0.0) + jnp.where(line == 1, rows[:, None, :], 0.0)
        out_ref[...] = both.reshape(128, 128).astype(BF16)


def pair_grad(slopes, normed, beside, atoms):
    return kernel_call(
        pair_back_kernel,
        [jax.ShapeDtypeStruct((128, 128), BF16)],
        grid=(4,),
        in_specs=[
            pl.BlockSpec((16, 32, 128), lambda i: (0, i, 0)),
            pl.BlockSpec((32, 128, 128), lambda i: (jnp.minimum(i, 1), 0, 0)),
            pl.BlockSpec((32, 128, 128), lambda i: (jnp.maximum(i - 2, 0), 0, 0)),
            fixed(64, 128),
        ],
        out_specs=[fixed(128, 128)],
        scratch=[pltpu.VMEM((16, 128), F32)],
        us=6,
        name="pair_grad",
    )(slopes, normed, beside, atoms)[0]


DA, DT, FT, FA = 128, 768, 1536, 256
RIM = 48
RING = [0, 1, 4, 5, 8, 9, 12, 13, 14, 15, 10, 11, 6, 7, 2, 3]
SPAN = 256 + 2 * RIM


def normed(x):
    centred = x - jnp.mean(x, axis=-1, keepdims=True)
    inverse = lax.rsqrt(jnp.mean(centred * centred, axis=-1, keepdims=True) + eps)
    return centred * inverse, inverse


def sigmoid(x):
    return 1.0 / (1.0 + jnp.exp(-x))


def own_head():
    shape = (1, 4, 32, 128)
    return lax.broadcasted_iota(jnp.int32, shape, 3) // 32 == lax.broadcasted_iota(jnp.int32, shape, 1)


def head_rows(rows):
    return jnp.where(own_head(), rows.reshape(8, 1, 32, 128), 0.0).reshape(1024, 128).astype(BF16)


def rows_of_heads(full):
    return jnp.sum(jnp.where(own_head(), full.reshape(8, 4, 32, 128), 0.0), axis=1).reshape(256, 128)


def by_window(made):
    return jnp.concatenate([made(w) for w in range(8)], axis=0)


def pair_norm(pair):
    centred = pair - jnp.mean(pair, axis=0, keepdims=True)
    inverse = lax.rsqrt(jnp.mean(centred * centred, axis=0, keepdims=True) + eps)
    return (centred * inverse).astype(BF16).astype(F32)


def part(ref, i, width, rows=slice(None)):
    return ref[rows, i * width : (i + 1) * width]


def front_kernel(
    x_ref, prev_ref, next_ref, cond_ref, pair_ref, mask_ref, w_pair_ref, w_cond_ref, w_qkvg_ref, w_out_ref,
    w_up_ref, w_down_ref, pool_ref, tok_ref, single_ref, tw_cond_hbm, tw_qkvg_hbm,
    first_ref, q_ref, kv_ref, probs_ref, gate_ref, att_ref, mid_ref, cond_low_ref, u_ref, pooled_ref,
    start_ref, tfirst_ref, tgate_ref, tu_ref, single_low_ref, runs_ref,
    bias_ref, y_ref, uh_ref, tw_cond_ref, tw_qkvg_ref, sems,
):
    loads = [
        pltpu.make_async_copy(tw_cond_hbm, tw_cond_ref, sems.at[0]),
        pltpu.make_async_copy(tw_qkvg_hbm, tw_qkvg_ref, sems.at[1]),
    ]
    for load in loads:
        load.start()
    cond = jnp.concatenate([prev_ref[4], cond_ref[...], next_ref[4]], axis=0).astype(F32)
    cond_low = normed(cond)[0].astype(BF16)
    cond_low_ref[...] = cond_low[RIM : RIM + 256]
    u_ref[...] = dot(cond_low[RIM : RIM + 256], w_cond_ref[...])
    uh_ref[...] = dot(cond_low, w_cond_ref[:, : 2 * DA])
    pairs = pair_norm(pair_ref[...].astype(F32))
    for h in range(4):
        bias = pairs[0] * w_pair_ref[0, h]
        for c in range(1, 16):
            bias += pairs[c] * w_pair_ref[c, h]
        for w in range(8):
            at = 128 * w + 32 * h
            bias_ref[at : at + 32, :] = bias[32 * w : 32 * w + 32] + mask_ref[w : w + 1, :]

    scale_a, shift_a = sigmoid(part(uh_ref, 0, DA)), part(uh_ref, 1, DA)
    gate_a, scale_b, shift_b, gate_b = (
        sigmoid(part(u_ref, 2, DA)), sigmoid(part(u_ref, 3, DA)), part(u_ref, 4, DA), sigmoid(part(u_ref, 5, DA)),
    )

    def atoms(s):
        x = jnp.concatenate([prev_ref[s], x_ref[s], next_ref[s]], axis=0).astype(F32)
        first = (scale_a * normed(x)[0] + shift_a).astype(BF16)
        projected = dot(first, w_qkvg_ref[...])
        own = projected[RIM : RIM + 256]
        first_ref[s] = first[RIM : RIM + 256]
        query = own[:, :DA].astype(BF16)
        q_ref[s] = query
        keys = projected[:, DA : 2 * DA].astype(BF16)
        values = projected[:, 2 * DA : 3 * DA].astype(BF16)
        kv_ref[s, :, :DA] = keys
        kv_ref[s, :, DA:] = values
        gate = sigmoid(own[:, 3 * DA :])
        gate_ref[s] = gate
        rows = head_rows(query.astype(F32))
        scores = by_window(lambda w: dot(rows[128 * w : 128 * w + 128], keys[32 * w : 32 * w + 128], ((1,), (1,))))
        scores = scores * 32 ** (-0.5) + bias_ref[...]
        exponent = jnp.exp(scores - jnp.max(scores, axis=1, keepdims=True))
        probs = (exponent * (1.0 / jnp.sum(exponent, axis=1, keepdims=True))).astype(BF16)
        probs_ref[s] = probs
        attended = rows_of_heads(
            by_window(lambda w: dot(probs[128 * w : 128 * w + 128], values[32 * w : 32 * w + 128]))
        )
        att_ref[s] = attended
        branch = dot((gate * attended).astype(BF16), w_out_ref[...])
        middle = x[RIM : RIM + 256] + gate_a * branch
        mid_ref[s] = middle
        second = (scale_b * normed(middle)[0] + shift_b).astype(BF16)
        up = dot(second, w_up_ref[...])
        hidden = (up[:, :FA] * sigmoid(up[:, :FA]) * up[:, FA:]).astype(BF16)
        y_ref[s] = middle + gate_b * dot(hidden, w_down_ref[...])
        pooled = y_ref[s, pl.ds(0, 64, stride=4), :]
        for k in range(1, 4):
            pooled += y_ref[s, pl.ds(k, 64, stride=4), :]
        pooled_ref[s] = (pooled * 0.25).astype(BF16)

    for s in range(4):
        atoms(s)

    for load in loads:
        load.wait()
    single_low = normed(single_ref[...].astype(F32))[0].astype(BF16)
    single_low_ref[...] = single_low
    for i in range(6):
        tu_ref[:, DT * i : DT * i + DT] = dot(single_low, tw_cond_ref[:, DT * i : DT * i + DT])
    pooled = pooled_ref[...].reshape(256, DA)
    start = tok_ref[...].reshape(256, DT).astype(F32) + dot(pooled, pool_ref[...])
    start_ref[...] = start
    lines = normed(start)[0]
    scale, shift = sigmoid(part(tu_ref, 0, DT)), part(tu_ref, 1, DT)
    for s in range(4):
        tfirst_ref[64 * s : 64 * s + 64, :] = (scale * lines[64 * s : 64 * s + 64] + shift).astype(BF16)
    first = tfirst_ref[...]
    for i in range(3):
        turned = dot(first, part(tw_qkvg_ref, i, DT)).T.astype(BF16)
        for h in range(16):
            runs_ref[h, HS * i : HS * i + HS, :] = turned[HS * h : HS * h + HS]
    tgate_ref[...] = sigmoid(dot(first, part(tw_qkvg_ref, 3, DT)))


def front(*args):
    sds = jax.ShapeDtypeStruct
    specs = [fixed(*a.shape) for a in args]
    specs[6] = pl.BlockSpec(memory_space=pltpu.SMEM)
    specs[15] = specs[16] = pl.BlockSpec(memory_space=pl.ANY)
    return kernel_call(
        front_kernel,
        [
            sds((4, 256, DA), BF16), sds((4, 256, DA), BF16), sds((4, SPAN, 2 * DA), BF16),
            sds((4, 1024, 128), BF16), sds((4, 256, DA), F32), sds((4, 256, DA), F32),
            sds((4, 256, DA), F32), sds((256, DA), BF16), sds((256, 6 * DA), F32), sds((4, 64, DA), BF16),
            sds((256, DT), F32), sds((256, DT), BF16), sds((256, DT), F32), sds((64, 6 * DT), F32),
            sds((64, 384), BF16), sds((16, 3 * HS, 256), BF16),
        ],
        in_specs=specs,
        scratch=[
            pltpu.VMEM((1024, 128), F32), pltpu.VMEM((4, 256, DA), F32), pltpu.VMEM((SPAN, 2 * DA), F32),
            pltpu.VMEM((384, 6 * DT), BF16), pltpu.VMEM((DT, 4 * DT), BF16), pltpu.SemaphoreType.DMA((2,)),
        ],
        us=24,
        name="front",
    )(*args)


def slope(squashed):
    return squashed * (1.0 - squashed)


def norm_back_rows(gradient, lines, inverse):
    return inverse * (
        gradient
        - jnp.mean(gradient, axis=-1, keepdims=True)
        - lines * jnp.mean(gradient * lines, axis=-1, keepdims=True)
    )


def turn_kernel(
    runs_ref, tgate_ref, start_ref, tu_ref, cot_ref, w_out_hbm, w_up_hbm, w_down_hbm,
    out_ref, cots_ref, dgate_ref, dmid_ref, a_ref, gbranch_ref, second_ref, dup_ref, hidden_ref, gdown_ref,
    du_ref,
    up_ref, mid_ref, branch_ref, down_ref, w_out_ref, w_up_ref, w_down_ref, sems,
):
    loads = [
        pltpu.make_async_copy(w_out_hbm, w_out_ref, sems.at[0]),
        pltpu.make_async_copy(w_up_hbm, w_up_ref, sems.at[1]),
        pltpu.make_async_copy(w_down_hbm, w_down_ref, sems.at[2]),
    ]
    for load in loads:
        load.start()
    attended = runs_ref[...].reshape(DT, 256).astype(F32).T
    gate = tgate_ref[...]
    gated = (gate * attended).astype(BF16)
    a_ref[...] = gated
    loads[0].wait()
    branch_ref[...] = dot(gated, w_out_ref[...])
    gate_a, scale_b, shift_b, gate_b = (
        sigmoid(part(tu_ref, 2, DT)), sigmoid(part(tu_ref, 3, DT)), part(tu_ref, 4, DT), sigmoid(part(tu_ref, 5, DT)),
    )
    runs = [slice(64 * s, 64 * s + 64) for s in range(4)]
    for r in runs:
        middle = start_ref[r, :] + gate_a * branch_ref[r, :]
        mid_ref[r, :] = middle
        second_ref[r, :] = (scale_b * normed(middle)[0] + shift_b).astype(BF16)
    second = second_ref[...]
    loads[1].wait()
    loads[2].wait()
    cut = 512
    for j in range(FT // cut):
        e = dot(second, w_up_ref[:, cut * j : cut * j + cut])
        f = dot(second, w_up_ref[:, FT + cut * j : FT + cut * j + cut])
        up_ref[:, cut * j : cut * j + cut] = e
        up_ref[:, FT + cut * j : FT + cut * j + cut] = f
        hidden = (e * sigmoid(e) * f).astype(BF16)
        hidden_ref[:, cut * j : cut * j + cut] = hidden
        piece = dot(hidden, w_down_ref[cut * j : cut * j + cut, :])
        if j == 0:
            down_ref[...] = piece
        else:
            down_ref[...] += piece
    total = jnp.zeros((64, DT), F32)
    for s, r in enumerate(runs):
        cot = cot_ref[s].astype(F32)
        out_ref[s] = (mid_ref[r, :] + gate_b * down_ref[r, :]).astype(BF16)
        gdown_ref[r, :] = (cot * gate_b).astype(BF16)
        total += cot * down_ref[r, :]
    du_ref[:, 3 * DT :] = (total * slope(gate_b)).astype(BF16)
    gdown = gdown_ref[...]
    dsecond = jnp.zeros((256, DT), F32)
    for j in range(FT // cut):
        dhidden = dot(gdown, w_down_ref[cut * j : cut * j + cut, :], ((1,), (1,)))
        e = up_ref[:, cut * j : cut * j + cut]
        f = up_ref[:, FT + cut * j : FT + cut * j + cut]
        half = sigmoid(e)
        de = (dhidden * f * half * (1.0 + e * (1.0 - half))).astype(BF16)
        df = (dhidden * e * half).astype(BF16)
        dup_ref[:, cut * j : cut * j + cut] = de
        dup_ref[:, FT + cut * j : FT + cut * j + cut] = df
        piece = dot(de, w_up_ref[:, cut * j : cut * j + cut], ((1,), (1,)))
        piece += dot(df, w_up_ref[:, FT + cut * j : FT + cut * j + cut], ((1,), (1,)))
        dsecond += piece
    down_ref[...] = dsecond
    total_a = jnp.zeros((64, DT), F32)
    total_b = jnp.zeros((64, DT), F32)
    total_c = jnp.zeros((64, DT), F32)
    for s, r in enumerate(runs):
        d = down_ref[r, :]
        lines, inverse = normed(mid_ref[r, :])
        dmid = cot_ref[s].astype(F32) + norm_back_rows(d * scale_b, lines, inverse)
        dmid_ref[r, :] = dmid
        gbranch_ref[r, :] = (dmid * gate_a).astype(BF16)
        total_a += dmid * branch_ref[r, :]
        total_b += d * lines
        total_c += d
    du_ref[:, :DT] = (total_a * slope(gate_a)).astype(BF16)
    du_ref[:, DT : 2 * DT] = (total_b * slope(scale_b)).astype(BF16)
    du_ref[:, 2 * DT : 3 * DT] = total_c.astype(BF16)
    dgated = dot(gbranch_ref[...], w_out_ref[...], ((1,), (1,)))
    dgate_ref[...] = (dgated * attended * slope(gate)).astype(BF16)
    cots_ref[...] = (dgated * gate).T.astype(BF16).reshape(16, HS, 256)


def turn(*args):
    sds = jax.ShapeDtypeStruct
    rows = lambda n, t=BF16: sds((256, n), t)
    return kernel_call(
        turn_kernel,
        [
            sds((4, 64, DT), BF16), sds((16, HS, 256), BF16), rows(DT), rows(DT, F32), rows(DT), rows(DT),
            rows(DT), rows(2 * FT), rows(FT), rows(DT), sds((64, 4 * DT), BF16),
        ],
        in_specs=[fixed(*a.shape) for a in args[:5]] + [pl.BlockSpec(memory_space=pl.ANY)] * 3,
        scratch=[pltpu.VMEM((256, 2 * FT), F32)]
        + [pltpu.VMEM((256, DT), F32)] * 3
        + [pltpu.VMEM(a.shape, BF16) for a in args[5:]]
        + [pltpu.SemaphoreType.DMA((3,))],
        us=12,
        name="turn",
    )(*args)


def weights_kernel(
    a_ref, gbranch_ref, first_ref, dgate_ref, second_ref, dup_ref, hidden_ref, gdown_ref, single_ref, du_ref, out_ref,
):
    step = pl.program_id(0)

    def write(rows, lanes=slice(None)):
        for at, run in enumerate(RING):
            out_ref[48 * at : 48 * at + 48, lanes] = rows[run]

    def square(left, right):
        return dot(left[...], right[...], ((0,), (0,))).astype(BF16)

    @pl.when(step < 2)
    def _():
        write(square(second_ref, dup_ref).reshape(16, 48, FT))

    @pl.when(step == 2)
    def _():
        write(square(a_ref, gbranch_ref).reshape(16, 48, DT), slice(0, DT))
        write(square(first_ref, dgate_ref).reshape(16, 48, DT), slice(DT, FT))

    @pl.when(step == 3)
    def _():
        made = square(hidden_ref, gdown_ref).reshape(16, 2, 48, DT)
        write(made[:, 0], slice(0, DT))
        write(made[:, 1], slice(DT, FT))

    @pl.when(step == 4)
    def _():
        made = dot(single_ref[...], du_ref[...], ((0,), (0,))).reshape(16, 24, 4 * DT)
        write(jnp.concatenate([made[:, :, :FT], made[:, :, FT:]], axis=1).astype(BF16))


def token_weights(*args):
    specs = [fixed(*a.shape) for a in args]
    specs[5] = pl.BlockSpec((256, FT), lambda i: (0, jnp.minimum(i, 1)))
    return kernel_call(
        weights_kernel,
        [jax.ShapeDtypeStruct((DT, 10 * DT), BF16)],
        grid=(5,),
        in_specs=specs,
        out_specs=[pl.BlockSpec((DT, FT), lambda i: (0, i))],
        us=12,
        name="token_weights",
    )(*args)[0]


def head_weights_kernel(grads_ref, lines_ref, out_ref, total_ref):
    step = pl.program_id(0)

    @pl.when(step == 0)
    def _():
        total_ref[...] = jnp.zeros_like(total_ref)

    for k in range(2):
        total_ref[...] += dot(grads_ref[k], lines_ref[k])

    @pl.when(step == 7)
    def _():
        made = total_ref[...].T.reshape(16, 6, 8, 3 * HS)
        out_ref[...] = jnp.zeros_like(out_ref)
        for s in range(6):
            out_ref[s, :, : 3 * HS] = made[:, s].reshape(DA, 3 * HS).astype(BF16)


def head_weights(grads, lines):
    return kernel_call(
        head_weights_kernel,
        [jax.ShapeDtypeStruct((8, DA, 256), BF16)],
        grid=(8,),
        in_specs=[
            pl.BlockSpec((2, 3 * HS, 256), lambda i: (jnp.where(i < 4, 2 * i, 15 - 2 * i), 0, 0)),
            pl.BlockSpec((2, 256, DT), lambda i: (i, 0, 0)),
        ],
        out_specs=[fixed(8, DA, 256)],
        scratch=[pltpu.VMEM((3 * HS, DT), F32)],
        us=6,
        name="head_weights",
    )(grads, lines)[0]


def back_kernel(
    runs_ref, dgate_ref, dmid_ref, start_ref, tu_ref, w_qkvg_hbm, pool_ref, pooled_ref,
    out_ref, gpooled_ref, dpool_ref, ducat_ref,
    dfirst_ref, gpool_ref, w_qkvg_ref, sems,
):
    loads = [
        pltpu.make_async_copy(
            w_qkvg_hbm.at[:, DT * i : DT * i + DT], w_qkvg_ref.at[:, DT * i : DT * i + DT], sems.at[i]
        )
        for i in range(4)
    ]
    for i in (3, 0, 1, 2):
        loads[i].start()
    loads[3].wait()
    dfirst = dot(dgate_ref[...], part(w_qkvg_ref, 3, DT), ((1,), (1,)))
    for i in range(3):
        piece = runs_ref[:, HS * i : HS * i + HS, :].reshape(DT, 256)
        loads[i].wait()
        dfirst += dot(piece.astype(F32).T.astype(BF16), part(w_qkvg_ref, i, DT), ((1,), (1,)))
    dfirst_ref[...] = dfirst
    scale = sigmoid(part(tu_ref, 0, DT))
    total_a = jnp.zeros((64, DT), F32)
    total_b = jnp.zeros((64, DT), F32)
    for s in range(4):
        r = slice(64 * s, 64 * s + 64)
        d = dfirst_ref[r, :]
        lines, inverse = normed(start_ref[r, :])
        grad = dmid_ref[r, :] + norm_back_rows(d * scale, lines, inverse)
        out_ref[s] = grad
        gpool_ref[r, :] = grad.astype(BF16)
        total_a += d * lines
        total_b += d
    ducat_ref[:, :DT] = (total_a * slope(scale)).astype(BF16)
    ducat_ref[:, DT : 2 * DT] = total_b.astype(BF16)
    gpool = gpool_ref[...]
    gpooled_ref[...] = dot(gpool, pool_ref[...], ((1,), (1,))) * 0.25
    dpool_ref[...] = dot(pooled_ref[...].reshape(256, DA), gpool, ((0,), (0,)))


def back(*args):
    sds = jax.ShapeDtypeStruct
    return kernel_call(
        back_kernel,
        [sds((4, 64, DT), F32), sds((256, DA), F32), sds((DA, DT), F32), sds((64, 2 * DT), BF16)],
        in_specs=[
            pl.BlockSpec(memory_space=pl.ANY) if i == 5 else fixed(*a.shape) for i, a in enumerate(args)
        ],
        scratch=[
            pltpu.VMEM((256, DT), F32), pltpu.VMEM((256, DT), BF16), pltpu.VMEM((DT, 4 * DT), BF16),
            pltpu.SemaphoreType.DMA((4,)),
        ],
        us=7,
        name="back",
    )(*args)


def atom_prep_kernel(
    u_ref, mid_ref, gate_ref, att_ref, w_out_ref, w_up_ref, w_down_ref,
    second_ref, hidden_ref, rate_ref, down_ref, gated_ref, branch_ref,
):
    scale_b, shift_b = sigmoid(part(u_ref, 3, DA)), part(u_ref, 4, DA)
    for s in range(4):
        second = (scale_b * normed(mid_ref[s])[0] + shift_b).astype(BF16)
        second_ref[s] = second
        up = dot(second, w_up_ref[...])
        e, f = up[:, :FA], up[:, FA:]
        half = sigmoid(e)
        rate_ref[s, :, :FA] = f * half * (1.0 + e * (1.0 - half))
        rate_ref[s, :, FA:] = e * half
        hidden = (e * half * f).astype(BF16)
        hidden_ref[s] = hidden
        down_ref[s] = dot(hidden, w_down_ref[...])
        gated = (gate_ref[s] * att_ref[s]).astype(BF16)
        gated_ref[s] = gated
        branch_ref[s] = dot(gated, w_out_ref[...])


def atom_prep(*args):
    sds = jax.ShapeDtypeStruct
    return kernel_call(
        atom_prep_kernel,
        [
            sds((4, 256, DA), BF16), sds((4, 256, FA), BF16), sds((4, 256, 2 * FA), F32), sds((4, 256, DA), F32),
            sds((4, 256, DA), BF16), sds((4, 256, DA), F32),
        ],
        us=6,
        name="atom_prep",
    )(*args)


def atom_back_kernel(
    gpooled_ref, u_ref, mid_ref, gate_ref, att_ref, q_ref, kv_ref, probs_ref, pair_ref, w_out_ref, w_up_ref,
    w_down_ref, second_ref, hidden_ref, rate_ref, down_ref, gated_ref, branch_ref,
    dq_ref, dgate_ref, dkv_ref, prev_ref, next_ref, dmid_ref, du_ref, dw_out_ref, dw_up_ref, dw_down_ref, dpair_ref,
    dy_ref, grads_ref, slopes_ref, sums_ref, gbranch_ref, dup_ref, gdown_ref,
):
    gate_a, scale_b, gate_b = sigmoid(part(u_ref, 2, DA)), sigmoid(part(u_ref, 3, DA)), sigmoid(part(u_ref, 5, DA))

    def atoms(s):
        for k in range(4):
            dy_ref[s, pl.ds(k, 64, stride=4), :] = gpooled_ref[s]
        dy = dy_ref[s]
        gdown = (dy * gate_b).astype(BF16)
        gdown_ref[s] = gdown
        dhidden = dot(gdown, w_down_ref[...], ((1,), (1,)))
        dup = (jnp.concatenate([dhidden, dhidden], axis=1) * rate_ref[s]).astype(BF16)
        dup_ref[s] = dup
        dsecond = dot(dup, w_up_ref[...], ((1,), (1,)))
        lines, inverse = normed(mid_ref[s])
        dmid = dy + norm_back_rows(dsecond * scale_b, lines, inverse)
        dmid_ref[s] = dmid
        gate, attended = gate_ref[s], att_ref[s]
        gbranch = (dmid * gate_a).astype(BF16)
        gbranch_ref[s] = gbranch
        sums = [dmid * branch_ref[s], dsecond * lines, dsecond, dy * down_ref[s]]
        for i in range(4):
            lanes = slice(DA * i, DA * i + DA)
            sums_ref[:, lanes] = sums[i] if s == 0 else sums_ref[:, lanes] + sums[i]
        dgated = dot(gbranch, w_out_ref[...], ((1,), (1,)))
        dgate_ref[s] = (dgated * attended * slope(gate)).astype(BF16)
        cots = head_rows(dgated * gate)
        rows = head_rows(q_ref[s].astype(F32))
        low = probs_ref[s]
        probs = low.astype(F32)

        def window(w):
            return slice(128 * w, 128 * w + 128), slice(32 * w, 32 * w + 128)

        def weights_of(w):
            at, span = window(w)
            return dot(cots[at], kv_ref[s, span, DA:], ((1,), (1,)))

        weighed = probs * by_window(weights_of)
        slopes = weighed - probs * jnp.sum(weighed, axis=1, keepdims=True)
        slopes_ref[...] = slopes if s == 0 else slopes_ref[...] + slopes
        slopes_low = slopes.astype(BF16)

        def query_of(w):
            at, span = window(w)
            return dot(slopes_low[at], kv_ref[s, span, :DA])

        dq_ref[s] = (rows_of_heads(by_window(query_of)) * 32 ** (-0.5)).astype(BF16)
        grads_ref[s] = jnp.zeros((SPAN, 2 * DA), F32)
        for w in range(8):
            at, span = window(w)
            grads_ref[s, span, :DA] += dot(slopes_low[at], rows[at], ((0,), (0,))) * 32 ** (-0.5)
            grads_ref[s, span, DA:] += dot(low[at], cots[at], ((0,), (0,)))
        dkv_ref[s] = grads_ref[s, RIM : RIM + 256, :]
        prev_ref[s] = grads_ref[s, :RIM, :].astype(BF16)
        next_ref[s] = grads_ref[s, RIM + 256 :, :].astype(BF16)

    for s in range(4):
        atoms(s)

    def rows_of(ref):
        return ref[...].reshape(1024, ref.shape[2])

    dw_out_ref[...] = dot(rows_of(gated_ref), rows_of(gbranch_ref), ((0,), (0,)))
    dw_up_ref[...] = dot(rows_of(second_ref), rows_of(dup_ref), ((0,), (0,)))
    dw_down_ref[...] = dot(rows_of(hidden_ref), rows_of(gdown_ref), ((0,), (0,)))
    du_ref[:, :DA] = sums_ref[:, :DA] * slope(gate_a)
    du_ref[:, DA : 2 * DA] = sums_ref[:, DA : 2 * DA] * slope(scale_b)
    du_ref[:, 2 * DA : 3 * DA] = sums_ref[:, 2 * DA : 3 * DA]
    du_ref[:, 3 * DA :] = sums_ref[:, 3 * DA :] * slope(gate_b)
    pairs = pair_norm(pair_ref[...].astype(F32))
    slopes = slopes_ref[...].reshape(8, 4, 32, 128)
    for h in range(4):
        own = slopes[:, h].reshape(256, 128)
        for c in range(16):
            dpair_ref[16 * h + c : 16 * h + c + 1, :] = jnp.sum(own * pairs[c], axis=0, keepdims=True)


def atom_back(*args):
    sds = jax.ShapeDtypeStruct
    return kernel_call(
        atom_back_kernel,
        [
            sds((4, 256, DA), BF16), sds((4, 256, DA), BF16), sds((4, 256, 2 * DA), F32),
            sds((4, RIM, 2 * DA), BF16), sds((4, RIM, 2 * DA), BF16), sds((4, 256, DA), F32),
            sds((256, 4 * DA), F32), sds((DA, DA), F32), sds((DA, 2 * FA), F32), sds((FA, DA), F32), sds((64, 128), F32),
        ],
        scratch=[
            pltpu.VMEM((4, 256, DA), F32), pltpu.VMEM((4, SPAN, 2 * DA), F32), pltpu.VMEM((1024, 128), F32),
            pltpu.VMEM((256, 4 * DA), F32), pltpu.VMEM((4, 256, DA), BF16), pltpu.VMEM((4, 256, 2 * FA), BF16),
            pltpu.VMEM((4, 256, DA), BF16),
        ],
        us=12,
        name="atom_back",
    )(*args)


def atom_end_kernel(
    core_ref, dq_ref, dgate_ref, dkv_ref, prev_ref, next_ref, dmid_ref, x_ref, first_ref, u_ref, du_ref, cond_low_ref,
    w_qkvg_ref, dw_out_ref, dw_up_ref, dw_down_ref, dpool_ref, single_ref, tdu_ref, heads_ref, misc_ref,
    out_ref, keep_ref, send_ref,
    dw_qkvg_ref, sums_ref, whole_ref,
):
    scale = sigmoid(part(u_ref, 0, DA))
    sums_ref[...] = jnp.zeros_like(sums_ref)
    dw_qkvg_ref[...] = jnp.zeros_like(dw_qkvg_ref)

    @pl.loop(0, 4)
    def _(s):
        whole_ref[...] = dkv_ref[s]
        whole_ref[:RIM, :] += prev_ref[s].astype(F32)
        whole_ref[256 - RIM :, :] += next_ref[s].astype(F32)
        grads = jnp.concatenate([dq_ref[s], whole_ref[...].astype(BF16), dgate_ref[s]], axis=1)
        dfirst = dot(grads, w_qkvg_ref[...], ((1,), (1,)))
        lines, inverse = normed(x_ref[s].astype(F32))
        out_ref[s] = dmid_ref[s] + norm_back_rows(dfirst * scale, lines, inverse)
        dw_qkvg_ref[...] += dot(first_ref[s], grads, ((0,), (0,)))
        sums_ref[:, :DA] += dfirst * lines
        sums_ref[:, DA:] += dfirst

    du = jnp.concatenate([sums_ref[:, :DA] * slope(scale), sums_ref[:, DA:], du_ref[...]], axis=1).astype(BF16)
    dw_cond = dot(cond_low_ref[...], du, ((0,), (0,)))
    down = dw_down_ref[...].reshape(16, 2, 8, DA)
    single = dot(single_ref[...], tdu_ref[...], ((0,), (0,))).reshape(16, 3, 8, 2 * DT)
    whole = jnp.concatenate(
        [
            dw_cond, dw_qkvg_ref[...], dw_out_ref[...], dw_up_ref[...], dpool_ref[...],
            down[:, 0].reshape(DA, DA), down[:, 1].reshape(DA, DA), misc_ref[...].astype(F32),
        ]
        + [single[:, i].reshape(DA, 2 * DT) for i in range(3)]
        + [jnp.zeros((DA, 512), F32)],
        axis=1,
    )
    even = core_ref[0] == 0

    def halves(rows, lanes):
        rows = rows.reshape(8, 2, 8, rows.shape[1])
        first, second = rows[:, 0].reshape(64, -1), rows[:, 1].reshape(64, -1)
        keep_ref[s, :, lanes] = jnp.where(even, first, second).astype(BF16)
        send_ref[s, :, lanes] = jnp.where(even, second, first).astype(BF16)

    for s in range(8):
        halves(whole[:, 1024 * s : 1024 * s + 1024], slice(0, 1024))
        own = heads_ref[s].astype(F32)
        halves(jnp.where(even, own, 0.0), slice(1024, 1280))
        halves(jnp.where(even, 0.0, own), slice(1280, 1536))


def atom_end(*args):
    sds = jax.ShapeDtypeStruct
    return kernel_call(
        atom_end_kernel,
        [sds((4, 256, DA), F32), sds((8, 64, 1536), BF16), sds((8, 64, 1536), BF16)],
        scratch=[pltpu.VMEM((DA, 4 * DA), F32), pltpu.VMEM((256, 2 * DA), F32), pltpu.VMEM((256, 2 * DA), F32)],
        scalars=1,
        us=6,
        name="atom_end",
    )(*args)


def split_kernel(samp_ref, wide_ref, *refs):
    out_refs, whole_ref = refs[:4], refs[4]
    whole_ref[:, : 10 * DT] = wide_ref[...]
    whole_ref[:, 10 * DT :] = jnp.zeros((48, 512), BF16)
    for k in range(8):
        lanes = pl.ds(pl.multiple_of((samp_ref[0] ^ k) * 1024, 1024), 1024)
        out_refs[k // 2][k % 2] = whole_ref[:, lanes]


def split(samp, wide):
    return kernel_call(
        split_kernel,
        [jax.ShapeDtypeStruct((2, 48, 1024), BF16)] * 4,
        scratch=[pltpu.VMEM((48, 64 * DA), BF16)],
        scalars=1,
        us=2,
        name="split",
    )(samp, wide)


def collect_kernel(wide_ref, wide_part_ref, packed_ref, out_ref, total_ref):
    step = pl.program_id(0)

    @pl.when(step == 0)
    def _():
        total_ref[...] = jnp.zeros_like(total_ref)

    rows = packed_ref[0, :, :1024].astype(F32)
    for i in range(1, 16):
        rows += packed_ref[i, :, :1024].astype(F32)
    total_ref[:8] += rows
    for h in range(16):
        at = slice(8 + 8 * (h // 4), 16 + 8 * (h // 4))
        lanes = slice(1024 + 256 * (h % 2), 1280 + 256 * (h % 2))
        total_ref[at, 256 * (h % 4) : 256 * (h % 4) + 256] += packed_ref[h // 2, :, lanes].astype(F32) + packed_ref[
            8 + h // 2, :, lanes
        ].astype(F32)

    @pl.when(step == 3)
    def _():
        wide = wide_ref[...].astype(F32) + wide_part_ref[...].astype(F32)
        whole = jnp.concatenate([wide, total_ref[...]], axis=0).astype(BF16)
        for i in range(8):
            out_ref[i] = whole


def collect(wide, wide_part, packed):
    return kernel_call(
        collect_kernel,
        [jax.ShapeDtypeStruct((8, 88, 1024), BF16)],
        grid=(4,),
        in_specs=[fixed(48, 1024), fixed(48, 1024), pl.BlockSpec((16, 8, 1536), lambda i: (i, 0, 0))],
        out_specs=[fixed(8, 88, 1024)],
        scratch=[pltpu.VMEM((40, 1024), F32)],
        us=4,
        name="collect",
    )(wide, wide_part, packed)[0]


def hand_out_kernel(
    parts_ref, a_cond_ref, a_qkvg_ref, a_out_ref, a_up_ref, a_down_ref, a_pair_ref, pool_ref, t_cond_ref, t_qkvg_ref,
    t_out_ref, t_up_ref, t_down_ref, t_pair_ref,
):
    def wide(first, last, rows=slice(0, 48)):
        pieces = []
        while first < last:
            s, at = divmod(first, 1024)
            end = min(last - 1024 * s, 1024)
            pieces.append(parts_ref[s, rows, at:end].astype(F32))
            first = 1024 * s + end
        return jnp.concatenate(pieces, axis=1)

    def atoms(first, last):
        return wide(first, last, slice(48, 64))[:8]

    t_up_ref[...] = wide(0, 4 * DT)
    t_out_ref[...] = wide(4 * DT, 5 * DT)
    t_qkvg_ref[:, 3 * DT :] = wide(5 * DT, 6 * DT)
    t_down_ref[:48, :] = wide(6 * DT, 7 * DT)
    t_down_ref[48:, :] = wide(7 * DT, 8 * DT)
    conds = wide(8 * DT, 10 * DT)
    t_cond_ref[:, 2 * DT : 4 * DT] = conds[:24]
    t_cond_ref[:, 4 * DT :] = conds[24:]
    for i in range(3):
        t_cond_ref[8 * i : 8 * i + 8, : 2 * DT] = atoms(3072 + 2 * DT * i, 3072 + 2 * DT * (i + 1))
    a_cond_ref[...] = atoms(0, 768)
    a_qkvg_ref[...] = atoms(768, 1280)
    a_out_ref[...] = atoms(1280, 1408)
    a_up_ref[...] = atoms(1408, 1920)
    pool_ref[...] = atoms(1920, 2688)
    a_down_ref[:8] = atoms(2688, 2816)
    a_down_ref[8:] = atoms(2816, 2944)
    misc = atoms(2944, 3072)
    t_pair_ref[...] = misc[0:1]
    a_pair_ref[...] = misc[1:2, :4]
    heads = []
    for h in range(16):
        at = 56 + 8 * (h // 4)
        lanes = slice(256 * (h % 4), 256 * (h % 4) + 3 * HS)
        base = at // 16 * 16
        rows = [parts_ref[s, base : min(base + 16, 88), lanes].astype(F32) for s in range(6)]
        heads.append(jnp.concatenate([r[at - base : at - base + 8] for r in rows], axis=0))
    for i in range(3):
        t_qkvg_ref[:, DT * i : DT * i + DT] = jnp.concatenate(
            [head[:, HS * i : HS * i + HS] for head in heads], axis=1
        )


def hand_out(parts):
    sds = jax.ShapeDtypeStruct
    shapes = [
        (8, 768), (8, 512), (8, 128), (8, 512), (16, 128), (1, 4), (8, 768), (24, 6 * DT), (48, 4 * DT), (48, DT),
        (48, 2 * FT), (96, DT), (1, 128),
    ]
    return kernel_call(
        hand_out_kernel,
        [sds(shape, F32) for shape in shapes],
        us=4,
        name="hand_out",
    )(parts)


def both_axes(x):
    return lax.all_to_all(x, ("samp", "seq"), 0, 0, tiled=True)


def along_seq(x):
    return lax.all_to_all(x, "seq", 0, 0, tiled=True)


ordered = lambda *x: lax.optimization_barrier(x)


def from_samp(part, k):
    return lax.ppermute(part, "samp", [(i, i ^ k) for i in range(8)])


def total(*parts):
    return sum(part.astype(F32) for part in parts).astype(BF16)


def body(
    atom_in,
    tok_in,
    atom_cond,
    single_cond,
    atom_pair,
    token_pair,
    atom_w_cond,
    atom_w_qkvg,
    atom_w_out,
    atom_w_up,
    atom_w_down,
    atom_w_pair,
    pool_weight,
    token_w_cond,
    token_w_qkvg,
    token_w_out,
    token_w_up,
    token_w_down,
    token_w_pair,
    cotangent,
):
    samp, seq = lax.axis_index("samp"), lax.axis_index("seq")
    up, down = [(i, i + 1) for i in range(15)], [(i + 1, i) for i in range(15)]
    rims = jnp.concatenate([atom_in, atom_cond[None]], axis=0)
    from_prev = lax.ppermute(rims[:, 256 - RIM :], "seq", up)
    from_next = lax.ppermute(rims[:, :RIM], "seq", down)
    samp = samp.astype(jnp.int32).reshape(1)
    normed_pair, token_bias = pair_bias(samp, token_pair, token_w_pair)
    token_bias = along_seq(token_bias).reshape(NT, 128)
    atom_in, token_bias = ordered(atom_in, token_bias)
    token_bias = lax.all_gather(token_bias, "samp", axis=0, axis_index_groups=[SAMP_RING])

    key_index = 256 * seq - RIM + 32 * jnp.arange(8)[:, None] + jnp.arange(128)[None, :]
    mask = jnp.where((key_index >= 0) & (key_index < 4096), 0.0, masked).astype(F32)
    (
        first, query, keyval, probs, gate, attended, middle, cond_low, cond_proj, pooled,
        start, tfirst, tgate, tcond_proj, single_low, runs,
    ) = front(
        atom_in, from_prev, from_next, atom_cond, atom_pair, mask, atom_w_pair.astype(F32), atom_w_cond,
        atom_w_qkvg, atom_w_out, atom_w_up, atom_w_down, pool_weight, tok_in, single_cond, token_w_cond, token_w_qkvg,
    )
    prep = atom_prep(cond_proj, middle, gate, attended, atom_w_out, atom_w_up, atom_w_down)
    beside = pair_beside(samp, token_pair)
    runs, beside, *prep = ordered(along_seq(runs), beside, *prep)
    qkv, tprobs, tattended = token_attention(runs, token_bias)
    tattended, sent = ordered(tattended, tfirst)
    lines = lax.all_gather(sent, "seq", axis=0, axis_index_groups=[RING])
    (
        token_out, cots, tdgate, tdmid, gated, gbranch, second, dup, hidden, gdown, tdu,
    ) = turn(
        along_seq(tattended), tgate, start, tcond_proj, cotangent, token_w_out, token_w_up, token_w_down
    )
    cots = along_seq(cots)
    wide = token_weights(gated, gbranch, tfirst, tdgate, second, dup, hidden, gdown, single_low, tdu)
    cots, wide = ordered(cots, wide)
    wide = lax.psum_scatter(wide, "seq", scatter_dimension=0, tiled=True, axis_index_groups=[RING])
    tgrads, *slopes = token_attention_back(samp, qkv, tprobs, cots)
    heads = head_weights(tgrads, lines)
    received = [from_samp(slopes[k], 2 * k) for k in range(1, 4)]
    tgrads, heads = ordered(along_seq(tgrads), heads)
    grad_tok, gpooled, dpool, tdu = back(
        tgrads, tdgate, tdmid, start, tcond_proj, token_w_qkvg, pool_weight, pooled
    )
    gpooled, *received = ordered(gpooled, *received)
    slopes = total(slopes[0], *received)
    slopes = along_seq(slopes.reshape(16, 128, 128))
    (
        dquery, dgate, dkeyval, to_prev, to_next, dmid, du, dw_out, dw_up, dw_down, dpair,
    ) = atom_back(
        gpooled.reshape(4, 64, DA), cond_proj, middle, gate, attended, query, keyval, probs, atom_pair,
        atom_w_out, atom_w_up, atom_w_down, *prep,
    )
    back_next = lax.ppermute(to_prev, "seq", down)
    back_prev = lax.ppermute(to_next, "seq", up)
    misc = pair_grad(slopes, normed_pair, beside, dpair)
    grad_atoms, packed, beside = atom_end(
        (seq % 2).astype(jnp.int32).reshape(1),
        dquery, dgate, dkeyval, back_prev, back_next, dmid, atom_in, first, cond_proj, du, cond_low,
        atom_w_qkvg, dw_out, dw_up, dw_down, dpool, single_low, tdu, heads, misc,
    )
    packed = total(packed, lax.ppermute(beside, "seq", [(i, i ^ 1) for i in range(16)])).reshape(64, 8, 1536)
    chips = [[core + 2 * i for i in range(64)] for core in range(2)]
    packed = lax.all_to_all(packed, ("samp", "seq"), 0, 0, tiled=True, axis_index_groups=chips)
    wide = split(samp, wide)
    wide = total(wide[0], *[from_samp(wide[k], 2 * k) for k in range(1, 4)])
    wide = wide[0], from_samp(wide[1], 1)
    parts = lax.all_to_all(collect(*wide, packed), "samp", 0, 0, tiled=True)
    return (token_out, grad_atoms, grad_tok, *hand_out(parts))


def solution(mesh):
    rows, both, whole = P("seq", None), P("samp", "seq", None), P()
    in_specs = (both, both, rows, rows, P(None, "seq", None), P(None, "seq", None)) + (whole,) * 13 + (both,)
    out_specs = (both,) * 3 + (rows,) * 13
    mapped = jax.shard_map(body, mesh=mesh, in_specs=in_specs, out_specs=out_specs, check_vma=False)

    def run(*args):
        with jax.sharding.use_abstract_mesh(mesh.abstract_mesh):
            return mapped(*args)

    return run
```

```python
import jax
import jax.numpy as jnp
from jax import lax
from jax.experimental import pallas as pl
from jax.experimental.pallas import tpu as pltpu
from jax.sharding import PartitionSpec as P

eps = 1e-05
masked = -1000000000.0

MIB = 1 << 20
LIMIT = 44
F32, BF16 = jnp.float32, jnp.bfloat16


def kernel_call(
    kernel, out_shape, grid=(1,), in_specs=None, out_specs=None, scratch=(), scalars=0, arrived=(), us=1, name=None
):
    def run(*args):
        ins = list(in_specs or [fixed(*a.shape) for a in args[scalars:]])
        outs = list(out_specs or [fixed(*o.shape) for o in out_shape])
        args = list(args)
        for i in range(len(ins)):
            if i not in arrived and ins[i].memory_space in (None, pl.ANY):
                args[scalars + i] = pltpu.with_memory_space_constraint(args[scalars + i], pltpu.HBM)
        return pl.pallas_call(
            kernel,
            out_shape=[pltpu.HBM(o.shape, o.dtype) for o in out_shape],
            grid_spec=pltpu.PrefetchScalarGridSpec(
                num_scalar_prefetch=scalars, grid=grid, in_specs=ins, out_specs=outs, scratch_shapes=list(scratch)
            ),
            compiler_params=pltpu.CompilerParams(vmem_limit_bytes=LIMIT * MIB),
            cost_estimate=pl.CostEstimate(flops=us << 30, bytes_accessed=us << 20, transcendentals=0),
            name=name,
        )(*args)

    return run


def fixed(*shape):
    return pl.BlockSpec(shape, lambda *_: (0,) * len(shape), pipeline_mode=pl.Buffered(1))


def dot(left, right, over=((1,), (0,))):
    return lax.dot_general(left, right, (over, ((), ())), preferred_element_type=F32)


def swap_halves(first, second):
    low = lax.broadcasted_iota(jnp.int32, first.shape, 1) < 64
    half = first.shape[1] // 2
    return (
        jnp.where(low, first, pltpu.roll(second, half, 1)),
        jnp.where(low, pltpu.roll(first, half, 1), second),
    )


def runs_to_tokens(runs_ref, tokens_ref):
    for pair in range(runs_ref.shape[0] // 2):
        for duo in range(2):
            lanes = slice(128 * duo, 128 * duo + 128)
            made = swap_halves(
                runs_ref[2 * pair, :, lanes].astype(F32), runs_ref[2 * pair + 1, :, lanes].astype(F32)
            )
            for k in range(2):
                tokens_ref[2 * duo + k, :, 128 * pair : 128 * pair + 128] = made[k].astype(
                    tokens_ref.dtype
                )


def tokens_to_runs(tokens_ref, runs_ref):
    for pair in range(runs_ref.shape[0] // 2):
        lanes = slice(128 * pair, 128 * pair + 128)
        for duo in range(2):
            made = swap_halves(tokens_ref[2 * duo, :, lanes], tokens_ref[2 * duo + 1, :, lanes])
            for k in range(2):
                runs_ref[2 * pair + k, :, 128 * duo : 128 * duo + 128] = made[k].astype(runs_ref.dtype)


HS = 48
NT = 1024
QB = 256
SAMP_RING = [0, 2, 4, 6, 7, 5, 3, 1]


def attention_kernel(runs_ref, bias_ref, qkv_ref, probs_ref, out_ref, heads_ref):
    sample = pl.program_id(0)

    @pl.when(sample == 0)
    def _():
        runs_to_tokens(runs_ref, qkv_ref)

    keys = qkv_ref[sample, HS : 2 * HS, :]
    values = qkv_ref[sample, 2 * HS :, :]

    def scores_of(block):
        rows = slice(block * QB, block * QB + QB)
        made = dot(qkv_ref[sample, :HS, rows], keys, ((0,), (0,))) * HS ** (-0.5)
        return made + jnp.concatenate([bias_ref[SAMP_RING.index(i), rows, :] for i in range(8)], axis=1).astype(F32)

    count = NT // QB
    ahead = scores_of(0)
    for block in range(count):
        rows = slice(block * QB, block * QB + QB)
        scores = ahead
        if block + 1 < count:
            ahead = scores_of(block + 1)
        exponent = jnp.exp(scores - jnp.max(scores, axis=1, keepdims=True))
        probs = (exponent * (1.0 / jnp.sum(exponent, axis=1, keepdims=True))).astype(BF16)
        probs_ref[0, rows, :] = probs
        heads_ref[sample, :, rows] = dot(probs, values, ((1,), (1,))).T

    @pl.when(sample == 3)
    def _():
        tokens_to_runs(heads_ref, out_ref)


def token_attention(runs, bias):
    return kernel_call(
        attention_kernel,
        [
            jax.ShapeDtypeStruct((4, 3 * HS, NT), BF16),
            jax.ShapeDtypeStruct((4, NT, NT), BF16),
            jax.ShapeDtypeStruct((16, HS, 256), BF16),
        ],
        grid=(4,),
        in_specs=[fixed(16, 3 * HS, 256)] + [fixed(8, NT, 128)],
        out_specs=[
            fixed(4, 3 * HS, NT), pl.BlockSpec((1, NT, NT), lambda s: (s, 0, 0)), fixed(16, HS, 256),
        ],
        scratch=[pltpu.VMEM((4, HS, NT), F32)],
        us=13,
        arrived=(0,),
        name="token_attention",
    )(runs, bias)


def attention_back_kernel(samp_ref, qkv_ref, probs_ref, cot_ref, out_ref, *refs):
    pair_refs, (cots_ref, grads_ref, total_ref) = refs[:4], refs[4:]
    sample = pl.program_id(0)

    @pl.when(sample == 0)
    def _():
        runs_to_tokens(cot_ref, cots_ref)
        total_ref[...] = jnp.zeros_like(total_ref)

    keys = qkv_ref[sample, HS : 2 * HS, :]
    values = qkv_ref[sample, 2 * HS :, :]

    def weights_of(block):
        return dot(cots_ref[sample, :, block * QB : block * QB + QB], values, ((0,), (0,)))

    key_grad, value_grad = 0.0, 0.0
    count = NT // QB
    ahead = weights_of(0)
    for block in range(count):
        rows = slice(block * QB, block * QB + QB)
        now = ahead
        if block + 1 < count:
            ahead = weights_of(block + 1)
        low = probs_ref[0, rows, :]
        probs = low.astype(F32)
        weighed = probs * now
        slopes = weighed - probs * jnp.sum(weighed, axis=1, keepdims=True)
        slopes_low = slopes.astype(BF16)
        total_ref[rows, :] += slopes
        grads_ref[sample, :HS, rows] = dot(keys, slopes_low, ((1,), (1,))) * HS ** (-0.5)
        key_grad += dot(qkv_ref[sample, :HS, rows], slopes_low)
        value_grad += dot(cots_ref[sample, :, rows], low)
    grads_ref[sample, HS : 2 * HS, :] = key_grad * HS ** (-0.5)
    grads_ref[sample, 2 * HS :, :] = value_grad

    @pl.when(sample == 3)
    def _():
        tokens_to_runs(grads_ref, out_ref)
        for k in range(4):
            lanes = pl.ds(pl.multiple_of(((samp_ref[0] // 2) ^ k) * 256, 256), 256)
            pair_refs[k][...] = total_ref[:, lanes].astype(BF16).reshape(16, 64, 256)


def token_attention_back(samp, qkv, probs, cots):
    return kernel_call(
        attention_back_kernel,
        [jax.ShapeDtypeStruct((16, 3 * HS, 256), BF16)] + [jax.ShapeDtypeStruct((16, 64, 256), BF16)] * 4,
        grid=(4,),
        in_specs=[fixed(4, 3 * HS, NT), pl.BlockSpec((1, NT, NT), lambda s, _: (s, 0, 0)), fixed(16, HS, 256)],
        out_specs=[fixed(16, 3 * HS, 256)] + [fixed(16, 64, 256)] * 4,
        scratch=[
            pltpu.VMEM((4, HS, NT), BF16),
            pltpu.VMEM((4, 3 * HS, NT), F32),
            pltpu.VMEM((NT, NT), F32),
        ],
        scalars=1,
        us=14,
        arrived=(2,),
        name="token_attention_back",
    )(samp, qkv, probs, cots)


def normed_rows(pair_ref):
    pair = pair_ref[...].astype(F32)
    centred = pair - jnp.mean(pair, axis=0, keepdims=True)
    inverse = lax.rsqrt(jnp.mean(centred * centred, axis=0, keepdims=True) + eps)
    return jnp.swapaxes((centred * inverse).astype(BF16), 0, 1)


def pair_kernel(samp_ref, pair_ref, weight_ref, bias_ref):
    low = normed_rows(pair_ref)
    weight = weight_ref[...]
    bias = jnp.stack([dot(weight, low[i]) for i in range(low.shape[0])], axis=0)
    bias_ref[...] = jnp.swapaxes(bias, 0, 1).astype(BF16)


def pair_bias(samp, pair, weight):
    return kernel_call(
        pair_kernel,
        [jax.ShapeDtypeStruct((16, 64, 128), BF16)],
        grid=(2,),
        in_specs=[pl.BlockSpec((128, 32, 128), lambda i, samp: (0, i, samp[0])), fixed(16, 128)],
        out_specs=[pl.BlockSpec((16, 32, 128), lambda i, _: (0, i, 0))],
        scalars=1,
        us=4,
        name="pair_bias",
    )(samp, pair, weight)[0]


def pair_norm_kernel(samp_ref, pair_ref, normed_ref):
    normed_ref[...] = normed_rows(pair_ref)


def pair_normed(samp, pair):
    return kernel_call(
        pair_norm_kernel,
        [jax.ShapeDtypeStruct((64, 128, 256), BF16)],
        grid=(4,),
        in_specs=[pl.BlockSpec((128, 16, 256), lambda i, samp: (0, i, samp[0] // 2))],
        out_specs=[pl.BlockSpec((16, 128, 256), lambda i, _: (i, 0, 0))],
        scalars=1,
        us=6,
        name="pair_normed",
    )(samp, pair)[0]


def pair_back_kernel(slopes_ref, normed_ref, atoms_ref, out_ref, grad_ref):
    step = pl.program_id(0)
    slopes = jnp.swapaxes(slopes_ref[...], 0, 1)
    made = dot(slopes[0], normed_ref[0], ((1,), (1,)))
    for i in range(1, slopes.shape[0]):
        made += dot(slopes[i], normed_ref[i], ((1,), (1,)))

    @pl.when(step == 0)
    def _():
        grad_ref[...] = made

    @pl.when(step > 0)
    def _():
        grad_ref[...] += made

    @pl.when(step == 3)
    def _():
        atoms = jnp.sum(atoms_ref[...], axis=1, keepdims=True)
        lane = lax.broadcasted_iota(jnp.int32, (16, 128), 1)
        rows = jnp.where(lane == 0, atoms[:16], 0.0)
        for h in range(1, 4):
            rows += jnp.where(lane == h, atoms[16 * h : 16 * h + 16], 0.0)
        line = lax.broadcasted_iota(jnp.int32, (16, 8, 128), 1)
        both = jnp.where(line == 0, grad_ref[...][:, None, :], 0.0) + jnp.where(line == 1, rows[:, None, :], 0.0)
        out_ref[...] = both.reshape(128, 128).astype(BF16)


def pair_grad(slopes, normed, atoms):
    return kernel_call(
        pair_back_kernel,
        [jax.ShapeDtypeStruct((128, 128), BF16)],
        grid=(4,),
        in_specs=[
            pl.BlockSpec((16, 16, 256), lambda i: (0, i, 0)),
            pl.BlockSpec((16, 128, 256), lambda i: (i, 0, 0)),
            fixed(64, 128),
        ],
        out_specs=[fixed(128, 128)],
        scratch=[pltpu.VMEM((16, 128), F32)],
        arrived=(0,),
        us=6,
        name="pair_grad",
    )(slopes, normed, atoms)[0]


DA, DT, FT, FA = 128, 768, 1536, 256
RIM = 48
RING = [0, 1, 4, 5, 8, 9, 12, 13, 14, 15, 10, 11, 6, 7, 2, 3]
SPAN = 256 + 2 * RIM


def normed(x):
    centred = x - jnp.mean(x, axis=-1, keepdims=True)
    inverse = lax.rsqrt(jnp.mean(centred * centred, axis=-1, keepdims=True) + eps)
    return centred * inverse, inverse


def sigmoid(x):
    return 1.0 / (1.0 + jnp.exp(-x))


def own_head():
    shape = (1, 4, 32, 128)
    return lax.broadcasted_iota(jnp.int32, shape, 3) // 32 == lax.broadcasted_iota(jnp.int32, shape, 1)


def head_rows(rows):
    return jnp.where(own_head(), rows.reshape(8, 1, 32, 128), 0.0).reshape(1024, 128).astype(BF16)


def rows_of_heads(full):
    return jnp.sum(jnp.where(own_head(), full.reshape(8, 4, 32, 128), 0.0), axis=1).reshape(256, 128)


def by_window(made):
    return jnp.concatenate([made(w) for w in range(8)], axis=0)


def pair_norm(pair):
    centred = pair - jnp.mean(pair, axis=0, keepdims=True)
    inverse = lax.rsqrt(jnp.mean(centred * centred, axis=0, keepdims=True) + eps)
    return (centred * inverse).astype(BF16).astype(F32)


def part(ref, i, width, rows=slice(None)):
    return ref[rows, i * width : (i + 1) * width]


def front_kernel(
    x_ref, prev_ref, next_ref, cond_ref, pair_ref, mask_ref, w_pair_ref, w_cond_ref, w_qkvg_ref, w_out_ref,
    w_up_ref, w_down_ref, pool_ref, tok_ref, single_ref, tw_cond_hbm, tw_qkvg_hbm,
    first_ref, q_ref, kv_ref, probs_ref, gate_ref, att_ref, mid_ref, cond_low_ref, u_ref, pooled_ref,
    start_ref, tfirst_ref, tgate_ref, tu_ref, single_low_ref, runs_ref,
    bias_ref, y_ref, uh_ref, tw_cond_ref, tw_qkvg_ref, sems,
):
    loads = [
        pltpu.make_async_copy(tw_cond_hbm, tw_cond_ref, sems.at[0]),
        pltpu.make_async_copy(tw_qkvg_hbm, tw_qkvg_ref, sems.at[1]),
    ]
    for load in loads:
        load.start()
    cond = jnp.concatenate([prev_ref[4], cond_ref[...], next_ref[4]], axis=0).astype(F32)
    cond_low = normed(cond)[0].astype(BF16)
    cond_low_ref[...] = cond_low[RIM : RIM + 256]
    u_ref[...] = dot(cond_low[RIM : RIM + 256], w_cond_ref[...])
    uh_ref[...] = dot(cond_low, w_cond_ref[:, : 2 * DA])
    pairs = pair_norm(pair_ref[...].astype(F32))
    for h in range(4):
        bias = pairs[0] * w_pair_ref[0, h]
        for c in range(1, 16):
            bias += pairs[c] * w_pair_ref[c, h]
        for w in range(8):
            at = 128 * w + 32 * h
            bias_ref[at : at + 32, :] = bias[32 * w : 32 * w + 32] + mask_ref[w : w + 1, :]

    scale_a, shift_a = sigmoid(part(uh_ref, 0, DA)), part(uh_ref, 1, DA)
    gate_a, scale_b, shift_b, gate_b = (
        sigmoid(part(u_ref, 2, DA)), sigmoid(part(u_ref, 3, DA)), part(u_ref, 4, DA), sigmoid(part(u_ref, 5, DA)),
    )

    def atoms(s):
        x = jnp.concatenate([prev_ref[s], x_ref[s], next_ref[s]], axis=0).astype(F32)
        first = (scale_a * normed(x)[0] + shift_a).astype(BF16)
        projected = dot(first, w_qkvg_ref[...])
        own = projected[RIM : RIM + 256]
        first_ref[s] = first[RIM : RIM + 256]
        query = own[:, :DA].astype(BF16)
        q_ref[s] = query
        keys = projected[:, DA : 2 * DA].astype(BF16)
        values = projected[:, 2 * DA : 3 * DA].astype(BF16)
        kv_ref[s, :, :DA] = keys
        kv_ref[s, :, DA:] = values
        gate = sigmoid(own[:, 3 * DA :])
        gate_ref[s] = gate
        rows = head_rows(query.astype(F32))
        scores = by_window(lambda w: dot(rows[128 * w : 128 * w + 128], keys[32 * w : 32 * w + 128], ((1,), (1,))))
        scores = scores * 32 ** (-0.5) + bias_ref[...]
        exponent = jnp.exp(scores - jnp.max(scores, axis=1, keepdims=True))
        probs = (exponent * (1.0 / jnp.sum(exponent, axis=1, keepdims=True))).astype(BF16)
        probs_ref[s] = probs
        attended = rows_of_heads(
            by_window(lambda w: dot(probs[128 * w : 128 * w + 128], values[32 * w : 32 * w + 128]))
        )
        att_ref[s] = attended
        branch = dot((gate * attended).astype(BF16), w_out_ref[...])
        middle = x[RIM : RIM + 256] + gate_a * branch
        mid_ref[s] = middle
        second = (scale_b * normed(middle)[0] + shift_b).astype(BF16)
        up = dot(second, w_up_ref[...])
        hidden = (up[:, :FA] * sigmoid(up[:, :FA]) * up[:, FA:]).astype(BF16)
        y_ref[s] = middle + gate_b * dot(hidden, w_down_ref[...])
        pooled = y_ref[s, pl.ds(0, 64, stride=4), :]
        for k in range(1, 4):
            pooled += y_ref[s, pl.ds(k, 64, stride=4), :]
        pooled_ref[s] = (pooled * 0.25).astype(BF16)

    for s in range(4):
        atoms(s)

    for load in loads:
        load.wait()
    single_low = normed(single_ref[...].astype(F32))[0].astype(BF16)
    single_low_ref[...] = single_low
    for i in range(6):
        tu_ref[:, DT * i : DT * i + DT] = dot(single_low, tw_cond_ref[:, DT * i : DT * i + DT])
    pooled = pooled_ref[...].reshape(256, DA)
    start = tok_ref[...].reshape(256, DT).astype(F32) + dot(pooled, pool_ref[...])
    start_ref[...] = start
    lines = normed(start)[0]
    scale, shift = sigmoid(part(tu_ref, 0, DT)), part(tu_ref, 1, DT)
    for s in range(4):
        tfirst_ref[64 * s : 64 * s + 64, :] = (scale * lines[64 * s : 64 * s + 64] + shift).astype(BF16)
    first = tfirst_ref[...]
    for i in range(3):
        turned = dot(first, part(tw_qkvg_ref, i, DT)).T.astype(BF16)
        for h in range(16):
            runs_ref[h, HS * i : HS * i + HS, :] = turned[HS * h : HS * h + HS]
    tgate_ref[...] = sigmoid(dot(first, part(tw_qkvg_ref, 3, DT)))


def front(*args):
    sds = jax.ShapeDtypeStruct
    specs = [fixed(*a.shape) for a in args]
    specs[6] = pl.BlockSpec(memory_space=pltpu.SMEM)
    specs[15] = specs[16] = pl.BlockSpec(memory_space=pl.ANY)
    return kernel_call(
        front_kernel,
        [
            sds((4, 256, DA), BF16), sds((4, 256, DA), BF16), sds((4, SPAN, 2 * DA), BF16),
            sds((4, 1024, 128), BF16), sds((4, 256, DA), F32), sds((4, 256, DA), F32),
            sds((4, 256, DA), F32), sds((256, DA), BF16), sds((256, 6 * DA), F32), sds((4, 64, DA), BF16),
            sds((256, DT), F32), sds((256, DT), BF16), sds((256, DT), F32), sds((64, 6 * DT), F32),
            sds((64, 384), BF16), sds((16, 3 * HS, 256), BF16),
        ],
        in_specs=specs,
        scratch=[
            pltpu.VMEM((1024, 128), F32), pltpu.VMEM((4, 256, DA), F32), pltpu.VMEM((SPAN, 2 * DA), F32),
            pltpu.VMEM((384, 6 * DT), BF16), pltpu.VMEM((DT, 4 * DT), BF16), pltpu.SemaphoreType.DMA((2,)),
        ],
        us=24,
        arrived=(1, 2),
        name="front",
    )(*args)


def slope(squashed):
    return squashed * (1.0 - squashed)


def norm_back_rows(gradient, lines, inverse):
    return inverse * (
        gradient
        - jnp.mean(gradient, axis=-1, keepdims=True)
        - lines * jnp.mean(gradient * lines, axis=-1, keepdims=True)
    )


def turn_kernel(
    runs_ref, tgate_ref, start_ref, tu_ref, cot_ref, w_out_hbm, w_up_hbm, w_down_hbm,
    out_ref, cots_ref, dgate_ref, dmid_ref, a_ref, gbranch_ref, second_ref, dup_ref, hidden_ref, gdown_ref,
    du_ref,
    up_ref, mid_ref, branch_ref, down_ref, w_out_ref, w_up_ref, w_down_ref, sems,
):
    loads = [
        pltpu.make_async_copy(w_out_hbm, w_out_ref, sems.at[0]),
        pltpu.make_async_copy(w_up_hbm, w_up_ref, sems.at[1]),
        pltpu.make_async_copy(w_down_hbm, w_down_ref, sems.at[2]),
    ]
    for load in loads:
        load.start()
    attended = runs_ref[...].reshape(DT, 256).astype(F32).T
    gate = tgate_ref[...]
    gated = (gate * attended).astype(BF16)
    a_ref[...] = gated
    loads[0].wait()
    branch_ref[...] = dot(gated, w_out_ref[...])
    gate_a, scale_b, shift_b, gate_b = (
        sigmoid(part(tu_ref, 2, DT)), sigmoid(part(tu_ref, 3, DT)), part(tu_ref, 4, DT), sigmoid(part(tu_ref, 5, DT)),
    )
    runs = [slice(64 * s, 64 * s + 64) for s in range(4)]
    for r in runs:
        middle = start_ref[r, :] + gate_a * branch_ref[r, :]
        mid_ref[r, :] = middle
        second_ref[r, :] = (scale_b * normed(middle)[0] + shift_b).astype(BF16)
    second = second_ref[...]
    loads[1].wait()
    loads[2].wait()
    cut = 512
    for j in range(FT // cut):
        e = dot(second, w_up_ref[:, cut * j : cut * j + cut])
        f = dot(second, w_up_ref[:, FT + cut * j : FT + cut * j + cut])
        up_ref[:, cut * j : cut * j + cut] = e
        up_ref[:, FT + cut * j : FT + cut * j + cut] = f
        hidden = (e * sigmoid(e) * f).astype(BF16)
        hidden_ref[:, cut * j : cut * j + cut] = hidden
        piece = dot(hidden, w_down_ref[cut * j : cut * j + cut, :])
        if j == 0:
            down_ref[...] = piece
        else:
            down_ref[...] += piece
    total = jnp.zeros((64, DT), F32)
    for s, r in enumerate(runs):
        cot = cot_ref[s].astype(F32)
        out_ref[s] = (mid_ref[r, :] + gate_b * down_ref[r, :]).astype(BF16)
        gdown_ref[r, :] = (cot * gate_b).astype(BF16)
        total += cot * down_ref[r, :]
    du_ref[:, 3 * DT :] = (total * slope(gate_b)).astype(BF16)
    gdown = gdown_ref[...]
    dsecond = jnp.zeros((256, DT), F32)
    for j in range(FT // cut):
        dhidden = dot(gdown, w_down_ref[cut * j : cut * j + cut, :], ((1,), (1,)))
        e = up_ref[:, cut * j : cut * j + cut]
        f = up_ref[:, FT + cut * j : FT + cut * j + cut]
        half = sigmoid(e)
        de = (dhidden * f * half * (1.0 + e * (1.0 - half))).astype(BF16)
        df = (dhidden * e * half).astype(BF16)
        dup_ref[:, cut * j : cut * j + cut] = de
        dup_ref[:, FT + cut * j : FT + cut * j + cut] = df
        piece = dot(de, w_up_ref[:, cut * j : cut * j + cut], ((1,), (1,)))
        piece += dot(df, w_up_ref[:, FT + cut * j : FT + cut * j + cut], ((1,), (1,)))
        dsecond += piece
    down_ref[...] = dsecond
    total_a = jnp.zeros((64, DT), F32)
    total_b = jnp.zeros((64, DT), F32)
    total_c = jnp.zeros((64, DT), F32)
    for s, r in enumerate(runs):
        d = down_ref[r, :]
        lines, inverse = normed(mid_ref[r, :])
        dmid = cot_ref[s].astype(F32) + norm_back_rows(d * scale_b, lines, inverse)
        dmid_ref[r, :] = dmid
        gbranch_ref[r, :] = (dmid * gate_a).astype(BF16)
        total_a += dmid * branch_ref[r, :]
        total_b += d * lines
        total_c += d
    du_ref[:, :DT] = (total_a * slope(gate_a)).astype(BF16)
    du_ref[:, DT : 2 * DT] = (total_b * slope(scale_b)).astype(BF16)
    du_ref[:, 2 * DT : 3 * DT] = total_c.astype(BF16)
    dgated = dot(gbranch_ref[...], w_out_ref[...], ((1,), (1,)))
    dgate_ref[...] = (dgated * attended * slope(gate)).astype(BF16)
    cots_ref[...] = (dgated * gate).T.astype(BF16).reshape(16, HS, 256)


def turn(*args):
    sds = jax.ShapeDtypeStruct
    rows = lambda n, t=BF16: sds((256, n), t)
    return kernel_call(
        turn_kernel,
        [
            sds((4, 64, DT), BF16), sds((16, HS, 256), BF16), rows(DT), rows(DT, F32), rows(DT), rows(DT),
            rows(DT), rows(2 * FT), rows(FT), rows(DT), sds((64, 4 * DT), BF16),
        ],
        in_specs=[fixed(*a.shape) for a in args[:5]] + [pl.BlockSpec(memory_space=pl.ANY)] * 3,
        scratch=[pltpu.VMEM((256, 2 * FT), F32)]
        + [pltpu.VMEM((256, DT), F32)] * 3
        + [pltpu.VMEM(a.shape, BF16) for a in args[5:]]
        + [pltpu.SemaphoreType.DMA((3,))],
        us=12,
        arrived=(0,),
        name="turn",
    )(*args)


def weights_kernel(
    a_ref, gbranch_ref, first_ref, dgate_ref, second_ref, dup_ref, hidden_ref, gdown_ref, single_ref, du_ref, out_ref,
):
    step = pl.program_id(0)

    def write(rows, lanes=slice(None)):
        for at, run in enumerate(RING):
            out_ref[48 * at : 48 * at + 48, lanes] = rows[run]

    def square(left, right):
        return dot(left[...], right[...], ((0,), (0,))).astype(BF16)

    @pl.when(step < 2)
    def _():
        write(square(second_ref, dup_ref).reshape(16, 48, FT))

    @pl.when(step == 2)
    def _():
        write(square(a_ref, gbranch_ref).reshape(16, 48, DT), slice(0, DT))
        write(square(first_ref, dgate_ref).reshape(16, 48, DT), slice(DT, FT))

    @pl.when(step == 3)
    def _():
        made = square(hidden_ref, gdown_ref).reshape(16, 2, 48, DT)
        write(made[:, 0], slice(0, DT))
        write(made[:, 1], slice(DT, FT))

    @pl.when(step == 4)
    def _():
        made = dot(single_ref[...], du_ref[...], ((0,), (0,))).reshape(16, 24, 4 * DT)
        write(jnp.concatenate([made[:, :, :FT], made[:, :, FT:]], axis=1).astype(BF16))


def token_weights(*args):
    specs = [fixed(*a.shape) for a in args]
    specs[5] = pl.BlockSpec((256, FT), lambda i: (0, jnp.minimum(i, 1)))
    return kernel_call(
        weights_kernel,
        [jax.ShapeDtypeStruct((DT, 10 * DT), BF16)],
        grid=(5,),
        in_specs=specs,
        out_specs=[pl.BlockSpec((DT, FT), lambda i: (0, i))],
        us=12,
        name="token_weights",
    )(*args)[0]


def head_weights_kernel(grads_ref, lines_ref, out_ref, total_ref):
    step = pl.program_id(0)

    @pl.when(step == 0)
    def _():
        total_ref[...] = jnp.zeros_like(total_ref)

    for k in range(2):
        total_ref[...] += dot(grads_ref[k], lines_ref[k])

    @pl.when(step == 7)
    def _():
        out_ref[:, :, : 3 * HS] = total_ref[...].T.astype(BF16).reshape(16, 48, 3 * HS)
        out_ref[:, :, 3 * HS :] = jnp.zeros((16, 48, 256 - 3 * HS), BF16)


def head_weights(grads, lines):
    return kernel_call(
        head_weights_kernel,
        [jax.ShapeDtypeStruct((16, 48, 256), BF16)],
        grid=(8,),
        in_specs=[
            pl.BlockSpec((2, 3 * HS, 256), lambda i: (jnp.where(i < 4, 2 * i, 15 - 2 * i), 0, 0)),
            pl.BlockSpec((2, 256, DT), lambda i: (i, 0, 0)),
        ],
        out_specs=[fixed(16, 48, 256)],
        scratch=[pltpu.VMEM((3 * HS, DT), F32)],
        us=6,
        name="head_weights",
    )(grads, lines)[0]


def back_kernel(
    runs_ref, dgate_ref, dmid_ref, start_ref, tu_ref, w_qkvg_hbm, pool_ref, pooled_ref,
    out_ref, gpooled_ref, dpool_ref, ducat_ref,
    dfirst_ref, gpool_ref, w_qkvg_ref, sems,
):
    loads = [
        pltpu.make_async_copy(
            w_qkvg_hbm.at[:, DT * i : DT * i + DT], w_qkvg_ref.at[:, DT * i : DT * i + DT], sems.at[i]
        )
        for i in range(4)
    ]
    for i in (3, 0, 1, 2):
        loads[i].start()
    loads[3].wait()
    dfirst = dot(dgate_ref[...], part(w_qkvg_ref, 3, DT), ((1,), (1,)))
    for i in range(3):
        piece = runs_ref[:, HS * i : HS * i + HS, :].reshape(DT, 256)
        loads[i].wait()
        dfirst += dot(piece.astype(F32).T.astype(BF16), part(w_qkvg_ref, i, DT), ((1,), (1,)))
    dfirst_ref[...] = dfirst
    scale = sigmoid(part(tu_ref, 0, DT))
    total_a = jnp.zeros((64, DT), F32)
    total_b = jnp.zeros((64, DT), F32)
    for s in range(4):
        r = slice(64 * s, 64 * s + 64)
        d = dfirst_ref[r, :]
        lines, inverse = normed(start_ref[r, :])
        grad = dmid_ref[r, :] + norm_back_rows(d * scale, lines, inverse)
        out_ref[s] = grad
        gpool_ref[r, :] = grad.astype(BF16)
        total_a += d * lines
        total_b += d
    ducat_ref[:, :DT] = (total_a * slope(scale)).astype(BF16)
    ducat_ref[:, DT : 2 * DT] = total_b.astype(BF16)
    gpool = gpool_ref[...]
    gpooled_ref[...] = dot(gpool, pool_ref[...], ((1,), (1,))) * 0.25
    dpool_ref[...] = dot(pooled_ref[...].reshape(256, DA), gpool, ((0,), (0,)))


def back(*args):
    sds = jax.ShapeDtypeStruct
    return kernel_call(
        back_kernel,
        [sds((4, 64, DT), F32), sds((256, DA), F32), sds((DA, DT), F32), sds((64, 2 * DT), BF16)],
        in_specs=[
            pl.BlockSpec(memory_space=pl.ANY) if i == 5 else fixed(64, 2 * DT) if i == 4 else fixed(*a.shape)
            for i, a in enumerate(args)
        ],
        scratch=[
            pltpu.VMEM((256, DT), F32), pltpu.VMEM((256, DT), BF16), pltpu.VMEM((DT, 4 * DT), BF16),
            pltpu.SemaphoreType.DMA((4,)),
        ],
        us=7,
        arrived=(0,),
        name="back",
    )(*args)


def atom_prep_kernel(
    u_ref, mid_ref, gate_ref, att_ref, w_out_ref, w_up_ref, w_down_ref,
    second_ref, hidden_ref, rate_ref, down_ref, gated_ref, branch_ref,
):
    scale_b, shift_b = sigmoid(part(u_ref, 3, DA)), part(u_ref, 4, DA)
    for s in range(4):
        second = (scale_b * normed(mid_ref[s])[0] + shift_b).astype(BF16)
        second_ref[s] = second
        up = dot(second, w_up_ref[...])
        e, f = up[:, :FA], up[:, FA:]
        half = sigmoid(e)
        rate_ref[s, :, :FA] = (f * half * (1.0 + e * (1.0 - half))).astype(BF16)
        rate_ref[s, :, FA:] = (e * half).astype(BF16)
        hidden = (e * half * f).astype(BF16)
        hidden_ref[s] = hidden
        down_ref[s] = dot(hidden, w_down_ref[...])
        gated = (gate_ref[s] * att_ref[s]).astype(BF16)
        gated_ref[s] = gated
        branch_ref[s] = dot(gated, w_out_ref[...])


def atom_prep(*args):
    sds = jax.ShapeDtypeStruct
    return kernel_call(
        atom_prep_kernel,
        [
            sds((4, 256, DA), BF16), sds((4, 256, FA), BF16), sds((4, 256, 2 * FA), BF16), sds((4, 256, DA), F32),
            sds((4, 256, DA), BF16), sds((4, 256, DA), F32),
        ],
        us=6,
        name="atom_prep",
    )(*args)


def atom_back_kernel(
    gpooled_ref, u_ref, mid_ref, gate_ref, att_ref, q_ref, kv_ref, probs_ref, pair_ref, w_out_ref, w_up_ref,
    w_down_ref, second_ref, hidden_ref, rate_ref, down_ref, gated_ref, branch_ref,
    dq_ref, dgate_ref, dkv_ref, prev_ref, next_ref, dmid_ref, du_ref, dw_out_ref, dw_up_ref, dw_down_ref, dpair_ref,
    dy_ref, grads_ref, slopes_ref, sums_ref, gbranch_ref, dup_ref, gdown_ref,
):
    gate_a, scale_b, gate_b = sigmoid(part(u_ref, 2, DA)), sigmoid(part(u_ref, 3, DA)), sigmoid(part(u_ref, 5, DA))

    def atoms(s):
        for k in range(4):
            dy_ref[s, pl.ds(k, 64, stride=4), :] = gpooled_ref[s]
        dy = dy_ref[s]
        gdown = (dy * gate_b).astype(BF16)
        gdown_ref[s] = gdown
        dhidden = dot(gdown, w_down_ref[...], ((1,), (1,)))
        dup = (jnp.concatenate([dhidden, dhidden], axis=1) * rate_ref[s].astype(F32)).astype(BF16)
        dup_ref[s] = dup
        dsecond = dot(dup, w_up_ref[...], ((1,), (1,)))
        lines, inverse = normed(mid_ref[s])
        dmid = dy + norm_back_rows(dsecond * scale_b, lines, inverse)
        dmid_ref[s] = dmid
        gate, attended = gate_ref[s], att_ref[s]
        gbranch = (dmid * gate_a).astype(BF16)
        gbranch_ref[s] = gbranch
        sums = [dmid * branch_ref[s], dsecond * lines, dsecond, dy * down_ref[s]]
        for i in range(4):
            lanes = slice(DA * i, DA * i + DA)
            sums_ref[:, lanes] = sums[i] if s == 0 else sums_ref[:, lanes] + sums[i]
        dgated = dot(gbranch, w_out_ref[...], ((1,), (1,)))
        dgate_ref[s] = (dgated * attended * slope(gate)).astype(BF16)
        cots = head_rows(dgated * gate)
        rows = head_rows(q_ref[s].astype(F32))
        low = probs_ref[s]
        probs = low.astype(F32)

        def window(w):
            return slice(128 * w, 128 * w + 128), slice(32 * w, 32 * w + 128)

        def weights_of(w):
            at, span = window(w)
            return dot(cots[at], kv_ref[s, span, DA:], ((1,), (1,)))

        weighed = probs * by_window(weights_of)
        slopes = weighed - probs * jnp.sum(weighed, axis=1, keepdims=True)
        slopes_ref[...] = slopes if s == 0 else slopes_ref[...] + slopes
        slopes_low = slopes.astype(BF16)

        def query_of(w):
            at, span = window(w)
            return dot(slopes_low[at], kv_ref[s, span, :DA])

        dq_ref[s] = (rows_of_heads(by_window(query_of)) * 32 ** (-0.5)).astype(BF16)
        grads_ref[s] = jnp.zeros((SPAN, 2 * DA), F32)
        for w in range(8):
            at, span = window(w)
            grads_ref[s, span, :DA] += dot(slopes_low[at], rows[at], ((0,), (0,))) * 32 ** (-0.5)
            grads_ref[s, span, DA:] += dot(low[at], cots[at], ((0,), (0,)))
        dkv_ref[s] = grads_ref[s, RIM : RIM + 256, :]
        prev_ref[s] = grads_ref[s, :RIM, :].astype(BF16)
        next_ref[s] = grads_ref[s, RIM + 256 :, :].astype(BF16)

    for s in range(4):
        atoms(s)

    def rows_of(ref):
        return ref[...].reshape(1024, ref.shape[2])

    dw_out_ref[...] = dot(rows_of(gated_ref), rows_of(gbranch_ref), ((0,), (0,)))
    dw_up_ref[...] = dot(rows_of(second_ref), rows_of(dup_ref), ((0,), (0,)))
    dw_down_ref[...] = dot(rows_of(hidden_ref), rows_of(gdown_ref), ((0,), (0,)))
    du_ref[:, :DA] = sums_ref[:, :DA] * slope(gate_a)
    du_ref[:, DA : 2 * DA] = sums_ref[:, DA : 2 * DA] * slope(scale_b)
    du_ref[:, 2 * DA : 3 * DA] = sums_ref[:, 2 * DA : 3 * DA]
    du_ref[:, 3 * DA :] = sums_ref[:, 3 * DA :] * slope(gate_b)
    pairs = pair_norm(pair_ref[...].astype(F32))
    slopes = slopes_ref[...].reshape(8, 4, 32, 128)
    for h in range(4):
        own = slopes[:, h].reshape(256, 128)
        for c in range(16):
            dpair_ref[16 * h + c : 16 * h + c + 1, :] = jnp.sum(own * pairs[c], axis=0, keepdims=True)


def atom_back(*args):
    sds = jax.ShapeDtypeStruct
    return kernel_call(
        atom_back_kernel,
        [
            sds((4, 256, DA), BF16), sds((4, 256, DA), BF16), sds((4, 256, 2 * DA), F32),
            sds((4, RIM, 2 * DA), BF16), sds((4, RIM, 2 * DA), BF16), sds((4, 256, DA), F32),
            sds((256, 4 * DA), F32), sds((DA, DA), F32), sds((DA, 2 * FA), F32), sds((FA, DA), F32), sds((64, 128), F32),
        ],
        scratch=[
            pltpu.VMEM((4, 256, DA), F32), pltpu.VMEM((4, SPAN, 2 * DA), F32), pltpu.VMEM((1024, 128), F32),
            pltpu.VMEM((256, 4 * DA), F32), pltpu.VMEM((4, 256, DA), BF16), pltpu.VMEM((4, 256, 2 * FA), BF16),
            pltpu.VMEM((4, 256, DA), BF16),
        ],
        us=12,
        name="atom_back",
    )(*args)


def atom_end_kernel(
    core_ref, dq_ref, dgate_ref, dkv_ref, prev_ref, next_ref, dmid_ref, x_ref, first_ref, u_ref, du_ref, cond_low_ref,
    w_qkvg_ref, dw_out_ref, dw_up_ref, dw_down_ref, dpool_ref, single_ref, tdu_ref, misc_ref,
    out_ref, keep_ref, send_ref,
    dw_qkvg_ref, sums_ref, whole_ref,
):
    scale = sigmoid(part(u_ref, 0, DA))
    sums_ref[...] = jnp.zeros_like(sums_ref)
    dw_qkvg_ref[...] = jnp.zeros_like(dw_qkvg_ref)

    @pl.loop(0, 4)
    def _(s):
        whole_ref[...] = dkv_ref[s]
        whole_ref[:RIM, :] += prev_ref[s].astype(F32)
        whole_ref[256 - RIM :, :] += next_ref[s].astype(F32)
        grads = jnp.concatenate([dq_ref[s], whole_ref[...].astype(BF16), dgate_ref[s]], axis=1)
        dfirst = dot(grads, w_qkvg_ref[...], ((1,), (1,)))
        lines, inverse = normed(x_ref[s].astype(F32))
        out_ref[s] = dmid_ref[s] + norm_back_rows(dfirst * scale, lines, inverse)
        dw_qkvg_ref[...] += dot(first_ref[s], grads, ((0,), (0,)))
        sums_ref[:, :DA] += dfirst * lines
        sums_ref[:, DA:] += dfirst

    du = jnp.concatenate([sums_ref[:, :DA] * slope(scale), sums_ref[:, DA:], du_ref[...]], axis=1).astype(BF16)
    dw_cond = dot(cond_low_ref[...], du, ((0,), (0,)))
    down = dw_down_ref[...].reshape(16, 2, 8, DA)
    single = dot(single_ref[...], tdu_ref[...], ((0,), (0,))).reshape(16, 3, 8, 2 * DT)
    whole = jnp.concatenate(
        [
            dw_cond, dw_qkvg_ref[...], dw_out_ref[...], dw_up_ref[...], dpool_ref[...],
            down[:, 0].reshape(DA, DA), down[:, 1].reshape(DA, DA), misc_ref[...].astype(F32),
        ]
        + [single[:, i].reshape(DA, 2 * DT) for i in range(3)]
        + [jnp.zeros((DA, 512), F32)],
        axis=1,
    )
    even = core_ref[0] == 0
    for s in range(8):
        rows = whole[:, 1024 * s : 1024 * s + 1024].reshape(8, 2, 8, 1024)
        first, second = rows[:, 0].reshape(64, 1024), rows[:, 1].reshape(64, 1024)
        keep_ref[s] = jnp.where(even, first, second).astype(BF16)
        send_ref[s] = jnp.where(even, second, first).astype(BF16)


def atom_end(*args):
    sds = jax.ShapeDtypeStruct
    return kernel_call(
        atom_end_kernel,
        [sds((4, 256, DA), F32), sds((8, 64, 1024), BF16), sds((8, 64, 1024), BF16)],
        in_specs=[pl.BlockSpec((256, DA), lambda *_: (0, 0)) if i == 8 else fixed(*a.shape) for i, a in enumerate(args[1:])],
        scratch=[pltpu.VMEM((DA, 4 * DA), F32), pltpu.VMEM((256, 2 * DA), F32), pltpu.VMEM((256, 2 * DA), F32)],
        scalars=1,
        us=6,
        arrived=(3, 4),
        name="atom_end",
    )(*args)


SHARE = 960


def split_kernel(samp_ref, wide_ref, heads_ref, *refs):
    out_refs, whole_ref = refs[:4], refs[4]
    for s in range(8):
        pieces = [wide_ref[:, SHARE * s : SHARE * s + SHARE].astype(F32)]
        pieces += [heads_ref[2 * s + i, 64:, : 3 * HS].astype(F32) for i in range(2)]
        whole_ref[s] = jnp.concatenate(pieces + [jnp.zeros((48, 32), F32)], axis=1).astype(BF16)
    for k in range(8):
        out_refs[k // 2][k % 2] = whole_ref[samp_ref[0] ^ k]


def split(samp, wide, heads):
    return kernel_call(
        split_kernel,
        [jax.ShapeDtypeStruct((2, 48, 1280), BF16)] * 4,
        scratch=[pltpu.VMEM((8, 48, 1280), BF16)],
        scalars=1,
        us=3,
        arrived=(0, 1),
        name="split",
    )(samp, wide, heads)


def collect_kernel(wide_ref, wide_part_ref, packed_ref, out_ref, total_ref):
    step = pl.program_id(0)

    @pl.when(step == 0)
    def _():
        total_ref[...] = jnp.zeros_like(total_ref)

    rows = packed_ref[0].astype(F32)
    for i in range(1, 16):
        rows += packed_ref[i].astype(F32)
    total_ref[:, :1024] += rows

    @pl.when(step == 3)
    def _():
        wide = wide_ref[...].astype(F32) + wide_part_ref[...].astype(F32)
        whole = jnp.concatenate([wide, total_ref[...]], axis=0).astype(BF16)
        for i in range(8):
            out_ref[i] = whole


def collect(wide, wide_part, packed):
    return kernel_call(
        collect_kernel,
        [jax.ShapeDtypeStruct((8, 56, 1280), BF16)],
        grid=(4,),
        in_specs=[fixed(48, 1280), fixed(48, 1280), pl.BlockSpec((16, 8, 1024), lambda i: (i, 0, 0))],
        out_specs=[fixed(8, 56, 1280)],
        scratch=[pltpu.VMEM((8, 1280), F32)],
        us=4,
        arrived=(0, 1, 2),
        name="collect",
    )(wide, wide_part, packed)[0]


def hand_out_kernel(
    parts_ref, a_cond_ref, a_qkvg_ref, a_out_ref, a_up_ref, a_down_ref, a_pair_ref, pool_ref, t_cond_ref, t_qkvg_ref,
    t_out_ref, t_up_ref, t_down_ref, t_pair_ref,
):
    def cut(first, last, rows, share):
        pieces = []
        while first < last:
            s, at = divmod(first, share)
            end = min(last - share * s, share)
            pieces.append(parts_ref[s, rows, at:end].astype(F32))
            first = share * s + end
        return jnp.concatenate(pieces, axis=1)

    def wide(first, last):
        return cut(first, last, slice(0, 48), SHARE)

    def atoms(first, last):
        return cut(first, last, slice(48, 56), 1024)

    t_up_ref[...] = wide(0, 4 * DT)
    t_out_ref[...] = wide(4 * DT, 5 * DT)
    t_qkvg_ref[:, 3 * DT :] = wide(5 * DT, 6 * DT)
    t_down_ref[:48, :] = wide(6 * DT, 7 * DT)
    t_down_ref[48:, :] = wide(7 * DT, 8 * DT)
    conds = wide(8 * DT, 10 * DT)
    t_cond_ref[:, 2 * DT : 4 * DT] = conds[:24]
    t_cond_ref[:, 4 * DT :] = conds[24:]
    for i in range(3):
        t_cond_ref[8 * i : 8 * i + 8, : 2 * DT] = atoms(3072 + 2 * DT * i, 3072 + 2 * DT * (i + 1))
    a_cond_ref[...] = atoms(0, 768)
    a_qkvg_ref[...] = atoms(768, 1280)
    a_out_ref[...] = atoms(1280, 1408)
    a_up_ref[...] = atoms(1408, 1920)
    pool_ref[...] = atoms(1920, 2688)
    a_down_ref[:8] = atoms(2688, 2816)
    a_down_ref[8:] = atoms(2816, 2944)
    misc = atoms(2944, 3072)
    t_pair_ref[...] = misc[0:1]
    a_pair_ref[...] = misc[1:2, :4]
    heads = []
    for h in range(16):
        at = SHARE + 3 * HS * (h % 2)
        heads.append(parts_ref[h // 2, :48, at : at + 3 * HS].astype(F32))
    for i in range(3):
        t_qkvg_ref[:, DT * i : DT * i + DT] = jnp.concatenate(
            [head[:, HS * i : HS * i + HS] for head in heads], axis=1
        )


def hand_out(parts):
    sds = jax.ShapeDtypeStruct
    shapes = [
        (8, 768), (8, 512), (8, 128), (8, 512), (16, 128), (1, 4), (8, 768), (24, 6 * DT), (48, 4 * DT), (48, DT),
        (48, 2 * FT), (96, DT), (1, 128),
    ]
    return kernel_call(
        hand_out_kernel,
        [sds(shape, F32) for shape in shapes],
        us=4,
        arrived=(0,),
        name="hand_out",
    )(parts)


def both_axes(x):
    return lax.all_to_all(x, ("samp", "seq"), 0, 0, tiled=True)


def along_seq(x):
    return lax.all_to_all(x, "seq", 0, 0, tiled=True)


ordered = lambda *x: lax.optimization_barrier(x)


def from_samp(part, k):
    return lax.ppermute(part, "samp", [(i, i ^ k) for i in range(8)])


def total(*parts):
    return sum(part.astype(F32) for part in parts).astype(BF16)


def body(
    atom_in,
    tok_in,
    atom_cond,
    single_cond,
    atom_pair,
    token_pair,
    atom_w_cond,
    atom_w_qkvg,
    atom_w_out,
    atom_w_up,
    atom_w_down,
    atom_w_pair,
    pool_weight,
    token_w_cond,
    token_w_qkvg,
    token_w_out,
    token_w_up,
    token_w_down,
    token_w_pair,
    cotangent,
):
    samp, seq = lax.axis_index("samp"), lax.axis_index("seq")
    up, down = [(i, i + 1) for i in range(15)], [(i + 1, i) for i in range(15)]
    rims = jnp.concatenate([atom_in, atom_cond[None]], axis=0)
    from_prev = lax.ppermute(rims[:, 256 - RIM :], "seq", up)
    from_next = lax.ppermute(rims[:, :RIM], "seq", down)
    samp = samp.astype(jnp.int32).reshape(1)
    token_bias = pair_bias(samp, token_pair, token_w_pair)
    token_bias = along_seq(token_bias).reshape(NT, 128)
    atom_in, token_bias = ordered(atom_in, token_bias)
    token_bias = lax.all_gather(token_bias, "samp", axis=0, axis_index_groups=[SAMP_RING])

    key_index = 256 * seq - RIM + 32 * jnp.arange(8)[:, None] + jnp.arange(128)[None, :]
    mask = jnp.where((key_index >= 0) & (key_index < 4096), 0.0, masked).astype(F32)
    (
        first, query, keyval, probs, gate, attended, middle, cond_low, cond_proj, pooled,
        start, tfirst, tgate, tcond_proj, single_low, runs,
    ) = front(
        atom_in, from_prev, from_next, atom_cond, atom_pair, mask, atom_w_pair.astype(F32), atom_w_cond,
        atom_w_qkvg, atom_w_out, atom_w_up, atom_w_down, pool_weight, tok_in, single_cond, token_w_cond, token_w_qkvg,
    )
    prep = atom_prep(cond_proj, middle, gate, attended, atom_w_out, atom_w_up, atom_w_down)
    normed_pair = pair_normed(samp, token_pair)
    runs, normed_pair, *prep = ordered(along_seq(runs), normed_pair, *prep)
    qkv, tprobs, tattended = token_attention(runs, token_bias)
    tattended, sent = ordered(tattended, tfirst)
    lines = lax.all_gather(sent, "seq", axis=0, axis_index_groups=[RING])
    (
        token_out, cots, tdgate, tdmid, gated, gbranch, second, dup, hidden, gdown, tdu,
    ) = turn(
        along_seq(tattended), tgate, start, tcond_proj, cotangent, token_w_out, token_w_up, token_w_down
    )
    cots = along_seq(cots)
    wide = token_weights(gated, gbranch, tfirst, tdgate, second, dup, hidden, gdown, single_low, tdu)
    cots, wide = ordered(cots, wide)
    wide = lax.psum_scatter(wide, "seq", scatter_dimension=0, tiled=True, axis_index_groups=[RING])
    tgrads, *slopes = token_attention_back(samp, qkv, tprobs, cots)
    heads = head_weights(tgrads, lines)
    received = [from_samp(slopes[k], 2 * k) for k in range(1, 4)]
    tgrads, heads = ordered(along_seq(tgrads), heads)
    grad_tok, gpooled, dpool, tdu = back(
        tgrads, tdgate, tdmid, start, tcond_proj, token_w_qkvg, pool_weight, pooled
    )
    gpooled, *received = ordered(gpooled, *received)
    slopes = total(slopes[0], *received)
    slopes = along_seq(jnp.concatenate([slopes, heads], axis=1))
    (
        dquery, dgate, dkeyval, to_prev, to_next, dmid, du, dw_out, dw_up, dw_down, dpair,
    ) = atom_back(
        gpooled.reshape(4, 64, DA), cond_proj, middle, gate, attended, query, keyval, probs, atom_pair,
        atom_w_out, atom_w_up, atom_w_down, *prep,
    )
    back_next = lax.ppermute(to_prev, "seq", down)
    back_prev = lax.ppermute(to_next, "seq", up)
    misc = pair_grad(slopes, normed_pair, dpair)
    grad_atoms, packed, beside = atom_end(
        (seq % 2).astype(jnp.int32).reshape(1),
        dquery, dgate, dkeyval, back_prev, back_next, dmid, atom_in, first, cond_proj, du, cond_low,
        atom_w_qkvg, dw_out, dw_up, dw_down, dpool, single_low, tdu, misc,
    )
    packed = total(packed, lax.ppermute(beside, "seq", [(i, i ^ 1) for i in range(16)])).reshape(64, 8, 1024)
    _, wide = ordered(packed, wide)
    chips = [[core + 2 * i for i in range(64)] for core in range(2)]
    packed = lax.all_to_all(packed, ("samp", "seq"), 0, 0, tiled=True, axis_index_groups=chips)
    wide = split(samp, wide, slopes)
    wide = total(wide[0], *[from_samp(wide[k], 2 * k) for k in range(1, 4)])
    wide = wide[0], from_samp(wide[1], 1)
    parts = lax.all_to_all(collect(*wide, packed), "samp", 0, 0, tiled=True)
    return (token_out, grad_atoms, grad_tok, *hand_out(parts))


def solution(mesh):
    rows, both, whole = P("seq", None), P("samp", "seq", None), P()
    in_specs = (both, both, rows, rows, P(None, "seq", None), P(None, "seq", None)) + (whole,) * 13 + (both,)
    out_specs = (both,) * 3 + (rows,) * 13
    mapped = jax.shard_map(body, mesh=mesh, in_specs=in_specs, out_specs=out_specs, check_vma=False)

    def run(*args):
        with jax.sharding.use_abstract_mesh(mesh.abstract_mesh):
            return mapped(*args)

    return run
```

```python
import jax
import jax.numpy as jnp
from jax import lax
from jax.experimental import pallas as pl
from jax.experimental.pallas import tpu as pltpu
from jax.sharding import PartitionSpec as P

eps = 1e-05
masked = -1000000000.0

MIB = 1 << 20
LIMIT = 44
F32, BF16 = jnp.float32, jnp.bfloat16


def kernel_call(
    kernel, out_shape, grid=(1,), in_specs=None, out_specs=None, scratch=(), scalars=0, arrived=(), us=1, name=None
):
    def run(*args):
        ins = list(in_specs or [fixed(*a.shape) for a in args[scalars:]])
        outs = list(out_specs or [fixed(*o.shape) for o in out_shape])
        args = list(args)
        for i in range(len(ins)):
            if i not in arrived and ins[i].memory_space in (None, pl.ANY):
                args[scalars + i] = pltpu.with_memory_space_constraint(args[scalars + i], pltpu.HBM)
        return pl.pallas_call(
            kernel,
            out_shape=[pltpu.HBM(o.shape, o.dtype) for o in out_shape],
            grid_spec=pltpu.PrefetchScalarGridSpec(
                num_scalar_prefetch=scalars, grid=grid, in_specs=ins, out_specs=outs, scratch_shapes=list(scratch)
            ),
            compiler_params=pltpu.CompilerParams(vmem_limit_bytes=LIMIT * MIB),
            cost_estimate=pl.CostEstimate(flops=us << 28, bytes_accessed=us << 20, transcendentals=0),
            name=name,
        )(*args)

    return run


def fixed(*shape):
    return pl.BlockSpec(shape, lambda *_: (0,) * len(shape), pipeline_mode=pl.Buffered(1))


def dot(left, right, over=((1,), (0,))):
    return lax.dot_general(left, right, (over, ((), ())), preferred_element_type=F32)


def swap_halves(first, second):
    low = lax.broadcasted_iota(jnp.int32, first.shape, 1) < 64
    half = first.shape[1] // 2
    return (
        jnp.where(low, first, pltpu.roll(second, half, 1)),
        jnp.where(low, pltpu.roll(first, half, 1), second),
    )


def runs_to_tokens(runs_ref, tokens_ref):
    for pair in range(runs_ref.shape[0] // 2):
        for duo in range(2):
            lanes = slice(128 * duo, 128 * duo + 128)
            made = swap_halves(
                runs_ref[2 * pair, :, lanes].astype(F32), runs_ref[2 * pair + 1, :, lanes].astype(F32)
            )
            for k in range(2):
                tokens_ref[2 * duo + k, :, 128 * pair : 128 * pair + 128] = made[k].astype(
                    tokens_ref.dtype
                )


def tokens_to_runs(tokens_ref, runs_ref):
    for pair in range(runs_ref.shape[0] // 2):
        lanes = slice(128 * pair, 128 * pair + 128)
        for duo in range(2):
            made = swap_halves(tokens_ref[2 * duo, :, lanes], tokens_ref[2 * duo + 1, :, lanes])
            for k in range(2):
                runs_ref[2 * pair + k, :, 128 * duo : 128 * duo + 128] = made[k].astype(runs_ref.dtype)


HS = 48
NT = 1024
QB = 256
SAMP_RING = [0, 2, 4, 6, 7, 5, 3, 1]


def attention_kernel(runs_ref, bias_ref, qkv_ref, probs_ref, out_ref, heads_ref):
    sample = pl.program_id(0)

    @pl.when(sample == 0)
    def _():
        runs_to_tokens(runs_ref, qkv_ref)

    keys = qkv_ref[sample, HS : 2 * HS, :]
    values = qkv_ref[sample, 2 * HS :, :]

    def scores_of(block):
        rows = slice(block * QB, block * QB + QB)
        made = dot(qkv_ref[sample, :HS, rows], keys, ((0,), (0,))) * HS ** (-0.5)
        return made + jnp.concatenate([bias_ref[SAMP_RING.index(i), rows, :] for i in range(8)], axis=1).astype(F32)

    count = NT // QB
    ahead = scores_of(0)
    for block in range(count):
        rows = slice(block * QB, block * QB + QB)
        scores = ahead
        if block + 1 < count:
            ahead = scores_of(block + 1)
        exponent = jnp.exp(scores - jnp.max(scores, axis=1, keepdims=True))
        probs = (exponent * (1.0 / jnp.sum(exponent, axis=1, keepdims=True))).astype(BF16)
        probs_ref[0, rows, :] = probs
        heads_ref[sample, :, rows] = dot(probs, values, ((1,), (1,))).T

    @pl.when(sample == 3)
    def _():
        tokens_to_runs(heads_ref, out_ref)


def token_attention(runs, bias):
    return kernel_call(
        attention_kernel,
        [
            jax.ShapeDtypeStruct((4, 3 * HS, NT), BF16),
            jax.ShapeDtypeStruct((4, NT, NT), BF16),
            jax.ShapeDtypeStruct((16, HS, 256), BF16),
        ],
        grid=(4,),
        in_specs=[fixed(16, 3 * HS, 256)] + [fixed(8, NT, 128)],
        out_specs=[
            fixed(4, 3 * HS, NT), pl.BlockSpec((1, NT, NT), lambda s: (s, 0, 0)), fixed(16, HS, 256),
        ],
        scratch=[pltpu.VMEM((4, HS, NT), F32)],
        us=13,
        arrived=(0,),
        name="token_attention",
    )(runs, bias)


def attention_back_kernel(samp_ref, qkv_ref, probs_ref, cot_ref, out_ref, *refs):
    pair_refs, (cots_ref, grads_ref, total_ref) = refs[:4], refs[4:]
    sample = pl.program_id(0)

    @pl.when(sample == 0)
    def _():
        runs_to_tokens(cot_ref, cots_ref)
        total_ref[...] = jnp.zeros_like(total_ref)

    keys = qkv_ref[sample, HS : 2 * HS, :]
    values = qkv_ref[sample, 2 * HS :, :]

    def weights_of(block):
        return dot(cots_ref[sample, :, block * QB : block * QB + QB], values, ((0,), (0,)))

    key_grad, value_grad = 0.0, 0.0
    count = NT // QB
    ahead = weights_of(0)
    for block in range(count):
        rows = slice(block * QB, block * QB + QB)
        now = ahead
        if block + 1 < count:
            ahead = weights_of(block + 1)
        low = probs_ref[0, rows, :]
        probs = low.astype(F32)
        weighed = probs * now
        slopes = weighed - probs * jnp.sum(weighed, axis=1, keepdims=True)
        slopes_low = slopes.astype(BF16)
        total_ref[rows, :] += slopes
        grads_ref[sample, :HS, rows] = dot(keys, slopes_low, ((1,), (1,))) * HS ** (-0.5)
        key_grad += dot(qkv_ref[sample, :HS, rows], slopes_low)
        value_grad += dot(cots_ref[sample, :, rows], low)
    grads_ref[sample, HS : 2 * HS, :] = key_grad * HS ** (-0.5)
    grads_ref[sample, 2 * HS :, :] = value_grad

    @pl.when(sample == 3)
    def _():
        tokens_to_runs(grads_ref, out_ref)
        for k in range(4):
            lanes = pl.ds(pl.multiple_of(((samp_ref[0] // 2) ^ k) * 256, 256), 256)
            pair_refs[k][...] = total_ref[:, lanes].astype(BF16).reshape(16, 64, 256)


def token_attention_back(samp, qkv, probs, cots):
    return kernel_call(
        attention_back_kernel,
        [jax.ShapeDtypeStruct((16, 3 * HS, 256), BF16)] + [jax.ShapeDtypeStruct((16, 64, 256), BF16)] * 4,
        grid=(4,),
        in_specs=[fixed(4, 3 * HS, NT), pl.BlockSpec((1, NT, NT), lambda s, _: (s, 0, 0)), fixed(16, HS, 256)],
        out_specs=[fixed(16, 3 * HS, 256)] + [fixed(16, 64, 256)] * 4,
        scratch=[
            pltpu.VMEM((4, HS, NT), BF16),
            pltpu.VMEM((4, 3 * HS, NT), F32),
            pltpu.VMEM((NT, NT), F32),
        ],
        scalars=1,
        us=14,
        arrived=(2,),
        name="token_attention_back",
    )(samp, qkv, probs, cots)


def normed_rows(pair_ref):
    pair = pair_ref[...].astype(F32)
    centred = pair - jnp.mean(pair, axis=0, keepdims=True)
    inverse = lax.rsqrt(jnp.mean(centred * centred, axis=0, keepdims=True) + eps)
    return jnp.swapaxes((centred * inverse).astype(BF16), 0, 1)


def pair_kernel(samp_ref, pair_ref, weight_ref, bias_ref):
    low = normed_rows(pair_ref)
    weight = weight_ref[...]
    bias = jnp.stack([dot(weight, low[i]) for i in range(low.shape[0])], axis=0)
    bias_ref[...] = jnp.swapaxes(bias, 0, 1).astype(BF16)


def pair_bias(samp, pair, weight):
    return kernel_call(
        pair_kernel,
        [jax.ShapeDtypeStruct((16, 64, 128), BF16)],
        grid=(2,),
        in_specs=[pl.BlockSpec((128, 32, 128), lambda i, samp: (0, i, samp[0])), fixed(16, 128)],
        out_specs=[pl.BlockSpec((16, 32, 128), lambda i, _: (0, i, 0))],
        scalars=1,
        us=4,
        name="pair_bias",
    )(samp, pair, weight)[0]


def pair_norm_kernel(samp_ref, pair_ref, normed_ref):
    normed_ref[...] = normed_rows(pair_ref)


def pair_normed(samp, pair):
    return kernel_call(
        pair_norm_kernel,
        [jax.ShapeDtypeStruct((64, 128, 256), BF16)],
        grid=(4,),
        in_specs=[pl.BlockSpec((128, 16, 256), lambda i, samp: (0, i, samp[0] // 2))],
        out_specs=[pl.BlockSpec((16, 128, 256), lambda i, _: (i, 0, 0))],
        scalars=1,
        us=6,
        name="pair_normed",
    )(samp, pair)[0]


def pair_back_kernel(slopes_ref, normed_ref, atoms_ref, out_ref, grad_ref):
    step = pl.program_id(0)
    slopes = jnp.swapaxes(slopes_ref[...], 0, 1)
    made = dot(slopes[0], normed_ref[0], ((1,), (1,)))
    for i in range(1, slopes.shape[0]):
        made += dot(slopes[i], normed_ref[i], ((1,), (1,)))

    @pl.when(step == 0)
    def _():
        grad_ref[...] = made

    @pl.when(step > 0)
    def _():
        grad_ref[...] += made

    @pl.when(step == 3)
    def _():
        atoms = jnp.sum(atoms_ref[...], axis=1, keepdims=True)
        lane = lax.broadcasted_iota(jnp.int32, (16, 128), 1)
        rows = jnp.where(lane == 0, atoms[:16], 0.0)
        for h in range(1, 4):
            rows += jnp.where(lane == h, atoms[16 * h : 16 * h + 16], 0.0)
        line = lax.broadcasted_iota(jnp.int32, (16, 8, 128), 1)
        both = jnp.where(line == 0, grad_ref[...][:, None, :], 0.0) + jnp.where(line == 1, rows[:, None, :], 0.0)
        out_ref[...] = both.reshape(128, 128).astype(BF16)


def pair_grad(slopes, normed, atoms):
    return kernel_call(
        pair_back_kernel,
        [jax.ShapeDtypeStruct((128, 128), BF16)],
        grid=(4,),
        in_specs=[
            pl.BlockSpec((16, 16, 256), lambda i: (0, i, 0)),
            pl.BlockSpec((16, 128, 256), lambda i: (i, 0, 0)),
            fixed(64, 128),
        ],
        out_specs=[fixed(128, 128)],
        scratch=[pltpu.VMEM((16, 128), F32)],
        arrived=(0,),
        us=6,
        name="pair_grad",
    )(slopes, normed, atoms)[0]


DA, DT, FT, FA = 128, 768, 1536, 256
RIM = 48
RING = [0, 1, 4, 5, 8, 9, 12, 13, 14, 15, 10, 11, 6, 7, 2, 3]
SPAN = 256 + 2 * RIM


def normed(x):
    centred = x - jnp.mean(x, axis=-1, keepdims=True)
    inverse = lax.rsqrt(jnp.mean(centred * centred, axis=-1, keepdims=True) + eps)
    return centred * inverse, inverse


def sigmoid(x):
    return 1.0 / (1.0 + jnp.exp(-x))


def own_head():
    shape = (1, 4, 32, 128)
    return lax.broadcasted_iota(jnp.int32, shape, 3) // 32 == lax.broadcasted_iota(jnp.int32, shape, 1)


def head_rows(rows):
    return jnp.where(own_head(), rows.reshape(8, 1, 32, 128), 0.0).reshape(1024, 128).astype(BF16)


def rows_of_heads(full):
    return jnp.sum(jnp.where(own_head(), full.reshape(8, 4, 32, 128), 0.0), axis=1).reshape(256, 128)


def by_window(made):
    return jnp.concatenate([made(w) for w in range(8)], axis=0)


def pair_norm(pair):
    centred = pair - jnp.mean(pair, axis=0, keepdims=True)
    inverse = lax.rsqrt(jnp.mean(centred * centred, axis=0, keepdims=True) + eps)
    return (centred * inverse).astype(BF16).astype(F32)


def part(ref, i, width, rows=slice(None)):
    return ref[rows, i * width : (i + 1) * width]


def front_kernel(
    x_ref, prev_ref, next_ref, cond_ref, pair_ref, mask_ref, w_pair_ref, w_cond_ref, w_qkvg_ref, w_out_ref,
    w_up_ref, w_down_ref, pool_ref, tok_ref, single_ref, tw_cond_hbm, tw_qkvg_hbm,
    first_ref, q_ref, kv_ref, probs_ref, gate_ref, att_ref, mid_ref, cond_low_ref, u_ref, pooled_ref,
    start_ref, tfirst_ref, tgate_ref, tu_ref, single_low_ref, runs_ref,
    bias_ref, y_ref, uh_ref, tw_cond_ref, tw_qkvg_ref, sems,
):
    loads = [
        pltpu.make_async_copy(tw_cond_hbm, tw_cond_ref, sems.at[0]),
        pltpu.make_async_copy(tw_qkvg_hbm, tw_qkvg_ref, sems.at[1]),
    ]
    for load in loads:
        load.start()
    cond = jnp.concatenate([prev_ref[4], cond_ref[...], next_ref[4]], axis=0).astype(F32)
    cond_low = normed(cond)[0].astype(BF16)
    cond_low_ref[...] = cond_low[RIM : RIM + 256]
    u_ref[...] = dot(cond_low[RIM : RIM + 256], w_cond_ref[...])
    uh_ref[...] = dot(cond_low, w_cond_ref[:, : 2 * DA])
    pairs = pair_norm(pair_ref[...].astype(F32))
    for h in range(4):
        bias = pairs[0] * w_pair_ref[0, h]
        for c in range(1, 16):
            bias += pairs[c] * w_pair_ref[c, h]
        for w in range(8):
            at = 128 * w + 32 * h
            bias_ref[at : at + 32, :] = bias[32 * w : 32 * w + 32] + mask_ref[w : w + 1, :]

    scale_a, shift_a = sigmoid(part(uh_ref, 0, DA)), part(uh_ref, 1, DA)
    gate_a, scale_b, shift_b, gate_b = (
        sigmoid(part(u_ref, 2, DA)), sigmoid(part(u_ref, 3, DA)), part(u_ref, 4, DA), sigmoid(part(u_ref, 5, DA)),
    )

    def atoms(s):
        x = jnp.concatenate([prev_ref[s], x_ref[s], next_ref[s]], axis=0).astype(F32)
        first = (scale_a * normed(x)[0] + shift_a).astype(BF16)
        projected = dot(first, w_qkvg_ref[...])
        own = projected[RIM : RIM + 256]
        first_ref[s] = first[RIM : RIM + 256]
        query = own[:, :DA].astype(BF16)
        q_ref[s] = query
        keys = projected[:, DA : 2 * DA].astype(BF16)
        values = projected[:, 2 * DA : 3 * DA].astype(BF16)
        kv_ref[s, :, :DA] = keys
        kv_ref[s, :, DA:] = values
        gate = sigmoid(own[:, 3 * DA :])
        gate_ref[s] = gate
        rows = head_rows(query.astype(F32))
        scores = by_window(lambda w: dot(rows[128 * w : 128 * w + 128], keys[32 * w : 32 * w + 128], ((1,), (1,))))
        scores = scores * 32 ** (-0.5) + bias_ref[...]
        exponent = jnp.exp(scores - jnp.max(scores, axis=1, keepdims=True))
        probs = (exponent * (1.0 / jnp.sum(exponent, axis=1, keepdims=True))).astype(BF16)
        probs_ref[s] = probs
        attended = rows_of_heads(
            by_window(lambda w: dot(probs[128 * w : 128 * w + 128], values[32 * w : 32 * w + 128]))
        )
        att_ref[s] = attended
        branch = dot((gate * attended).astype(BF16), w_out_ref[...])
        middle = x[RIM : RIM + 256] + gate_a * branch
        mid_ref[s] = middle
        second = (scale_b * normed(middle)[0] + shift_b).astype(BF16)
        up = dot(second, w_up_ref[...])
        hidden = (up[:, :FA] * sigmoid(up[:, :FA]) * up[:, FA:]).astype(BF16)
        y_ref[s] = middle + gate_b * dot(hidden, w_down_ref[...])
        pooled = y_ref[s, pl.ds(0, 64, stride=4), :]
        for k in range(1, 4):
            pooled += y_ref[s, pl.ds(k, 64, stride=4), :]
        pooled_ref[s] = (pooled * 0.25).astype(BF16)

    for s in range(4):
        atoms(s)

    for load in loads:
        load.wait()
    single_low = normed(single_ref[...].astype(F32))[0].astype(BF16)
    single_low_ref[...] = single_low
    for i in range(6):
        tu_ref[:, DT * i : DT * i + DT] = dot(single_low, tw_cond_ref[:, DT * i : DT * i + DT])
    pooled = pooled_ref[...].reshape(256, DA)
    start = tok_ref[...].reshape(256, DT).astype(F32) + dot(pooled, pool_ref[...])
    start_ref[...] = start
    lines = normed(start)[0]
    scale, shift = sigmoid(part(tu_ref, 0, DT)), part(tu_ref, 1, DT)
    for s in range(4):
        tfirst_ref[64 * s : 64 * s + 64, :] = (scale * lines[64 * s : 64 * s + 64] + shift).astype(BF16)
    first = tfirst_ref[...]
    for i in range(3):
        turned = dot(first, part(tw_qkvg_ref, i, DT)).T.astype(BF16)
        for h in range(16):
            runs_ref[h, HS * i : HS * i + HS, :] = turned[HS * h : HS * h + HS]
    tgate_ref[...] = sigmoid(dot(first, part(tw_qkvg_ref, 3, DT)))


def front(*args):
    sds = jax.ShapeDtypeStruct
    specs = [fixed(*a.shape) for a in args]
    specs[6] = pl.BlockSpec(memory_space=pltpu.SMEM)
    specs[15] = specs[16] = pl.BlockSpec(memory_space=pl.ANY)
    return kernel_call(
        front_kernel,
        [
            sds((4, 256, DA), BF16), sds((4, 256, DA), BF16), sds((4, SPAN, 2 * DA), BF16),
            sds((4, 1024, 128), BF16), sds((4, 256, DA), F32), sds((4, 256, DA), F32),
            sds((4, 256, DA), F32), sds((256, DA), BF16), sds((256, 6 * DA), F32), sds((4, 64, DA), BF16),
            sds((256, DT), F32), sds((256, DT), BF16), sds((256, DT), F32), sds((64, 6 * DT), F32),
            sds((64, 384), BF16), sds((16, 3 * HS, 256), BF16),
        ],
        in_specs=specs,
        scratch=[
            pltpu.VMEM((1024, 128), F32), pltpu.VMEM((4, 256, DA), F32), pltpu.VMEM((SPAN, 2 * DA), F32),
            pltpu.VMEM((384, 6 * DT), BF16), pltpu.VMEM((DT, 4 * DT), BF16), pltpu.SemaphoreType.DMA((2,)),
        ],
        us=24,
        arrived=(1, 2),
        name="front",
    )(*args)


def slope(squashed):
    return squashed * (1.0 - squashed)


def norm_back_rows(gradient, lines, inverse):
    return inverse * (
        gradient
        - jnp.mean(gradient, axis=-1, keepdims=True)
        - lines * jnp.mean(gradient * lines, axis=-1, keepdims=True)
    )


def turn_kernel(
    runs_ref, tgate_ref, start_ref, tu_ref, cot_ref, w_out_hbm, w_up_hbm, w_down_hbm,
    out_ref, cots_ref, dgate_ref, dmid_ref, a_ref, gbranch_ref, second_ref, dup_ref, hidden_ref, gdown_ref,
    du_ref,
    up_ref, mid_ref, branch_ref, down_ref, w_out_ref, w_up_ref, w_down_ref, sems,
):
    loads = [
        pltpu.make_async_copy(w_out_hbm, w_out_ref, sems.at[0]),
        pltpu.make_async_copy(w_up_hbm, w_up_ref, sems.at[1]),
        pltpu.make_async_copy(w_down_hbm, w_down_ref, sems.at[2]),
    ]
    for load in loads:
        load.start()
    attended = runs_ref[...].reshape(DT, 256).astype(F32).T
    gate = tgate_ref[...]
    gated = (gate * attended).astype(BF16)
    a_ref[...] = gated
    loads[0].wait()
    branch_ref[...] = dot(gated, w_out_ref[...])
    gate_a, scale_b, shift_b, gate_b = (
        sigmoid(part(tu_ref, 2, DT)), sigmoid(part(tu_ref, 3, DT)), part(tu_ref, 4, DT), sigmoid(part(tu_ref, 5, DT)),
    )
    runs = [slice(64 * s, 64 * s + 64) for s in range(4)]
    for r in runs:
        middle = start_ref[r, :] + gate_a * branch_ref[r, :]
        mid_ref[r, :] = middle
        second_ref[r, :] = (scale_b * normed(middle)[0] + shift_b).astype(BF16)
    second = second_ref[...]
    loads[1].wait()
    loads[2].wait()
    cut = 512
    for j in range(FT // cut):
        e = dot(second, w_up_ref[:, cut * j : cut * j + cut])
        f = dot(second, w_up_ref[:, FT + cut * j : FT + cut * j + cut])
        up_ref[:, cut * j : cut * j + cut] = e
        up_ref[:, FT + cut * j : FT + cut * j + cut] = f
        hidden = (e * sigmoid(e) * f).astype(BF16)
        hidden_ref[:, cut * j : cut * j + cut] = hidden
        piece = dot(hidden, w_down_ref[cut * j : cut * j + cut, :])
        if j == 0:
            down_ref[...] = piece
        else:
            down_ref[...] += piece
    total = jnp.zeros((64, DT), F32)
    for s, r in enumerate(runs):
        cot = cot_ref[s].astype(F32)
        out_ref[s] = (mid_ref[r, :] + gate_b * down_ref[r, :]).astype(BF16)
        gdown_ref[r, :] = (cot * gate_b).astype(BF16)
        total += cot * down_ref[r, :]
    du_ref[:, 3 * DT :] = (total * slope(gate_b)).astype(BF16)
    gdown = gdown_ref[...]
    dsecond = jnp.zeros((256, DT), F32)
    for j in range(FT // cut):
        dhidden = dot(gdown, w_down_ref[cut * j : cut * j + cut, :], ((1,), (1,)))
        e = up_ref[:, cut * j : cut * j + cut]
        f = up_ref[:, FT + cut * j : FT + cut * j + cut]
        half = sigmoid(e)
        de = (dhidden * f * half * (1.0 + e * (1.0 - half))).astype(BF16)
        df = (dhidden * e * half).astype(BF16)
        dup_ref[:, cut * j : cut * j + cut] = de
        dup_ref[:, FT + cut * j : FT + cut * j + cut] = df
        piece = dot(de, w_up_ref[:, cut * j : cut * j + cut], ((1,), (1,)))
        piece += dot(df, w_up_ref[:, FT + cut * j : FT + cut * j + cut], ((1,), (1,)))
        dsecond += piece
    down_ref[...] = dsecond
    total_a = jnp.zeros((64, DT), F32)
    total_b = jnp.zeros((64, DT), F32)
    total_c = jnp.zeros((64, DT), F32)
    for s, r in enumerate(runs):
        d = down_ref[r, :]
        lines, inverse = normed(mid_ref[r, :])
        dmid = cot_ref[s].astype(F32) + norm_back_rows(d * scale_b, lines, inverse)
        dmid_ref[r, :] = dmid
        gbranch_ref[r, :] = (dmid * gate_a).astype(BF16)
        total_a += dmid * branch_ref[r, :]
        total_b += d * lines
        total_c += d
    du_ref[:, :DT] = (total_a * slope(gate_a)).astype(BF16)
    du_ref[:, DT : 2 * DT] = (total_b * slope(scale_b)).astype(BF16)
    du_ref[:, 2 * DT : 3 * DT] = total_c.astype(BF16)
    dgated = dot(gbranch_ref[...], w_out_ref[...], ((1,), (1,)))
    dgate_ref[...] = (dgated * attended * slope(gate)).astype(BF16)
    cots_ref[...] = (dgated * gate).T.astype(BF16).reshape(16, HS, 256)


def turn(*args):
    sds = jax.ShapeDtypeStruct
    rows = lambda n, t=BF16: sds((256, n), t)
    return kernel_call(
        turn_kernel,
        [
            sds((4, 64, DT), BF16), sds((16, HS, 256), BF16), rows(DT), rows(DT, F32), rows(DT), rows(DT),
            rows(DT), rows(2 * FT), rows(FT), rows(DT), sds((64, 4 * DT), BF16),
        ],
        in_specs=[fixed(*a.shape) for a in args[:5]] + [pl.BlockSpec(memory_space=pl.ANY)] * 3,
        scratch=[pltpu.VMEM((256, 2 * FT), F32)]
        + [pltpu.VMEM((256, DT), F32)] * 3
        + [pltpu.VMEM(a.shape, BF16) for a in args[5:]]
        + [pltpu.SemaphoreType.DMA((3,))],
        us=12,
        arrived=(0,),
        name="turn",
    )(*args)


def weights_kernel(
    a_ref, gbranch_ref, first_ref, dgate_ref, second_ref, dup_ref, hidden_ref, gdown_ref, single_ref, du_ref, out_ref,
):
    step = pl.program_id(0)

    def write(rows, lanes=slice(None)):
        for at, run in enumerate(RING):
            out_ref[48 * at : 48 * at + 48, lanes] = rows[run]

    def square(left, right):
        return dot(left[...], right[...], ((0,), (0,))).astype(BF16)

    @pl.when(step < 2)
    def _():
        write(square(second_ref, dup_ref).reshape(16, 48, FT))

    @pl.when(step == 2)
    def _():
        write(square(a_ref, gbranch_ref).reshape(16, 48, DT), slice(0, DT))
        write(square(first_ref, dgate_ref).reshape(16, 48, DT), slice(DT, FT))

    @pl.when(step == 3)
    def _():
        made = square(hidden_ref, gdown_ref).reshape(16, 2, 48, DT)
        write(made[:, 0], slice(0, DT))
        write(made[:, 1], slice(DT, FT))

    @pl.when(step == 4)
    def _():
        made = dot(single_ref[...], du_ref[...], ((0,), (0,))).reshape(16, 24, 4 * DT)
        write(jnp.concatenate([made[:, :, :FT], made[:, :, FT:]], axis=1).astype(BF16))


def token_weights(*args):
    specs = [fixed(*a.shape) for a in args]
    specs[5] = pl.BlockSpec((256, FT), lambda i: (0, jnp.minimum(i, 1)))
    return kernel_call(
        weights_kernel,
        [jax.ShapeDtypeStruct((DT, 10 * DT), BF16)],
        grid=(5,),
        in_specs=specs,
        out_specs=[pl.BlockSpec((DT, FT), lambda i: (0, i))],
        us=12,
        name="token_weights",
    )(*args)[0]


def head_weights_kernel(grads_ref, lines_ref, out_ref, total_ref):
    step = pl.program_id(0)

    @pl.when(step == 0)
    def _():
        total_ref[...] = jnp.zeros_like(total_ref)

    for k in range(2):
        total_ref[...] += dot(grads_ref[k], lines_ref[k])

    @pl.when(step == 7)
    def _():
        out_ref[:, :, : 3 * HS] = total_ref[...].T.astype(BF16).reshape(16, 48, 3 * HS)
        out_ref[:, :, 3 * HS :] = jnp.zeros((16, 48, 256 - 3 * HS), BF16)


def head_weights(grads, lines):
    return kernel_call(
        head_weights_kernel,
        [jax.ShapeDtypeStruct((16, 48, 256), BF16)],
        grid=(8,),
        in_specs=[
            pl.BlockSpec((2, 3 * HS, 256), lambda i: (jnp.where(i < 4, 2 * i, 15 - 2 * i), 0, 0)),
            pl.BlockSpec((2, 256, DT), lambda i: (i, 0, 0)),
        ],
        out_specs=[fixed(16, 48, 256)],
        scratch=[pltpu.VMEM((3 * HS, DT), F32)],
        us=6,
        name="head_weights",
    )(grads, lines)[0]


def back_kernel(
    runs_ref, dgate_ref, dmid_ref, start_ref, tu_ref, w_qkvg_hbm, pool_ref, pooled_ref,
    out_ref, gpooled_ref, dpool_ref, ducat_ref,
    dfirst_ref, gpool_ref, w_qkvg_ref, sems,
):
    loads = [
        pltpu.make_async_copy(
            w_qkvg_hbm.at[:, DT * i : DT * i + DT], w_qkvg_ref.at[:, DT * i : DT * i + DT], sems.at[i]
        )
        for i in range(4)
    ]
    for i in (3, 0, 1, 2):
        loads[i].start()
    loads[3].wait()
    dfirst = dot(dgate_ref[...], part(w_qkvg_ref, 3, DT), ((1,), (1,)))
    for i in range(3):
        piece = runs_ref[:, HS * i : HS * i + HS, :].reshape(DT, 256)
        loads[i].wait()
        dfirst += dot(piece.astype(F32).T.astype(BF16), part(w_qkvg_ref, i, DT), ((1,), (1,)))
    dfirst_ref[...] = dfirst
    scale = sigmoid(part(tu_ref, 0, DT))
    total_a = jnp.zeros((64, DT), F32)
    total_b = jnp.zeros((64, DT), F32)
    for s in range(4):
        r = slice(64 * s, 64 * s + 64)
        d = dfirst_ref[r, :]
        lines, inverse = normed(start_ref[r, :])
        grad = dmid_ref[r, :] + norm_back_rows(d * scale, lines, inverse)
        out_ref[s] = grad
        gpool_ref[r, :] = grad.astype(BF16)
        total_a += d * lines
        total_b += d
    ducat_ref[:, :DT] = (total_a * slope(scale)).astype(BF16)
    ducat_ref[:, DT : 2 * DT] = total_b.astype(BF16)
    gpool = gpool_ref[...]
    gpooled_ref[...] = dot(gpool, pool_ref[...], ((1,), (1,))) * 0.25
    dpool_ref[...] = dot(pooled_ref[...].reshape(256, DA), gpool, ((0,), (0,)))


def back(*args):
    sds = jax.ShapeDtypeStruct
    return kernel_call(
        back_kernel,
        [sds((4, 64, DT), F32), sds((256, DA), F32), sds((DA, DT), F32), sds((64, 2 * DT), BF16)],
        in_specs=[
            pl.BlockSpec(memory_space=pl.ANY) if i == 5 else fixed(64, 2 * DT) if i == 4 else fixed(*a.shape)
            for i, a in enumerate(args)
        ],
        scratch=[
            pltpu.VMEM((256, DT), F32), pltpu.VMEM((256, DT), BF16), pltpu.VMEM((DT, 4 * DT), BF16),
            pltpu.SemaphoreType.DMA((4,)),
        ],
        us=7,
        arrived=(0,),
        name="back",
    )(*args)


def atom_prep_kernel(
    u_ref, mid_ref, gate_ref, att_ref, w_out_ref, w_up_ref, w_down_ref,
    second_ref, hidden_ref, rate_ref, down_ref, gated_ref, branch_ref,
):
    scale_b, shift_b = sigmoid(part(u_ref, 3, DA)), part(u_ref, 4, DA)
    for s in range(4):
        second = (scale_b * normed(mid_ref[s])[0] + shift_b).astype(BF16)
        second_ref[s] = second
        up = dot(second, w_up_ref[...])
        e, f = up[:, :FA], up[:, FA:]
        half = sigmoid(e)
        rate_ref[s, :, :FA] = (f * half * (1.0 + e * (1.0 - half))).astype(BF16)
        rate_ref[s, :, FA:] = (e * half).astype(BF16)
        hidden = (e * half * f).astype(BF16)
        hidden_ref[s] = hidden
        down_ref[s] = dot(hidden, w_down_ref[...])
        gated = (gate_ref[s] * att_ref[s]).astype(BF16)
        gated_ref[s] = gated
        branch_ref[s] = dot(gated, w_out_ref[...])


def atom_prep(*args):
    sds = jax.ShapeDtypeStruct
    return kernel_call(
        atom_prep_kernel,
        [
            sds((4, 256, DA), BF16), sds((4, 256, FA), BF16), sds((4, 256, 2 * FA), BF16), sds((4, 256, DA), F32),
            sds((4, 256, DA), BF16), sds((4, 256, DA), F32),
        ],
        us=6,
        name="atom_prep",
    )(*args)


def atom_back_kernel(
    gpooled_ref, u_ref, mid_ref, gate_ref, att_ref, q_ref, kv_ref, probs_ref, pair_ref, w_out_ref, w_up_ref,
    w_down_ref, second_ref, hidden_ref, rate_ref, down_ref, gated_ref, branch_ref,
    dq_ref, dgate_ref, dkv_ref, prev_ref, next_ref, dmid_ref, du_ref, dw_out_ref, dw_up_ref, dw_down_ref, dpair_ref,
    dy_ref, grads_ref, slopes_ref, sums_ref, gbranch_ref, dup_ref, gdown_ref,
):
    gate_a, scale_b, gate_b = sigmoid(part(u_ref, 2, DA)), sigmoid(part(u_ref, 3, DA)), sigmoid(part(u_ref, 5, DA))

    def atoms(s):
        for k in range(4):
            dy_ref[s, pl.ds(k, 64, stride=4), :] = gpooled_ref[s]
        dy = dy_ref[s]
        gdown = (dy * gate_b).astype(BF16)
        gdown_ref[s] = gdown
        dhidden = dot(gdown, w_down_ref[...], ((1,), (1,)))
        dup = (jnp.concatenate([dhidden, dhidden], axis=1) * rate_ref[s].astype(F32)).astype(BF16)
        dup_ref[s] = dup
        dsecond = dot(dup, w_up_ref[...], ((1,), (1,)))
        lines, inverse = normed(mid_ref[s])
        dmid = dy + norm_back_rows(dsecond * scale_b, lines, inverse)
        dmid_ref[s] = dmid
        gate, attended = gate_ref[s], att_ref[s]
        gbranch = (dmid * gate_a).astype(BF16)
        gbranch_ref[s] = gbranch
        sums = [dmid * branch_ref[s], dsecond * lines, dsecond, dy * down_ref[s]]
        for i in range(4):
            lanes = slice(DA * i, DA * i + DA)
            sums_ref[:, lanes] = sums[i] if s == 0 else sums_ref[:, lanes] + sums[i]
        dgated = dot(gbranch, w_out_ref[...], ((1,), (1,)))
        dgate_ref[s] = (dgated * attended * slope(gate)).astype(BF16)
        cots = head_rows(dgated * gate)
        rows = head_rows(q_ref[s].astype(F32))
        low = probs_ref[s]
        probs = low.astype(F32)

        def window(w):
            return slice(128 * w, 128 * w + 128), slice(32 * w, 32 * w + 128)

        def weights_of(w):
            at, span = window(w)
            return dot(cots[at], kv_ref[s, span, DA:], ((1,), (1,)))

        weighed = probs * by_window(weights_of)
        slopes = weighed - probs * jnp.sum(weighed, axis=1, keepdims=True)
        slopes_ref[...] = slopes if s == 0 else slopes_ref[...] + slopes
        slopes_low = slopes.astype(BF16)

        def query_of(w):
            at, span = window(w)
            return dot(slopes_low[at], kv_ref[s, span, :DA])

        dq_ref[s] = (rows_of_heads(by_window(query_of)) * 32 ** (-0.5)).astype(BF16)
        grads_ref[s] = jnp.zeros((SPAN, 2 * DA), F32)
        for w in range(8):
            at, span = window(w)
            grads_ref[s, span, :DA] += dot(slopes_low[at], rows[at], ((0,), (0,))) * 32 ** (-0.5)
            grads_ref[s, span, DA:] += dot(low[at], cots[at], ((0,), (0,)))
        dkv_ref[s] = grads_ref[s, RIM : RIM + 256, :]
        prev_ref[s] = grads_ref[s, :RIM, :].astype(BF16)
        next_ref[s] = grads_ref[s, RIM + 256 :, :].astype(BF16)

    for s in range(4):
        atoms(s)

    def rows_of(ref):
        return ref[...].reshape(1024, ref.shape[2])

    dw_out_ref[...] = dot(rows_of(gated_ref), rows_of(gbranch_ref), ((0,), (0,)))
    dw_up_ref[...] = dot(rows_of(second_ref), rows_of(dup_ref), ((0,), (0,)))
    dw_down_ref[...] = dot(rows_of(hidden_ref), rows_of(gdown_ref), ((0,), (0,)))
    du_ref[:, :DA] = sums_ref[:, :DA] * slope(gate_a)
    du_ref[:, DA : 2 * DA] = sums_ref[:, DA : 2 * DA] * slope(scale_b)
    du_ref[:, 2 * DA : 3 * DA] = sums_ref[:, 2 * DA : 3 * DA]
    du_ref[:, 3 * DA :] = sums_ref[:, 3 * DA :] * slope(gate_b)
    pairs = pair_norm(pair_ref[...].astype(F32))
    slopes = slopes_ref[...].reshape(8, 4, 32, 128)
    for h in range(4):
        own = slopes[:, h].reshape(256, 128)
        for c in range(16):
            dpair_ref[16 * h + c : 16 * h + c + 1, :] = jnp.sum(own * pairs[c], axis=0, keepdims=True)


def atom_back(*args):
    sds = jax.ShapeDtypeStruct
    return kernel_call(
        atom_back_kernel,
        [
            sds((4, 256, DA), BF16), sds((4, 256, DA), BF16), sds((4, 256, 2 * DA), F32),
            sds((4, RIM, 2 * DA), BF16), sds((4, RIM, 2 * DA), BF16), sds((4, 256, DA), F32),
            sds((256, 4 * DA), F32), sds((DA, DA), F32), sds((DA, 2 * FA), F32), sds((FA, DA), F32), sds((64, 128), F32),
        ],
        scratch=[
            pltpu.VMEM((4, 256, DA), F32), pltpu.VMEM((4, SPAN, 2 * DA), F32), pltpu.VMEM((1024, 128), F32),
            pltpu.VMEM((256, 4 * DA), F32), pltpu.VMEM((4, 256, DA), BF16), pltpu.VMEM((4, 256, 2 * FA), BF16),
            pltpu.VMEM((4, 256, DA), BF16),
        ],
        us=12,
        name="atom_back",
    )(*args)


def atom_end_kernel(
    core_ref, dq_ref, dgate_ref, dkv_ref, prev_ref, next_ref, dmid_ref, x_ref, first_ref, u_ref, du_ref, cond_low_ref,
    w_qkvg_ref, dw_out_ref, dw_up_ref, dw_down_ref, dpool_ref, single_ref, tdu_ref, misc_ref,
    out_ref, keep_ref, send_ref,
    dw_qkvg_ref, sums_ref, whole_ref,
):
    scale = sigmoid(part(u_ref, 0, DA))
    sums_ref[...] = jnp.zeros_like(sums_ref)
    dw_qkvg_ref[...] = jnp.zeros_like(dw_qkvg_ref)

    @pl.loop(0, 4)
    def _(s):
        whole_ref[...] = dkv_ref[s]
        whole_ref[:RIM, :] += prev_ref[s].astype(F32)
        whole_ref[256 - RIM :, :] += next_ref[s].astype(F32)
        grads = jnp.concatenate([dq_ref[s], whole_ref[...].astype(BF16), dgate_ref[s]], axis=1)
        dfirst = dot(grads, w_qkvg_ref[...], ((1,), (1,)))
        lines, inverse = normed(x_ref[s].astype(F32))
        out_ref[s] = dmid_ref[s] + norm_back_rows(dfirst * scale, lines, inverse)
        dw_qkvg_ref[...] += dot(first_ref[s], grads, ((0,), (0,)))
        sums_ref[:, :DA] += dfirst * lines
        sums_ref[:, DA:] += dfirst

    du = jnp.concatenate([sums_ref[:, :DA] * slope(scale), sums_ref[:, DA:], du_ref[...]], axis=1).astype(BF16)
    dw_cond = dot(cond_low_ref[...], du, ((0,), (0,)))
    down = dw_down_ref[...].reshape(16, 2, 8, DA)
    single = dot(single_ref[...], tdu_ref[...], ((0,), (0,))).reshape(16, 3, 8, 2 * DT)
    whole = jnp.concatenate(
        [
            dw_cond, dw_qkvg_ref[...], dw_out_ref[...], dw_up_ref[...], dpool_ref[...],
            down[:, 0].reshape(DA, DA), down[:, 1].reshape(DA, DA), misc_ref[...].astype(F32),
        ]
        + [single[:, i].reshape(DA, 2 * DT) for i in range(3)]
        + [jnp.zeros((DA, 512), F32)],
        axis=1,
    )
    even = core_ref[0] == 0
    for s in range(8):
        rows = whole[:, 1024 * s : 1024 * s + 1024].reshape(8, 2, 8, 1024)
        first, second = rows[:, 0].reshape(64, 1024), rows[:, 1].reshape(64, 1024)
        keep_ref[s] = jnp.where(even, first, second).astype(BF16)
        send_ref[s] = jnp.where(even, second, first).astype(BF16)


def atom_end(*args):
    sds = jax.ShapeDtypeStruct
    return kernel_call(
        atom_end_kernel,
        [sds((4, 256, DA), F32), sds((8, 64, 1024), BF16), sds((8, 64, 1024), BF16)],
        in_specs=[pl.BlockSpec((256, DA), lambda *_: (0, 0)) if i == 8 else fixed(*a.shape) for i, a in enumerate(args[1:])],
        scratch=[pltpu.VMEM((DA, 4 * DA), F32), pltpu.VMEM((256, 2 * DA), F32), pltpu.VMEM((256, 2 * DA), F32)],
        scalars=1,
        us=6,
        arrived=(3, 4),
        name="atom_end",
    )(*args)


SHARE = 960


def split_kernel(samp_ref, wide_ref, heads_ref, *refs):
    out_refs, whole_ref = refs[:4], refs[4]
    for s in range(8):
        pieces = [wide_ref[:, SHARE * s : SHARE * s + SHARE].astype(F32)]
        pieces += [heads_ref[2 * s + i, 64:, : 3 * HS].astype(F32) for i in range(2)]
        whole_ref[s] = jnp.concatenate(pieces + [jnp.zeros((48, 32), F32)], axis=1).astype(BF16)
    for k in range(8):
        out_refs[k // 2][k % 2] = whole_ref[samp_ref[0] ^ k]


def split(samp, wide, heads):
    return kernel_call(
        split_kernel,
        [jax.ShapeDtypeStruct((2, 48, 1280), BF16)] * 4,
        scratch=[pltpu.VMEM((8, 48, 1280), BF16)],
        scalars=1,
        us=3,
        arrived=(0, 1),
        name="split",
    )(samp, wide, heads)


def collect_kernel(wide_ref, wide_part_ref, packed_ref, out_ref, total_ref):
    step = pl.program_id(0)

    @pl.when(step == 0)
    def _():
        total_ref[...] = jnp.zeros_like(total_ref)

    rows = packed_ref[0].astype(F32)
    for i in range(1, 16):
        rows += packed_ref[i].astype(F32)
    total_ref[:, :1024] += rows

    @pl.when(step == 3)
    def _():
        wide = wide_ref[...].astype(F32) + wide_part_ref[...].astype(F32)
        whole = jnp.concatenate([wide, total_ref[...]], axis=0).astype(BF16)
        for i in range(8):
            out_ref[i] = whole


def collect(wide, wide_part, packed):
    return kernel_call(
        collect_kernel,
        [jax.ShapeDtypeStruct((8, 56, 1280), BF16)],
        grid=(4,),
        in_specs=[fixed(48, 1280), fixed(48, 1280), pl.BlockSpec((16, 8, 1024), lambda i: (i, 0, 0))],
        out_specs=[fixed(8, 56, 1280)],
        scratch=[pltpu.VMEM((8, 1280), F32)],
        us=4,
        arrived=(0, 1, 2),
        name="collect",
    )(wide, wide_part, packed)[0]


def hand_out_kernel(
    parts_ref, a_cond_ref, a_qkvg_ref, a_out_ref, a_up_ref, a_down_ref, a_pair_ref, pool_ref, t_cond_ref, t_qkvg_ref,
    t_out_ref, t_up_ref, t_down_ref, t_pair_ref,
):
    def cut(first, last, rows, share):
        pieces = []
        while first < last:
            s, at = divmod(first, share)
            end = min(last - share * s, share)
            pieces.append(parts_ref[s, rows, at:end].astype(F32))
            first = share * s + end
        return jnp.concatenate(pieces, axis=1)

    def wide(first, last):
        return cut(first, last, slice(0, 48), SHARE)

    def atoms(first, last):
        return cut(first, last, slice(48, 56), 1024)

    t_up_ref[...] = wide(0, 4 * DT)
    t_out_ref[...] = wide(4 * DT, 5 * DT)
    t_qkvg_ref[:, 3 * DT :] = wide(5 * DT, 6 * DT)
    t_down_ref[:48, :] = wide(6 * DT, 7 * DT)
    t_down_ref[48:, :] = wide(7 * DT, 8 * DT)
    conds = wide(8 * DT, 10 * DT)
    t_cond_ref[:, 2 * DT : 4 * DT] = conds[:24]
    t_cond_ref[:, 4 * DT :] = conds[24:]
    for i in range(3):
        t_cond_ref[8 * i : 8 * i + 8, : 2 * DT] = atoms(3072 + 2 * DT * i, 3072 + 2 * DT * (i + 1))
    a_cond_ref[...] = atoms(0, 768)
    a_qkvg_ref[...] = atoms(768, 1280)
    a_out_ref[...] = atoms(1280, 1408)
    a_up_ref[...] = atoms(1408, 1920)
    pool_ref[...] = atoms(1920, 2688)
    a_down_ref[:8] = atoms(2688, 2816)
    a_down_ref[8:] = atoms(2816, 2944)
    misc = atoms(2944, 3072)
    t_pair_ref[...] = misc[0:1]
    a_pair_ref[...] = misc[1:2, :4]
    heads = []
    for h in range(16):
        at = SHARE + 3 * HS * (h % 2)
        heads.append(parts_ref[h // 2, :48, at : at + 3 * HS].astype(F32))
    for i in range(3):
        t_qkvg_ref[:, DT * i : DT * i + DT] = jnp.concatenate(
            [head[:, HS * i : HS * i + HS] for head in heads], axis=1
        )


def hand_out(parts):
    sds = jax.ShapeDtypeStruct
    shapes = [
        (8, 768), (8, 512), (8, 128), (8, 512), (16, 128), (1, 4), (8, 768), (24, 6 * DT), (48, 4 * DT), (48, DT),
        (48, 2 * FT), (96, DT), (1, 128),
    ]
    return kernel_call(
        hand_out_kernel,
        [sds(shape, F32) for shape in shapes],
        us=4,
        arrived=(0,),
        name="hand_out",
    )(parts)


def both_axes(x):
    return lax.all_to_all(x, ("samp", "seq"), 0, 0, tiled=True)


def along_seq(x):
    return lax.all_to_all(x, "seq", 0, 0, tiled=True)


ordered = lambda *x: lax.optimization_barrier(x)


def from_samp(part, k):
    return lax.ppermute(part, "samp", [(i, i ^ k) for i in range(8)])


def total(*parts):
    return sum(part.astype(F32) for part in parts).astype(BF16)


def body(
    atom_in,
    tok_in,
    atom_cond,
    single_cond,
    atom_pair,
    token_pair,
    atom_w_cond,
    atom_w_qkvg,
    atom_w_out,
    atom_w_up,
    atom_w_down,
    atom_w_pair,
    pool_weight,
    token_w_cond,
    token_w_qkvg,
    token_w_out,
    token_w_up,
    token_w_down,
    token_w_pair,
    cotangent,
):
    samp, seq = lax.axis_index("samp"), lax.axis_index("seq")
    up, down = [(i, i + 1) for i in range(15)], [(i + 1, i) for i in range(15)]
    rims = jnp.concatenate([atom_in, atom_cond[None]], axis=0)
    from_prev = lax.ppermute(rims[:, 256 - RIM :], "seq", up)
    from_next = lax.ppermute(rims[:, :RIM], "seq", down)
    samp = samp.astype(jnp.int32).reshape(1)
    token_bias = pair_bias(samp, token_pair, token_w_pair)
    token_bias = along_seq(token_bias).reshape(NT, 128)
    atom_in, token_bias = ordered(atom_in, token_bias)
    token_bias = lax.all_gather(token_bias, "samp", axis=0, axis_index_groups=[SAMP_RING])

    key_index = 256 * seq - RIM + 32 * jnp.arange(8)[:, None] + jnp.arange(128)[None, :]
    mask = jnp.where((key_index >= 0) & (key_index < 4096), 0.0, masked).astype(F32)
    (
        first, query, keyval, probs, gate, attended, middle, cond_low, cond_proj, pooled,
        start, tfirst, tgate, tcond_proj, single_low, runs,
    ) = front(
        atom_in, from_prev, from_next, atom_cond, atom_pair, mask, atom_w_pair.astype(F32), atom_w_cond,
        atom_w_qkvg, atom_w_out, atom_w_up, atom_w_down, pool_weight, tok_in, single_cond, token_w_cond, token_w_qkvg,
    )
    prep = atom_prep(cond_proj, middle, gate, attended, atom_w_out, atom_w_up, atom_w_down)
    normed_pair = pair_normed(samp, token_pair)
    runs, normed_pair, sent, *prep = ordered(along_seq(runs), normed_pair, tfirst, *prep)
    qkv, tprobs, tattended = token_attention(runs, token_bias)
    lines = lax.all_gather(sent, "seq", axis=0, axis_index_groups=[RING])
    (
        token_out, cots, tdgate, tdmid, gated, gbranch, second, dup, hidden, gdown, tdu,
    ) = turn(
        along_seq(tattended), tgate, start, tcond_proj, cotangent, token_w_out, token_w_up, token_w_down
    )
    cots = along_seq(cots)
    wide = token_weights(gated, gbranch, tfirst, tdgate, second, dup, hidden, gdown, single_low, tdu)
    cots, wide = ordered(cots, wide)
    wide = lax.psum_scatter(wide, "seq", scatter_dimension=0, tiled=True, axis_index_groups=[RING])
    tgrads, *slopes = token_attention_back(samp, qkv, tprobs, cots)
    heads = head_weights(tgrads, lines)
    received = [from_samp(slopes[k], 2 * k) for k in range(1, 4)]
    tgrads, heads = ordered(along_seq(tgrads), heads)
    grad_tok, gpooled, dpool, tdu = back(
        tgrads, tdgate, tdmid, start, tcond_proj, token_w_qkvg, pool_weight, pooled
    )
    gpooled, *received = ordered(gpooled, *received)
    slopes = total(slopes[0], *received)
    slopes = along_seq(jnp.concatenate([slopes, heads], axis=1))
    (
        dquery, dgate, dkeyval, to_prev, to_next, dmid, du, dw_out, dw_up, dw_down, dpair,
    ) = atom_back(
        gpooled.reshape(4, 64, DA), cond_proj, middle, gate, attended, query, keyval, probs, atom_pair,
        atom_w_out, atom_w_up, atom_w_down, *prep,
    )
    back_next = lax.ppermute(to_prev, "seq", down)
    back_prev = lax.ppermute(to_next, "seq", up)
    misc = pair_grad(slopes, normed_pair, dpair)
    grad_atoms, packed, beside = atom_end(
        (seq % 2).astype(jnp.int32).reshape(1),
        dquery, dgate, dkeyval, back_prev, back_next, dmid, atom_in, first, cond_proj, du, cond_low,
        atom_w_qkvg, dw_out, dw_up, dw_down, dpool, single_low, tdu, misc,
    )
    packed = total(packed, lax.ppermute(beside, "seq", [(i, i ^ 1) for i in range(16)])).reshape(64, 8, 1024)
    _, wide = ordered(packed, wide)
    chips = [[core + 2 * i for i in range(64)] for core in range(2)]
    packed = lax.all_to_all(packed, ("samp", "seq"), 0, 0, tiled=True, axis_index_groups=chips)
    wide = split(samp, wide, slopes)
    wide = total(wide[0], *[from_samp(wide[k], 2 * k) for k in range(1, 4)])
    wide = wide[0], from_samp(wide[1], 1)
    parts = lax.all_to_all(collect(*wide, packed), "samp", 0, 0, tiled=True)
    return (token_out, grad_atoms, grad_tok, *hand_out(parts))


def solution(mesh):
    rows, both, whole = P("seq", None), P("samp", "seq", None), P()
    in_specs = (both, both, rows, rows, P(None, "seq", None), P(None, "seq", None)) + (whole,) * 13 + (both,)
    out_specs = (both,) * 3 + (rows,) * 13
    mapped = jax.shard_map(body, mesh=mesh, in_specs=in_specs, out_specs=out_specs, check_vma=False)

    def run(*args):
        with jax.sharding.use_abstract_mesh(mesh.abstract_mesh):
            return mapped(*args)

    return run
```

```python
import jax
import jax.numpy as jnp
from jax import lax
from jax.experimental import pallas as pl
from jax.experimental.pallas import tpu as pltpu
from jax.sharding import PartitionSpec as P

eps = 1e-05
masked = -1000000000.0

MIB = 1 << 20
LIMIT = 44
F32, BF16 = jnp.float32, jnp.bfloat16


def kernel_call(
    kernel, out_shape, grid=(1,), in_specs=None, out_specs=None, scratch=(), scalars=0, arrived=(), us=1, name=None
):
    def run(*args):
        ins = list(in_specs or [fixed(*a.shape) for a in args[scalars:]])
        outs = list(out_specs or [fixed(*o.shape) for o in out_shape])
        args = list(args)
        for i in range(len(ins)):
            if i not in arrived and ins[i].memory_space in (None, pl.ANY):
                args[scalars + i] = pltpu.with_memory_space_constraint(args[scalars + i], pltpu.HBM)
        return pl.pallas_call(
            kernel,
            out_shape=[pltpu.HBM(o.shape, o.dtype) for o in out_shape],
            grid_spec=pltpu.PrefetchScalarGridSpec(
                num_scalar_prefetch=scalars, grid=grid, in_specs=ins, out_specs=outs, scratch_shapes=list(scratch)
            ),
            compiler_params=pltpu.CompilerParams(vmem_limit_bytes=LIMIT * MIB),
            cost_estimate=pl.CostEstimate(flops=us << 28, bytes_accessed=us << 20, transcendentals=0),
            name=name,
        )(*args)

    return run


def fixed(*shape):
    return pl.BlockSpec(shape, lambda *_: (0,) * len(shape), pipeline_mode=pl.Buffered(1))


def dot(left, right, over=((1,), (0,))):
    return lax.dot_general(left, right, (over, ((), ())), preferred_element_type=F32)


def swap_halves(first, second):
    low = lax.broadcasted_iota(jnp.int32, first.shape, 1) < 64
    half = first.shape[1] // 2
    return (
        jnp.where(low, first, pltpu.roll(second, half, 1)),
        jnp.where(low, pltpu.roll(first, half, 1), second),
    )


def runs_to_tokens(runs_ref, tokens_ref):
    for pair in range(runs_ref.shape[0] // 2):
        for duo in range(2):
            lanes = slice(128 * duo, 128 * duo + 128)
            made = swap_halves(
                runs_ref[2 * pair, :, lanes].astype(F32), runs_ref[2 * pair + 1, :, lanes].astype(F32)
            )
            for k in range(2):
                tokens_ref[2 * duo + k, :, 128 * pair : 128 * pair + 128] = made[k].astype(
                    tokens_ref.dtype
                )


def tokens_to_runs(tokens_ref, runs_ref):
    for pair in range(runs_ref.shape[0] // 2):
        lanes = slice(128 * pair, 128 * pair + 128)
        for duo in range(2):
            made = swap_halves(tokens_ref[2 * duo, :, lanes], tokens_ref[2 * duo + 1, :, lanes])
            for k in range(2):
                runs_ref[2 * pair + k, :, 128 * duo : 128 * duo + 128] = made[k].astype(runs_ref.dtype)


HS = 48
NT = 1024
QB = 256
SAMP_RING = [0, 2, 4, 6, 7, 5, 3, 1]


def attention_kernel(runs_ref, bias_ref, qkv_ref, probs_ref, out_ref, heads_ref):
    sample = pl.program_id(0)

    @pl.when(sample == 0)
    def _():
        runs_to_tokens(runs_ref, qkv_ref)

    keys = qkv_ref[sample, HS : 2 * HS, :]
    values = qkv_ref[sample, 2 * HS :, :]

    def scores_of(block):
        rows = slice(block * QB, block * QB + QB)
        made = dot(qkv_ref[sample, :HS, rows], keys, ((0,), (0,))) * HS ** (-0.5)
        return made + jnp.concatenate([bias_ref[SAMP_RING.index(i), rows, :] for i in range(8)], axis=1).astype(F32)

    count = NT // QB
    ahead = scores_of(0)
    for block in range(count):
        rows = slice(block * QB, block * QB + QB)
        scores = ahead
        if block + 1 < count:
            ahead = scores_of(block + 1)
        exponent = jnp.exp(scores - jnp.max(scores, axis=1, keepdims=True))
        probs = (exponent * (1.0 / jnp.sum(exponent, axis=1, keepdims=True))).astype(BF16)
        probs_ref[0, rows, :] = probs
        heads_ref[sample, :, rows] = dot(probs, values, ((1,), (1,))).T

    @pl.when(sample == 3)
    def _():
        tokens_to_runs(heads_ref, out_ref)


def token_attention(runs, bias):
    return kernel_call(
        attention_kernel,
        [
            jax.ShapeDtypeStruct((4, 3 * HS, NT), BF16),
            jax.ShapeDtypeStruct((4, NT, NT), BF16),
            jax.ShapeDtypeStruct((16, HS, 256), BF16),
        ],
        grid=(4,),
        in_specs=[fixed(16, 3 * HS, 256)] + [fixed(8, NT, 128)],
        out_specs=[
            fixed(4, 3 * HS, NT), pl.BlockSpec((1, NT, NT), lambda s: (s, 0, 0)), fixed(16, HS, 256),
        ],
        scratch=[pltpu.VMEM((4, HS, NT), F32)],
        us=13,
        arrived=(0,),
        name="token_attention",
    )(runs, bias)


def attention_back_kernel(samp_ref, qkv_ref, probs_ref, cot_ref, out_ref, *refs):
    pair_refs, (cots_ref, grads_ref, total_ref) = refs[:4], refs[4:]
    sample = pl.program_id(0)

    @pl.when(sample == 0)
    def _():
        runs_to_tokens(cot_ref, cots_ref)
        total_ref[...] = jnp.zeros_like(total_ref)

    keys = qkv_ref[sample, HS : 2 * HS, :]
    values = qkv_ref[sample, 2 * HS :, :]

    def weights_of(block):
        return dot(cots_ref[sample, :, block * QB : block * QB + QB], values, ((0,), (0,)))

    key_grad, value_grad = 0.0, 0.0
    count = NT // QB
    ahead = weights_of(0)
    for block in range(count):
        rows = slice(block * QB, block * QB + QB)
        now = ahead
        if block + 1 < count:
            ahead = weights_of(block + 1)
        low = probs_ref[0, rows, :]
        probs = low.astype(F32)
        weighed = probs * now
        slopes = weighed - probs * jnp.sum(weighed, axis=1, keepdims=True)
        slopes_low = slopes.astype(BF16)
        total_ref[rows, :] += slopes
        grads_ref[sample, :HS, rows] = dot(keys, slopes_low, ((1,), (1,))) * HS ** (-0.5)
        key_grad += dot(qkv_ref[sample, :HS, rows], slopes_low)
        value_grad += dot(cots_ref[sample, :, rows], low)
    grads_ref[sample, HS : 2 * HS, :] = key_grad * HS ** (-0.5)
    grads_ref[sample, 2 * HS :, :] = value_grad

    @pl.when(sample == 3)
    def _():
        tokens_to_runs(grads_ref, out_ref)
        for k in range(4):
            lanes = pl.ds(pl.multiple_of(((samp_ref[0] // 2) ^ k) * 256, 256), 256)
            pair_refs[k][...] = total_ref[:, lanes].astype(BF16).reshape(16, 64, 256)


def token_attention_back(samp, qkv, probs, cots):
    return kernel_call(
        attention_back_kernel,
        [jax.ShapeDtypeStruct((16, 3 * HS, 256), BF16)] + [jax.ShapeDtypeStruct((16, 64, 256), BF16)] * 4,
        grid=(4,),
        in_specs=[fixed(4, 3 * HS, NT), pl.BlockSpec((1, NT, NT), lambda s, _: (s, 0, 0)), fixed(16, HS, 256)],
        out_specs=[fixed(16, 3 * HS, 256)] + [fixed(16, 64, 256)] * 4,
        scratch=[
            pltpu.VMEM((4, HS, NT), BF16),
            pltpu.VMEM((4, 3 * HS, NT), F32),
            pltpu.VMEM((NT, NT), F32),
        ],
        scalars=1,
        us=14,
        arrived=(2,),
        name="token_attention_back",
    )(samp, qkv, probs, cots)


def normed_rows(pair_ref):
    pair = pair_ref[...].astype(F32)
    centred = pair - jnp.mean(pair, axis=0, keepdims=True)
    inverse = lax.rsqrt(jnp.mean(centred * centred, axis=0, keepdims=True) + eps)
    return jnp.swapaxes((centred * inverse).astype(BF16), 0, 1)


def pair_kernel(samp_ref, pair_ref, weight_ref, bias_ref):
    low = normed_rows(pair_ref)
    weight = weight_ref[...]
    bias = jnp.stack([dot(weight, low[i]) for i in range(low.shape[0])], axis=0)
    bias_ref[...] = jnp.swapaxes(bias, 0, 1).astype(BF16)


def pair_bias(samp, pair, weight):
    return kernel_call(
        pair_kernel,
        [jax.ShapeDtypeStruct((16, 64, 128), BF16)],
        grid=(2,),
        in_specs=[pl.BlockSpec((128, 32, 128), lambda i, samp: (0, i, samp[0])), fixed(16, 128)],
        out_specs=[pl.BlockSpec((16, 32, 128), lambda i, _: (0, i, 0))],
        scalars=1,
        us=4,
        name="pair_bias",
    )(samp, pair, weight)[0]


def pair_norm_kernel(samp_ref, pair_ref, normed_ref):
    normed_ref[...] = normed_rows(pair_ref)


def pair_normed(samp, pair):
    return kernel_call(
        pair_norm_kernel,
        [jax.ShapeDtypeStruct((64, 128, 256), BF16)],
        grid=(4,),
        in_specs=[pl.BlockSpec((128, 16, 256), lambda i, samp: (0, i, samp[0] // 2))],
        out_specs=[pl.BlockSpec((16, 128, 256), lambda i, _: (i, 0, 0))],
        scalars=1,
        us=6,
        name="pair_normed",
    )(samp, pair)[0]


def pair_back_kernel(slopes_ref, normed_ref, atoms_ref, out_ref, grad_ref):
    step = pl.program_id(0)
    slopes = jnp.swapaxes(slopes_ref[...], 0, 1)
    made = dot(slopes[0], normed_ref[0], ((1,), (1,)))
    for i in range(1, slopes.shape[0]):
        made += dot(slopes[i], normed_ref[i], ((1,), (1,)))

    @pl.when(step == 0)
    def _():
        grad_ref[...] = made

    @pl.when(step > 0)
    def _():
        grad_ref[...] += made

    @pl.when(step == 3)
    def _():
        atoms = jnp.sum(atoms_ref[...], axis=1, keepdims=True)
        lane = lax.broadcasted_iota(jnp.int32, (16, 128), 1)
        rows = jnp.where(lane == 0, atoms[:16], 0.0)
        for h in range(1, 4):
            rows += jnp.where(lane == h, atoms[16 * h : 16 * h + 16], 0.0)
        line = lax.broadcasted_iota(jnp.int32, (16, 8, 128), 1)
        both = jnp.where(line == 0, grad_ref[...][:, None, :], 0.0) + jnp.where(line == 1, rows[:, None, :], 0.0)
        out_ref[...] = both.reshape(128, 128).astype(BF16)


def pair_grad(slopes, normed, atoms):
    return kernel_call(
        pair_back_kernel,
        [jax.ShapeDtypeStruct((128, 128), BF16)],
        grid=(4,),
        in_specs=[
            pl.BlockSpec((16, 16, 256), lambda i: (0, i, 0)),
            pl.BlockSpec((16, 128, 256), lambda i: (i, 0, 0)),
            fixed(64, 128),
        ],
        out_specs=[fixed(128, 128)],
        scratch=[pltpu.VMEM((16, 128), F32)],
        arrived=(0,),
        us=6,
        name="pair_grad",
    )(slopes, normed, atoms)[0]


DA, DT, FT, FA = 128, 768, 1536, 256
RIM = 48
RING = [0, 1, 4, 5, 8, 9, 12, 13, 14, 15, 10, 11, 6, 7, 2, 3]
SPAN = 256 + 2 * RIM


def normed(x):
    centred = x - jnp.mean(x, axis=-1, keepdims=True)
    inverse = lax.rsqrt(jnp.mean(centred * centred, axis=-1, keepdims=True) + eps)
    return centred * inverse, inverse


def sigmoid(x):
    return 1.0 / (1.0 + jnp.exp(-x))


def own_head():
    shape = (1, 4, 32, 128)
    return lax.broadcasted_iota(jnp.int32, shape, 3) // 32 == lax.broadcasted_iota(jnp.int32, shape, 1)


def head_rows(rows):
    return jnp.where(own_head(), rows.reshape(8, 1, 32, 128), 0.0).reshape(1024, 128).astype(BF16)


def rows_of_heads(full):
    return jnp.sum(jnp.where(own_head(), full.reshape(8, 4, 32, 128), 0.0), axis=1).reshape(256, 128)


def by_window(made):
    return jnp.concatenate([made(w) for w in range(8)], axis=0)


def pair_norm(pair):
    centred = pair - jnp.mean(pair, axis=0, keepdims=True)
    inverse = lax.rsqrt(jnp.mean(centred * centred, axis=0, keepdims=True) + eps)
    return (centred * inverse).astype(BF16).astype(F32)


def part(ref, i, width, rows=slice(None)):
    return ref[rows, i * width : (i + 1) * width]


def front_kernel(
    x_ref, prev_ref, next_ref, cond_ref, pair_ref, mask_ref, w_pair_ref, w_cond_ref, w_qkvg_ref, w_out_ref,
    w_up_ref, w_down_ref, pool_ref, tok_ref, single_ref, tw_cond_hbm, tw_qkvg_hbm,
    first_ref, q_ref, kv_ref, probs_ref, gate_ref, att_ref, mid_ref, cond_low_ref, u_ref, pooled_ref,
    start_ref, tfirst_ref, tgate_ref, tu_ref, single_low_ref, runs_ref,
    bias_ref, y_ref, uh_ref, tw_cond_ref, tw_qkvg_ref, sems,
):
    loads = [
        pltpu.make_async_copy(tw_cond_hbm, tw_cond_ref, sems.at[0]),
        pltpu.make_async_copy(tw_qkvg_hbm, tw_qkvg_ref, sems.at[1]),
    ]
    for load in loads:
        load.start()
    cond = jnp.concatenate([prev_ref[4], cond_ref[...], next_ref[4]], axis=0).astype(F32)
    cond_low = normed(cond)[0].astype(BF16)
    cond_low_ref[...] = cond_low[RIM : RIM + 256]
    u_ref[...] = dot(cond_low[RIM : RIM + 256], w_cond_ref[...])
    uh_ref[...] = dot(cond_low, w_cond_ref[:, : 2 * DA])
    pairs = pair_norm(pair_ref[...].astype(F32))
    for h in range(4):
        bias = pairs[0] * w_pair_ref[0, h]
        for c in range(1, 16):
            bias += pairs[c] * w_pair_ref[c, h]
        for w in range(8):
            at = 128 * w + 32 * h
            bias_ref[at : at + 32, :] = bias[32 * w : 32 * w + 32] + mask_ref[w : w + 1, :]

    scale_a, shift_a = sigmoid(part(uh_ref, 0, DA)), part(uh_ref, 1, DA)
    gate_a, scale_b, shift_b, gate_b = (
        sigmoid(part(u_ref, 2, DA)), sigmoid(part(u_ref, 3, DA)), part(u_ref, 4, DA), sigmoid(part(u_ref, 5, DA)),
    )

    def atoms(s):
        x = jnp.concatenate([prev_ref[s], x_ref[s], next_ref[s]], axis=0).astype(F32)
        first = (scale_a * normed(x)[0] + shift_a).astype(BF16)
        projected = dot(first, w_qkvg_ref[...])
        own = projected[RIM : RIM + 256]
        first_ref[s] = first[RIM : RIM + 256]
        query = own[:, :DA].astype(BF16)
        q_ref[s] = query
        keys = projected[:, DA : 2 * DA].astype(BF16)
        values = projected[:, 2 * DA : 3 * DA].astype(BF16)
        kv_ref[s, :, :DA] = keys
        kv_ref[s, :, DA:] = values
        gate = sigmoid(own[:, 3 * DA :])
        gate_ref[s] = gate
        rows = head_rows(query.astype(F32))
        scores = by_window(lambda w: dot(rows[128 * w : 128 * w + 128], keys[32 * w : 32 * w + 128], ((1,), (1,))))
        scores = scores * 32 ** (-0.5) + bias_ref[...]
        exponent = jnp.exp(scores - jnp.max(scores, axis=1, keepdims=True))
        probs = (exponent * (1.0 / jnp.sum(exponent, axis=1, keepdims=True))).astype(BF16)
        probs_ref[s] = probs
        attended = rows_of_heads(
            by_window(lambda w: dot(probs[128 * w : 128 * w + 128], values[32 * w : 32 * w + 128]))
        )
        att_ref[s] = attended
        branch = dot((gate * attended).astype(BF16), w_out_ref[...])
        middle = x[RIM : RIM + 256] + gate_a * branch
        mid_ref[s] = middle
        second = (scale_b * normed(middle)[0] + shift_b).astype(BF16)
        up = dot(second, w_up_ref[...])
        hidden = (up[:, :FA] * sigmoid(up[:, :FA]) * up[:, FA:]).astype(BF16)
        y_ref[s] = middle + gate_b * dot(hidden, w_down_ref[...])
        pooled = y_ref[s, pl.ds(0, 64, stride=4), :]
        for k in range(1, 4):
            pooled += y_ref[s, pl.ds(k, 64, stride=4), :]
        pooled_ref[s] = (pooled * 0.25).astype(BF16)

    for s in range(4):
        atoms(s)

    for load in loads:
        load.wait()
    single_low = normed(single_ref[...].astype(F32))[0].astype(BF16)
    single_low_ref[...] = single_low
    for i in range(6):
        tu_ref[:, DT * i : DT * i + DT] = dot(single_low, tw_cond_ref[:, DT * i : DT * i + DT])
    pooled = pooled_ref[...].reshape(256, DA)
    start = tok_ref[...].reshape(256, DT).astype(F32) + dot(pooled, pool_ref[...])
    start_ref[...] = start
    lines = normed(start)[0]
    scale, shift = sigmoid(part(tu_ref, 0, DT)), part(tu_ref, 1, DT)
    for s in range(4):
        tfirst_ref[64 * s : 64 * s + 64, :] = (scale * lines[64 * s : 64 * s + 64] + shift).astype(BF16)
    first = tfirst_ref[...]
    for i in range(3):
        turned = dot(first, part(tw_qkvg_ref, i, DT)).T.astype(BF16)
        for h in range(16):
            runs_ref[h, HS * i : HS * i + HS, :] = turned[HS * h : HS * h + HS]
    tgate_ref[...] = sigmoid(dot(first, part(tw_qkvg_ref, 3, DT)))


def front(*args):
    sds = jax.ShapeDtypeStruct
    specs = [fixed(*a.shape) for a in args]
    specs[6] = pl.BlockSpec(memory_space=pltpu.SMEM)
    specs[15] = specs[16] = pl.BlockSpec(memory_space=pl.ANY)
    return kernel_call(
        front_kernel,
        [
            sds((4, 256, DA), BF16), sds((4, 256, DA), BF16), sds((4, SPAN, 2 * DA), BF16),
            sds((4, 1024, 128), BF16), sds((4, 256, DA), F32), sds((4, 256, DA), F32),
            sds((4, 256, DA), F32), sds((256, DA), BF16), sds((256, 6 * DA), F32), sds((4, 64, DA), BF16),
            sds((256, DT), F32), sds((256, DT), BF16), sds((256, DT), F32), sds((64, 6 * DT), F32),
            sds((64, 384), BF16), sds((16, 3 * HS, 256), BF16),
        ],
        in_specs=specs,
        scratch=[
            pltpu.VMEM((1024, 128), F32), pltpu.VMEM((4, 256, DA), F32), pltpu.VMEM((SPAN, 2 * DA), F32),
            pltpu.VMEM((384, 6 * DT), BF16), pltpu.VMEM((DT, 4 * DT), BF16), pltpu.SemaphoreType.DMA((2,)),
        ],
        us=24,
        arrived=(1, 2),
        name="front",
    )(*args)


def slope(squashed):
    return squashed * (1.0 - squashed)


def norm_back_rows(gradient, lines, inverse):
    return inverse * (
        gradient
        - jnp.mean(gradient, axis=-1, keepdims=True)
        - lines * jnp.mean(gradient * lines, axis=-1, keepdims=True)
    )


def turn_kernel(
    runs_ref, tgate_ref, start_ref, tu_ref, cot_ref, w_out_hbm, w_up_hbm, w_down_hbm,
    out_ref, cots_ref, dgate_ref, dmid_ref, a_ref, gbranch_ref, second_ref, dup_ref, hidden_ref, gdown_ref,
    du_ref,
    up_ref, mid_ref, branch_ref, down_ref, w_out_ref, w_up_ref, w_down_ref, sems,
):
    loads = [
        pltpu.make_async_copy(w_out_hbm, w_out_ref, sems.at[0]),
        pltpu.make_async_copy(w_up_hbm, w_up_ref, sems.at[1]),
        pltpu.make_async_copy(w_down_hbm, w_down_ref, sems.at[2]),
    ]
    for load in loads:
        load.start()
    attended = runs_ref[...].reshape(DT, 256).astype(F32).T
    gate = tgate_ref[...]
    gated = (gate * attended).astype(BF16)
    a_ref[...] = gated
    loads[0].wait()
    branch_ref[...] = dot(gated, w_out_ref[...])
    gate_a, scale_b, shift_b, gate_b = (
        sigmoid(part(tu_ref, 2, DT)), sigmoid(part(tu_ref, 3, DT)), part(tu_ref, 4, DT), sigmoid(part(tu_ref, 5, DT)),
    )
    runs = [slice(64 * s, 64 * s + 64) for s in range(4)]
    for r in runs:
        middle = start_ref[r, :] + gate_a * branch_ref[r, :]
        mid_ref[r, :] = middle
        second_ref[r, :] = (scale_b * normed(middle)[0] + shift_b).astype(BF16)
    second = second_ref[...]
    loads[1].wait()
    loads[2].wait()
    cut = 768
    for j in range(FT // cut):
        e = dot(second, w_up_ref[:, cut * j : cut * j + cut])
        f = dot(second, w_up_ref[:, FT + cut * j : FT + cut * j + cut])
        up_ref[:, cut * j : cut * j + cut] = e
        up_ref[:, FT + cut * j : FT + cut * j + cut] = f
        hidden = (e * sigmoid(e) * f).astype(BF16)
        hidden_ref[:, cut * j : cut * j + cut] = hidden
        piece = dot(hidden, w_down_ref[cut * j : cut * j + cut, :])
        if j == 0:
            down_ref[...] = piece
        else:
            down_ref[...] += piece
    total = jnp.zeros((64, DT), F32)
    for s, r in enumerate(runs):
        cot = cot_ref[s].astype(F32)
        out_ref[s] = (mid_ref[r, :] + gate_b * down_ref[r, :]).astype(BF16)
        gdown_ref[r, :] = (cot * gate_b).astype(BF16)
        total += cot * down_ref[r, :]
    du_ref[:, 3 * DT :] = (total * slope(gate_b)).astype(BF16)
    gdown = gdown_ref[...]
    dsecond = jnp.zeros((256, DT), F32)
    for j in range(FT // cut):
        dhidden = dot(gdown, w_down_ref[cut * j : cut * j + cut, :], ((1,), (1,)))
        e = up_ref[:, cut * j : cut * j + cut]
        f = up_ref[:, FT + cut * j : FT + cut * j + cut]
        half = sigmoid(e)
        de = (dhidden * f * half * (1.0 + e * (1.0 - half))).astype(BF16)
        df = (dhidden * e * half).astype(BF16)
        dup_ref[:, cut * j : cut * j + cut] = de
        dup_ref[:, FT + cut * j : FT + cut * j + cut] = df
        piece = dot(de, w_up_ref[:, cut * j : cut * j + cut], ((1,), (1,)))
        piece += dot(df, w_up_ref[:, FT + cut * j : FT + cut * j + cut], ((1,), (1,)))
        dsecond += piece
    down_ref[...] = dsecond
    total_a = jnp.zeros((64, DT), F32)
    total_b = jnp.zeros((64, DT), F32)
    total_c = jnp.zeros((64, DT), F32)
    for s, r in enumerate(runs):
        d = down_ref[r, :]
        lines, inverse = normed(mid_ref[r, :])
        dmid = cot_ref[s].astype(F32) + norm_back_rows(d * scale_b, lines, inverse)
        dmid_ref[r, :] = dmid
        gbranch_ref[r, :] = (dmid * gate_a).astype(BF16)
        total_a += dmid * branch_ref[r, :]
        total_b += d * lines
        total_c += d
    du_ref[:, :DT] = (total_a * slope(gate_a)).astype(BF16)
    du_ref[:, DT : 2 * DT] = (total_b * slope(scale_b)).astype(BF16)
    du_ref[:, 2 * DT : 3 * DT] = total_c.astype(BF16)
    dgated = dot(gbranch_ref[...], w_out_ref[...], ((1,), (1,)))
    dgate_ref[...] = (dgated * attended * slope(gate)).astype(BF16)
    cots_ref[...] = (dgated * gate).T.astype(BF16).reshape(16, HS, 256)


def turn(*args):
    sds = jax.ShapeDtypeStruct
    rows = lambda n, t=BF16: sds((256, n), t)
    return kernel_call(
        turn_kernel,
        [
            sds((4, 64, DT), BF16), sds((16, HS, 256), BF16), rows(DT), rows(DT, F32), rows(DT), rows(DT),
            rows(DT), rows(2 * FT), rows(FT), rows(DT), sds((64, 4 * DT), BF16),
        ],
        in_specs=[fixed(*a.shape) for a in args[:5]] + [pl.BlockSpec(memory_space=pl.ANY)] * 3,
        scratch=[pltpu.VMEM((256, 2 * FT), F32)]
        + [pltpu.VMEM((256, DT), F32)] * 3
        + [pltpu.VMEM(a.shape, BF16) for a in args[5:]]
        + [pltpu.SemaphoreType.DMA((3,))],
        us=12,
        arrived=(0,),
        name="turn",
    )(*args)


def weights_kernel(
    a_ref, gbranch_ref, first_ref, dgate_ref, second_ref, dup_ref, hidden_ref, gdown_ref, single_ref, du_ref, out_ref,
):
    step = pl.program_id(0)

    def write(rows, lanes=slice(None)):
        for at, run in enumerate(RING):
            out_ref[48 * at : 48 * at + 48, lanes] = rows[run]

    def square(left, right):
        return dot(left[...], right[...], ((0,), (0,))).astype(BF16)

    @pl.when(step < 2)
    def _():
        write(square(second_ref, dup_ref).reshape(16, 48, FT))

    @pl.when(step == 2)
    def _():
        write(square(a_ref, gbranch_ref).reshape(16, 48, DT), slice(0, DT))
        write(square(first_ref, dgate_ref).reshape(16, 48, DT), slice(DT, FT))

    @pl.when(step == 3)
    def _():
        made = square(hidden_ref, gdown_ref).reshape(16, 2, 48, DT)
        write(made[:, 0], slice(0, DT))
        write(made[:, 1], slice(DT, FT))

    @pl.when(step == 4)
    def _():
        made = dot(single_ref[...], du_ref[...], ((0,), (0,))).reshape(16, 24, 4 * DT)
        write(jnp.concatenate([made[:, :, :FT], made[:, :, FT:]], axis=1).astype(BF16))


def token_weights(*args):
    specs = [fixed(*a.shape) for a in args]
    specs[5] = pl.BlockSpec((256, FT), lambda i: (0, jnp.minimum(i, 1)))
    return kernel_call(
        weights_kernel,
        [jax.ShapeDtypeStruct((DT, 10 * DT), BF16)],
        grid=(5,),
        in_specs=specs,
        out_specs=[pl.BlockSpec((DT, FT), lambda i: (0, i))],
        us=12,
        name="token_weights",
    )(*args)[0]


def head_weights_kernel(grads_ref, lines_ref, out_ref, total_ref):
    step = pl.program_id(0)

    @pl.when(step == 0)
    def _():
        total_ref[...] = jnp.zeros_like(total_ref)

    for k in range(2):
        total_ref[...] += dot(grads_ref[k], lines_ref[k])

    @pl.when(step == 7)
    def _():
        out_ref[:, :, : 3 * HS] = total_ref[...].T.astype(BF16).reshape(16, 48, 3 * HS)
        out_ref[:, :, 3 * HS :] = jnp.zeros((16, 48, 256 - 3 * HS), BF16)


def head_weights(grads, lines):
    return kernel_call(
        head_weights_kernel,
        [jax.ShapeDtypeStruct((16, 48, 256), BF16)],
        grid=(8,),
        in_specs=[
            pl.BlockSpec((2, 3 * HS, 256), lambda i: (jnp.where(i < 4, 2 * i, 15 - 2 * i), 0, 0)),
            pl.BlockSpec((2, 256, DT), lambda i: (i, 0, 0)),
        ],
        out_specs=[fixed(16, 48, 256)],
        scratch=[pltpu.VMEM((3 * HS, DT), F32)],
        us=6,
        name="head_weights",
    )(grads, lines)[0]


def back_kernel(
    runs_ref, dgate_ref, dmid_ref, start_ref, tu_ref, w_qkvg_hbm, pool_ref, pooled_ref,
    out_ref, gpooled_ref, dpool_ref, ducat_ref,
    dfirst_ref, gpool_ref, w_qkvg_ref, sems,
):
    loads = [
        pltpu.make_async_copy(
            w_qkvg_hbm.at[:, DT * i : DT * i + DT], w_qkvg_ref.at[:, DT * i : DT * i + DT], sems.at[i]
        )
        for i in range(4)
    ]
    for i in (3, 0, 1, 2):
        loads[i].start()
    loads[3].wait()
    dfirst = dot(dgate_ref[...], part(w_qkvg_ref, 3, DT), ((1,), (1,)))
    for i in range(3):
        piece = runs_ref[:, HS * i : HS * i + HS, :].reshape(DT, 256)
        loads[i].wait()
        dfirst += dot(piece.astype(F32).T.astype(BF16), part(w_qkvg_ref, i, DT), ((1,), (1,)))
    dfirst_ref[...] = dfirst
    scale = sigmoid(part(tu_ref, 0, DT))
    total_a = jnp.zeros((64, DT), F32)
    total_b = jnp.zeros((64, DT), F32)
    for s in range(4):
        r = slice(64 * s, 64 * s + 64)
        d = dfirst_ref[r, :]
        lines, inverse = normed(start_ref[r, :])
        grad = dmid_ref[r, :] + norm_back_rows(d * scale, lines, inverse)
        out_ref[s] = grad
        gpool_ref[r, :] = grad.astype(BF16)
        total_a += d * lines
        total_b += d
    ducat_ref[:, :DT] = (total_a * slope(scale)).astype(BF16)
    ducat_ref[:, DT : 2 * DT] = total_b.astype(BF16)
    gpool = gpool_ref[...]
    gpooled_ref[...] = dot(gpool, pool_ref[...], ((1,), (1,))) * 0.25
    dpool_ref[...] = dot(pooled_ref[...].reshape(256, DA), gpool, ((0,), (0,)))


def back(*args):
    sds = jax.ShapeDtypeStruct
    return kernel_call(
        back_kernel,
        [sds((4, 64, DT), F32), sds((256, DA), F32), sds((DA, DT), F32), sds((64, 2 * DT), BF16)],
        in_specs=[
            pl.BlockSpec(memory_space=pl.ANY) if i == 5 else fixed(64, 2 * DT) if i == 4 else fixed(*a.shape)
            for i, a in enumerate(args)
        ],
        scratch=[
            pltpu.VMEM((256, DT), F32), pltpu.VMEM((256, DT), BF16), pltpu.VMEM((DT, 4 * DT), BF16),
            pltpu.SemaphoreType.DMA((4,)),
        ],
        us=7,
        arrived=(0,),
        name="back",
    )(*args)


def atom_prep_kernel(
    u_ref, mid_ref, gate_ref, att_ref, w_out_ref, w_up_ref, w_down_ref,
    second_ref, hidden_ref, rate_ref, down_ref, gated_ref, branch_ref, gates_ref,
):
    scale_b, shift_b = sigmoid(part(u_ref, 3, DA)), part(u_ref, 4, DA)
    gates_ref[:, :DA] = sigmoid(part(u_ref, 2, DA))
    gates_ref[:, DA : 2 * DA] = scale_b
    gates_ref[:, 2 * DA :] = sigmoid(part(u_ref, 5, DA))
    for s in range(4):
        second = (scale_b * normed(mid_ref[s])[0] + shift_b).astype(BF16)
        second_ref[s] = second
        up = dot(second, w_up_ref[...])
        e, f = up[:, :FA], up[:, FA:]
        half = sigmoid(e)
        rate_ref[s, :, :FA] = (f * half * (1.0 + e * (1.0 - half))).astype(BF16)
        rate_ref[s, :, FA:] = (e * half).astype(BF16)
        hidden = (e * half * f).astype(BF16)
        hidden_ref[s] = hidden
        down_ref[s] = dot(hidden, w_down_ref[...]).astype(BF16)
        gated = (gate_ref[s] * att_ref[s]).astype(BF16)
        gated_ref[s] = gated
        branch_ref[s] = dot(gated, w_out_ref[...]).astype(BF16)


def atom_prep(*args):
    sds = jax.ShapeDtypeStruct
    return kernel_call(
        atom_prep_kernel,
        [
            sds((4, 256, DA), BF16), sds((4, 256, FA), BF16), sds((4, 256, 2 * FA), BF16), sds((4, 256, DA), BF16),
            sds((4, 256, DA), BF16), sds((4, 256, DA), BF16), sds((256, 3 * DA), F32),
        ],
        us=6,
        name="atom_prep",
    )(*args)


def atom_back_kernel(
    gpooled_ref, gates_ref, mid_ref, gate_ref, att_ref, q_ref, kv_ref, probs_ref, pair_ref, w_out_ref, w_up_ref,
    w_down_ref, second_ref, hidden_ref, rate_ref, down_ref, gated_ref, branch_ref,
    dq_ref, dgate_ref, dkv_ref, prev_ref, next_ref, dmid_ref, du_ref, dw_out_ref, dw_up_ref, dw_down_ref, dpair_ref,
    dy_ref, grads_ref, slopes_ref, sums_ref, gbranch_ref, dup_ref, gdown_ref,
):
    gate_a, scale_b, gate_b = (part(gates_ref, i, DA) for i in range(3))

    def atoms(s):
        for k in range(4):
            dy_ref[s, pl.ds(k, 64, stride=4), :] = gpooled_ref[s]
        dy = dy_ref[s]
        gdown = (dy * gate_b).astype(BF16)
        gdown_ref[s] = gdown
        dhidden = dot(gdown, w_down_ref[...], ((1,), (1,)))
        dup = (jnp.concatenate([dhidden, dhidden], axis=1) * rate_ref[s].astype(F32)).astype(BF16)
        dup_ref[s] = dup
        dsecond = dot(dup, w_up_ref[...], ((1,), (1,)))
        lines, inverse = normed(mid_ref[s])
        dmid = dy + norm_back_rows(dsecond * scale_b, lines, inverse)
        dmid_ref[s] = dmid
        gate, attended = gate_ref[s], att_ref[s]
        gbranch = (dmid * gate_a).astype(BF16)
        gbranch_ref[s] = gbranch
        sums = [dmid * branch_ref[s].astype(F32), dsecond * lines, dsecond, dy * down_ref[s].astype(F32)]
        for i in range(4):
            lanes = slice(DA * i, DA * i + DA)
            sums_ref[:, lanes] = sums[i] if s == 0 else sums_ref[:, lanes] + sums[i]
        dgated = dot(gbranch, w_out_ref[...], ((1,), (1,)))
        dgate_ref[s] = (dgated * attended * slope(gate)).astype(BF16)
        cots = head_rows(dgated * gate)
        rows = head_rows(q_ref[s].astype(F32))
        low = probs_ref[s]
        probs = low.astype(F32)

        def window(w):
            return slice(128 * w, 128 * w + 128), slice(32 * w, 32 * w + 128)

        def weights_of(w):
            at, span = window(w)
            return dot(cots[at], kv_ref[s, span, DA:], ((1,), (1,)))

        weighed = probs * by_window(weights_of)
        slopes = weighed - probs * jnp.sum(weighed, axis=1, keepdims=True)
        slopes_ref[...] = slopes if s == 0 else slopes_ref[...] + slopes
        slopes_low = slopes.astype(BF16)

        def query_of(w):
            at, span = window(w)
            return dot(slopes_low[at], kv_ref[s, span, :DA])

        dq_ref[s] = (rows_of_heads(by_window(query_of)) * 32 ** (-0.5)).astype(BF16)
        grads_ref[s] = jnp.zeros((SPAN, 2 * DA), F32)
        for w in range(8):
            at, span = window(w)
            grads_ref[s, span, :DA] += dot(slopes_low[at], rows[at], ((0,), (0,))) * 32 ** (-0.5)
            grads_ref[s, span, DA:] += dot(low[at], cots[at], ((0,), (0,)))
        dkv_ref[s] = grads_ref[s, RIM : RIM + 256, :]
        prev_ref[s] = grads_ref[s, :RIM, :].astype(BF16)
        next_ref[s] = grads_ref[s, RIM + 256 :, :].astype(BF16)

    for s in range(4):
        atoms(s)

    def rows_of(ref):
        return ref[...].reshape(1024, ref.shape[2])

    dw_out_ref[...] = dot(rows_of(gated_ref), rows_of(gbranch_ref), ((0,), (0,)))
    dw_up_ref[...] = dot(rows_of(second_ref), rows_of(dup_ref), ((0,), (0,)))
    dw_down_ref[...] = dot(rows_of(hidden_ref), rows_of(gdown_ref), ((0,), (0,)))
    du_ref[:, :DA] = sums_ref[:, :DA] * slope(gate_a)
    du_ref[:, DA : 2 * DA] = sums_ref[:, DA : 2 * DA] * slope(scale_b)
    du_ref[:, 2 * DA : 3 * DA] = sums_ref[:, 2 * DA : 3 * DA]
    du_ref[:, 3 * DA :] = sums_ref[:, 3 * DA :] * slope(gate_b)
    pairs = pair_norm(pair_ref[...].astype(F32))
    slopes = slopes_ref[...].reshape(8, 4, 32, 128)
    for h in range(4):
        own = slopes[:, h].reshape(256, 128)
        for c in range(16):
            dpair_ref[16 * h + c : 16 * h + c + 1, :] = jnp.sum(own * pairs[c], axis=0, keepdims=True)


def atom_back(*args):
    sds = jax.ShapeDtypeStruct
    return kernel_call(
        atom_back_kernel,
        [
            sds((4, 256, DA), BF16), sds((4, 256, DA), BF16), sds((4, 256, 2 * DA), F32),
            sds((4, RIM, 2 * DA), BF16), sds((4, RIM, 2 * DA), BF16), sds((4, 256, DA), F32),
            sds((256, 4 * DA), F32), sds((DA, DA), F32), sds((DA, 2 * FA), F32), sds((FA, DA), F32), sds((64, 128), F32),
        ],
        scratch=[
            pltpu.VMEM((4, 256, DA), F32), pltpu.VMEM((4, SPAN, 2 * DA), F32), pltpu.VMEM((1024, 128), F32),
            pltpu.VMEM((256, 4 * DA), F32), pltpu.VMEM((4, 256, DA), BF16), pltpu.VMEM((4, 256, 2 * FA), BF16),
            pltpu.VMEM((4, 256, DA), BF16),
        ],
        us=12,
        name="atom_back",
    )(*args)


def atom_end_kernel(
    core_ref, dq_ref, dgate_ref, dkv_ref, prev_ref, next_ref, dmid_ref, x_ref, first_ref, u_ref, du_ref, cond_low_ref,
    w_qkvg_ref, dw_out_ref, dw_up_ref, dw_down_ref, dpool_ref, single_ref, tdu_ref, misc_ref,
    out_ref, keep_ref, send_ref,
    dw_qkvg_ref, sums_ref, whole_ref,
):
    scale = sigmoid(part(u_ref, 0, DA))
    sums_ref[...] = jnp.zeros_like(sums_ref)
    dw_qkvg_ref[...] = jnp.zeros_like(dw_qkvg_ref)

    @pl.loop(0, 4)
    def _(s):
        whole_ref[...] = dkv_ref[s]
        whole_ref[:RIM, :] += prev_ref[s].astype(F32)
        whole_ref[256 - RIM :, :] += next_ref[s].astype(F32)
        grads = jnp.concatenate([dq_ref[s], whole_ref[...].astype(BF16), dgate_ref[s]], axis=1)
        dfirst = dot(grads, w_qkvg_ref[...], ((1,), (1,)))
        lines, inverse = normed(x_ref[s].astype(F32))
        out_ref[s] = dmid_ref[s] + norm_back_rows(dfirst * scale, lines, inverse)
        dw_qkvg_ref[...] += dot(first_ref[s], grads, ((0,), (0,)))
        sums_ref[:, :DA] += dfirst * lines
        sums_ref[:, DA:] += dfirst

    du = jnp.concatenate([sums_ref[:, :DA] * slope(scale), sums_ref[:, DA:], du_ref[...]], axis=1).astype(BF16)
    dw_cond = dot(cond_low_ref[...], du, ((0,), (0,)))
    down = dw_down_ref[...].reshape(16, 2, 8, DA)
    single = dot(single_ref[...], tdu_ref[...], ((0,), (0,))).reshape(16, 3, 8, 2 * DT)
    whole = jnp.concatenate(
        [
            dw_cond, dw_qkvg_ref[...], dw_out_ref[...], dw_up_ref[...], dpool_ref[...],
            down[:, 0].reshape(DA, DA), down[:, 1].reshape(DA, DA), misc_ref[...].astype(F32),
        ]
        + [single[:, i].reshape(DA, 2 * DT) for i in range(3)]
        + [jnp.zeros((DA, 512), F32)],
        axis=1,
    )
    even = core_ref[0] == 0
    for s in range(8):
        rows = whole[:, 1024 * s : 1024 * s + 1024].reshape(8, 2, 8, 1024)
        first, second = rows[:, 0].reshape(64, 1024), rows[:, 1].reshape(64, 1024)
        keep_ref[s] = jnp.where(even, first, second).astype(BF16)
        send_ref[s] = jnp.where(even, second, first).astype(BF16)


def atom_end(*args):
    sds = jax.ShapeDtypeStruct
    return kernel_call(
        atom_end_kernel,
        [sds((4, 256, DA), F32), sds((8, 64, 1024), BF16), sds((8, 64, 1024), BF16)],
        in_specs=[pl.BlockSpec((256, DA), lambda *_: (0, 0)) if i == 8 else fixed(*a.shape) for i, a in enumerate(args[1:])],
        scratch=[pltpu.VMEM((DA, 4 * DA), F32), pltpu.VMEM((256, 2 * DA), F32), pltpu.VMEM((256, 2 * DA), F32)],
        scalars=1,
        us=6,
        arrived=(3, 4),
        name="atom_end",
    )(*args)


SHARE = 960


def split_kernel(samp_ref, wide_ref, heads_ref, *refs):
    out_refs, whole_ref = refs[:4], refs[4]
    for s in range(8):
        pieces = [wide_ref[:, SHARE * s : SHARE * s + SHARE].astype(F32)]
        pieces += [heads_ref[2 * s + i, 64:, : 3 * HS].astype(F32) for i in range(2)]
        whole_ref[s] = jnp.concatenate(pieces + [jnp.zeros((48, 32), F32)], axis=1).astype(BF16)
    for k in range(8):
        out_refs[k // 2][k % 2] = whole_ref[samp_ref[0] ^ k]


def split(samp, wide, heads):
    return kernel_call(
        split_kernel,
        [jax.ShapeDtypeStruct((2, 48, 1280), BF16)] * 4,
        scratch=[pltpu.VMEM((8, 48, 1280), BF16)],
        scalars=1,
        us=3,
        arrived=(0, 1),
        name="split",
    )(samp, wide, heads)


def collect_kernel(wide_ref, wide_part_ref, packed_ref, out_ref, total_ref):
    step = pl.program_id(0)

    @pl.when(step == 0)
    def _():
        total_ref[...] = jnp.zeros_like(total_ref)

    rows = packed_ref[0].astype(F32)
    for i in range(1, 16):
        rows += packed_ref[i].astype(F32)
    total_ref[:, :1024] += rows

    @pl.when(step == 3)
    def _():
        wide = wide_ref[...].astype(F32) + wide_part_ref[...].astype(F32)
        whole = jnp.concatenate([wide, total_ref[...]], axis=0).astype(BF16)
        for i in range(8):
            out_ref[i] = whole


def collect(wide, wide_part, packed):
    return kernel_call(
        collect_kernel,
        [jax.ShapeDtypeStruct((8, 56, 1280), BF16)],
        grid=(4,),
        in_specs=[fixed(48, 1280), fixed(48, 1280), pl.BlockSpec((16, 8, 1024), lambda i: (i, 0, 0))],
        out_specs=[fixed(8, 56, 1280)],
        scratch=[pltpu.VMEM((8, 1280), F32)],
        us=4,
        arrived=(0, 1, 2),
        name="collect",
    )(wide, wide_part, packed)[0]


def hand_out_kernel(
    parts_ref, a_cond_ref, a_qkvg_ref, a_out_ref, a_up_ref, a_down_ref, a_pair_ref, pool_ref, t_cond_ref, t_qkvg_ref,
    t_out_ref, t_up_ref, t_down_ref, t_pair_ref,
):
    def cut(first, last, rows, share):
        pieces = []
        while first < last:
            s, at = divmod(first, share)
            end = min(last - share * s, share)
            pieces.append(parts_ref[s, rows, at:end].astype(F32))
            first = share * s + end
        return jnp.concatenate(pieces, axis=1)

    def wide(first, last):
        return cut(first, last, slice(0, 48), SHARE)

    def atoms(first, last):
        return cut(first, last, slice(48, 56), 1024)

    t_up_ref[...] = wide(0, 4 * DT)
    t_out_ref[...] = wide(4 * DT, 5 * DT)
    t_qkvg_ref[:, 3 * DT :] = wide(5 * DT, 6 * DT)
    t_down_ref[:48, :] = wide(6 * DT, 7 * DT)
    t_down_ref[48:, :] = wide(7 * DT, 8 * DT)
    conds = wide(8 * DT, 10 * DT)
    t_cond_ref[:, 2 * DT : 4 * DT] = conds[:24]
    t_cond_ref[:, 4 * DT :] = conds[24:]
    for i in range(3):
        t_cond_ref[8 * i : 8 * i + 8, : 2 * DT] = atoms(3072 + 2 * DT * i, 3072 + 2 * DT * (i + 1))
    a_cond_ref[...] = atoms(0, 768)
    a_qkvg_ref[...] = atoms(768, 1280)
    a_out_ref[...] = atoms(1280, 1408)
    a_up_ref[...] = atoms(1408, 1920)
    pool_ref[...] = atoms(1920, 2688)
    a_down_ref[:8] = atoms(2688, 2816)
    a_down_ref[8:] = atoms(2816, 2944)
    misc = atoms(2944, 3072)
    t_pair_ref[...] = misc[0:1]
    a_pair_ref[...] = misc[1:2, :4]
    heads = []
    for h in range(16):
        at = SHARE + 3 * HS * (h % 2)
        heads.append(parts_ref[h // 2, :48, at : at + 3 * HS].astype(F32))
    for i in range(3):
        t_qkvg_ref[:, DT * i : DT * i + DT] = jnp.concatenate(
            [head[:, HS * i : HS * i + HS] for head in heads], axis=1
        )


def hand_out(parts):
    sds = jax.ShapeDtypeStruct
    shapes = [
        (8, 768), (8, 512), (8, 128), (8, 512), (16, 128), (1, 4), (8, 768), (24, 6 * DT), (48, 4 * DT), (48, DT),
        (48, 2 * FT), (96, DT), (1, 128),
    ]
    return kernel_call(
        hand_out_kernel,
        [sds(shape, F32) for shape in shapes],
        us=4,
        arrived=(0,),
        name="hand_out",
    )(parts)


def both_axes(x):
    return lax.all_to_all(x, ("samp", "seq"), 0, 0, tiled=True)


def along_seq(x):
    return lax.all_to_all(x, "seq", 0, 0, tiled=True)


ordered = lambda *x: lax.optimization_barrier(x)


def from_samp(part, k):
    return lax.ppermute(part, "samp", [(i, i ^ k) for i in range(8)])


def total(*parts):
    return sum(part.astype(F32) for part in parts).astype(BF16)


def body(
    atom_in,
    tok_in,
    atom_cond,
    single_cond,
    atom_pair,
    token_pair,
    atom_w_cond,
    atom_w_qkvg,
    atom_w_out,
    atom_w_up,
    atom_w_down,
    atom_w_pair,
    pool_weight,
    token_w_cond,
    token_w_qkvg,
    token_w_out,
    token_w_up,
    token_w_down,
    token_w_pair,
    cotangent,
):
    samp, seq = lax.axis_index("samp"), lax.axis_index("seq")
    up, down = [(i, i + 1) for i in range(15)], [(i + 1, i) for i in range(15)]
    rims = jnp.concatenate([atom_in, atom_cond[None]], axis=0)
    from_prev = lax.ppermute(rims[:, 256 - RIM :], "seq", up)
    from_next = lax.ppermute(rims[:, :RIM], "seq", down)
    samp = samp.astype(jnp.int32).reshape(1)
    token_bias = pair_bias(samp, token_pair, token_w_pair)
    token_bias = along_seq(token_bias).reshape(NT, 128)
    atom_in, token_bias = ordered(atom_in, token_bias)
    token_bias = lax.all_gather(token_bias, "samp", axis=0, axis_index_groups=[SAMP_RING])

    key_index = 256 * seq - RIM + 32 * jnp.arange(8)[:, None] + jnp.arange(128)[None, :]
    mask = jnp.where((key_index >= 0) & (key_index < 4096), 0.0, masked).astype(F32)
    (
        first, query, keyval, probs, gate, attended, middle, cond_low, cond_proj, pooled,
        start, tfirst, tgate, tcond_proj, single_low, runs,
    ) = front(
        atom_in, from_prev, from_next, atom_cond, atom_pair, mask, atom_w_pair.astype(F32), atom_w_cond,
        atom_w_qkvg, atom_w_out, atom_w_up, atom_w_down, pool_weight, tok_in, single_cond, token_w_cond, token_w_qkvg,
    )
    *prep, gates = atom_prep(cond_proj, middle, gate, attended, atom_w_out, atom_w_up, atom_w_down)
    normed_pair = pair_normed(samp, token_pair)
    runs, normed_pair, sent, gates, *prep = ordered(along_seq(runs), normed_pair, tfirst, gates, *prep)
    qkv, tprobs, tattended = token_attention(runs, token_bias)
    lines = lax.all_gather(sent, "seq", axis=0, axis_index_groups=[RING])
    (
        token_out, cots, tdgate, tdmid, gated, gbranch, second, dup, hidden, gdown, tdu,
    ) = turn(
        along_seq(tattended), tgate, start, tcond_proj, cotangent, token_w_out, token_w_up, token_w_down
    )
    cots = along_seq(cots)
    wide = token_weights(gated, gbranch, tfirst, tdgate, second, dup, hidden, gdown, single_low, tdu)
    cots, wide = ordered(cots, wide)
    wide = lax.psum_scatter(wide, "seq", scatter_dimension=0, tiled=True, axis_index_groups=[RING])
    tgrads, *slopes = token_attention_back(samp, qkv, tprobs, cots)
    heads = head_weights(tgrads, lines)
    received = [from_samp(slopes[k], 2 * k) for k in range(1, 4)]
    tgrads, heads = ordered(along_seq(tgrads), heads)
    grad_tok, gpooled, dpool, tdu = back(
        tgrads, tdgate, tdmid, start, tcond_proj, token_w_qkvg, pool_weight, pooled
    )
    gpooled, *received = ordered(gpooled, *received)
    slopes = total(slopes[0], *received)
    slopes = along_seq(jnp.concatenate([slopes, heads], axis=1))
    (
        dquery, dgate, dkeyval, to_prev, to_next, dmid, du, dw_out, dw_up, dw_down, dpair,
    ) = atom_back(
        gpooled.reshape(4, 64, DA), gates, middle, gate, attended, query, keyval, probs, atom_pair,
        atom_w_out, atom_w_up, atom_w_down, *prep,
    )
    back_next = lax.ppermute(to_prev, "seq", down)
    back_prev = lax.ppermute(to_next, "seq", up)
    misc = pair_grad(slopes, normed_pair, dpair)
    grad_atoms, packed, beside = atom_end(
        (seq % 2).astype(jnp.int32).reshape(1),
        dquery, dgate, dkeyval, back_prev, back_next, dmid, atom_in, first, cond_proj, du, cond_low,
        atom_w_qkvg, dw_out, dw_up, dw_down, dpool, single_low, tdu, misc,
    )
    packed = total(packed, lax.ppermute(beside, "seq", [(i, i ^ 1) for i in range(16)])).reshape(64, 8, 1024)
    _, wide = ordered(packed, wide)
    chips = [[core + 2 * i for i in range(64)] for core in range(2)]
    packed = lax.all_to_all(packed, ("samp", "seq"), 0, 0, tiled=True, axis_index_groups=chips)
    wide = split(samp, wide, slopes)
    wide = total(wide[0], *[from_samp(wide[k], 2 * k) for k in range(1, 4)])
    wide = wide[0], from_samp(wide[1], 1)
    parts = lax.all_to_all(collect(*wide, packed), "samp", 0, 0, tiled=True)
    return (token_out, grad_atoms, grad_tok, *hand_out(parts))


def solution(mesh):
    rows, both, whole = P("seq", None), P("samp", "seq", None), P()
    in_specs = (both, both, rows, rows, P(None, "seq", None), P(None, "seq", None)) + (whole,) * 13 + (both,)
    out_specs = (both,) * 3 + (rows,) * 13
    mapped = jax.shard_map(body, mesh=mesh, in_specs=in_specs, out_specs=out_specs, check_vma=False)

    def run(*args):
        with jax.sharding.use_abstract_mesh(mesh.abstract_mesh):
            return mapped(*args)

    return run
```
